32 devices in a mesh: grp: 2 (over y), row: 4 (over z), col: 4 (over x, core).
Axes of the slice: x: 2, y: 2, z: 4, core: 2. Of those that a mesh axis runs over, the one named last changes fastest.
Arguments:
- root_covariance: float32 [40, 4, 128, 20, 4, 128], P('grp', 'col', None, None, 'row'), parts along dimension 0, as said below
- factor_one: float32 [40, 4, 128, 512], P('grp', 'row', None, 'col'), parts along dimension 0, may hold values from -0.18 to 0.18
- inverse_one: float32 [1024, 512], P(('grp', 'col')), parts along dimension 0, as said below
- pattern_one: int32 [160], P('grp'), parts along dimension 0, may hold values from 0 to 1, as said below
- factor_parent: float32 [1024, 512], P(('grp', 'row'), 'col'), parts along dimension 0, may hold values from -0.18 to 0.18
- factor_root: float32 [40, 4, 128, 512], P('grp', 'row', None, 'col'), parts along dimension 0, may hold values from -0.18 to 0.18
- inverse_two: float32 [1024, 512], P(('grp', 'col')), parts along dimension 0, as said below
- pattern_two: int32 [160], P('grp'), parts along dimension 0, may hold values from 0 to 1, as said below
Outputs:
- sigma_cross_one: float32 [1024, 20, 4, 128], P(('grp', 'row'), None, 'col'), parts along dimension 0
- sigma_block_one: float32 [1024, 512], P(('grp', 'col'), 'row'), parts along dimension 0
- sigma_parent_two: float32 [1024, 512], P(('grp', 'row')), parts along dimension 0
- sigma_cross_two: float32 [1024, 20, 4, 128], P(('grp', 'row'), None, 'col'), parts along dimension 0
- sigma_block_two: float32 [1024, 512], P(('grp', 'col'), 'row'), parts along dimension 0
The draws below stay inside these ranges and needn't reach their ends.
There are 2 independent parts, one for each index of `grp`. The reference program is written for one: setup_inputs(seed, part) draws one part's arguments, and reference() takes and returns one part's arrays. A program takes and returns all parts, laid end to end along the dimension named above; each array names one. Nothing has to cross between parts.
Inputs may be any that keep to these rules, and one draw needn't show every extreme that they name: `root_covariance`: symmetric and positive definite. `inverse_one`: lower triangular with a positive diagonal. `inverse_two`: lower triangular with a positive diagonal. `pattern_one`: 1 marks a root block in the row structure. `pattern_two`: 1 only where pattern_one is 1.
All inputs are finite; a program needn't handle non-finite values.
Results may differ from the reference program's by a relative error of at most 0.0001.
Values sent between devices are 32-bit elements; how exact they have to be, the bound alone decides.
No kernel may reach another device: no remote copies, remote signals or barrier semaphores. Data moves between devices by JAX's collectives and lax.ppermute only.
A program may use at most 256 MiB of HBM per device.

```python
import math
import jax
import jax.numpy as jnp
from jax import lax

B = 128
NR = 10240
W = 512
RB = 80
RBL = 20
N_ROW = 4
N_COL = 4


def pattern_bits(key):
    return jax.random.randint(key, (2, RB), 0, 10)


def draw_root_covariance(key, part):
    key = jax.random.fold_in(key, 11)
    first_key, second_key = jax.random.split(key, 2)
    noise = jax.random.normal(first_key, (NR, NR), jnp.float32)
    matrix = (noise + noise.T) * (0.25 / math.sqrt(NR))
    diagonal = jax.random.uniform(second_key, (NR,), jnp.float32, 1.0, 2.0)
    matrix = matrix + jnp.diag(diagonal)
    return matrix.reshape(RBL, N_COL, B, RBL, N_ROW, B)


def draw_inverse_one(key, part):
    key = jax.random.fold_in(key, 21)
    first_key, second_key = jax.random.split(key)
    noise = jax.random.normal(first_key, (W, W), jnp.float32)
    positions = jnp.arange(W)
    lower_part = jnp.where(positions[:, None] > positions[None, :], noise * (0.8 / math.sqrt(W)), 0.0)
    return lower_part + jnp.diag(jax.random.uniform(second_key, (W,), jnp.float32, 1.0, 2.0))


def draw_inverse_two(key, part):
    key = jax.random.fold_in(key, 22)
    first_key, second_key = jax.random.split(key)
    noise = jax.random.normal(first_key, (W, W), jnp.float32)
    positions = jnp.arange(W)
    lower_part = jnp.where(positions[:, None] > positions[None, :], noise * (0.8 / math.sqrt(W)), 0.0)
    return lower_part + jnp.diag(jax.random.uniform(second_key, (W,), jnp.float32, 1.0, 2.0))


def draw_pattern_one(key, part):
    shared = pattern_bits(key)
    return (shared[0] < 6).astype(jnp.int32)


def draw_pattern_two(key, part):
    shared = pattern_bits(key)
    return ((shared[0] < 6) & (shared[1] < 7)).astype(jnp.int32)


def levels(own_key, shape, shards, smallest, top_value):
    level = 1.0
    for dim, shards_of in shards:
        draws = jax.random.uniform(jax.random.fold_in(jax.random.fold_in(own_key, 6), dim), (shards_of,), jnp.float32, smallest / len(shards), top_value / len(shards))
        level = level * jnp.repeat(jnp.exp(draws), shape[dim] // shards_of).reshape((-1,) + (1,) * (len(shape) - 1 - dim))
    return level


def bell_draw(stream_key, shape, scale, limit, cuts=(), held_as=jnp.bfloat16):
    drawn = jax.random.normal(stream_key, shape, jnp.float32) * scale
    if len(cuts) > 0:
        drawn = levels(stream_key, shape, cuts, -0.22, 0.18) * drawn
    return jnp.clip(drawn, min=-limit, max=limit).astype(held_as)


def setup_inputs(seed: int = 0, part: int = 0) -> dict:
    arg_keys = jax.random.split(jax.random.key(seed), 9)
    part_splits = jax.random.split(jax.random.fold_in(arg_keys[8], part), 9)
    return {
        "root_covariance": draw_root_covariance(jax.random.fold_in(jax.random.fold_in(arg_keys[8], part), 71), part),
        "factor_one": bell_draw(part_splits[1], (RBL, N_ROW, B, W), 0.03, 0.18, ((1, 4), (3, 4)), jnp.float32),
        "inverse_one": draw_inverse_one(jax.random.fold_in(jax.random.fold_in(arg_keys[8], part), 71), part),
        "pattern_one": draw_pattern_one(jax.random.fold_in(jax.random.fold_in(arg_keys[8], part), 71), part),
        "factor_parent": bell_draw(part_splits[4], (W, W), 0.03, 0.18, ((0, 4), (1, 4)), jnp.float32),
        "factor_root": bell_draw(part_splits[5], (RBL, N_ROW, B, W), 0.03, 0.18, ((1, 4), (3, 4)), jnp.float32),
        "inverse_two": draw_inverse_two(jax.random.fold_in(jax.random.fold_in(arg_keys[8], part), 71), part),
        "pattern_two": draw_pattern_two(jax.random.fold_in(jax.random.fold_in(arg_keys[8], part), 71), part),
    }


def matmul(left_side, right_side):
    return jnp.dot(left_side, right_side, precision=lax.Precision.HIGHEST, preferred_element_type=jnp.float32)


def contract_lead(left_side, right_side):
    return lax.dot_general(left_side, right_side, (((0,), (0,)), ((), ())), precision=lax.Precision.HIGHEST, preferred_element_type=jnp.float32)


def reference(root_covariance, factor_one, inverse_one, pattern_one, factor_parent, factor_root, inverse_two, pattern_two):
    covariance = root_covariance.reshape(NR, NR)
    mask_one = jnp.repeat(pattern_one.astype(jnp.float32), B)[:, None]
    mask_two = jnp.repeat(pattern_two.astype(jnp.float32), B)[:, None]
    solved_one = matmul(factor_one.reshape(NR, W) * mask_one, inverse_one)
    image_one = matmul(covariance, solved_one)
    cross_one = -mask_one * image_one
    block_one = contract_lead(inverse_one, inverse_one) + contract_lead(solved_one, image_one)
    solved_parent = matmul(factor_parent, inverse_two)
    solved_root = matmul(factor_root.reshape(NR, W) * mask_two, inverse_two)
    image_parent = matmul(block_one, solved_parent) + contract_lead(cross_one, solved_root)
    image_root = matmul(cross_one, solved_parent) + matmul(covariance, solved_root)
    block_two = contract_lead(inverse_two, inverse_two) + contract_lead(solved_parent, image_parent) + contract_lead(solved_root, image_root)
    cross_two = -mask_two * image_root
    return (cross_one.T.reshape(W, RBL, N_COL, B), block_one, -image_parent, cross_two.T.reshape(W, RBL, N_COL, B), block_two)
```

```python
import functools

import jax
import jax.numpy as jnp
from jax import lax
from jax.experimental import pallas as pl
from jax.experimental.pallas import tpu as pltpu
from jax.sharding import PartitionSpec as P

B = 128
VMEM_LIMIT = 52 * 1024 * 1024
VMEM = pl.BlockSpec(memory_space=pltpu.VMEM)
SMEM = pl.BlockSpec(memory_space=pltpu.SMEM)


def split(values):
    high = values.astype(jnp.bfloat16)
    low = (values - high.astype(jnp.float32)).astype(jnp.bfloat16)
    return high, low


def lanes_dot(left, right):
    return lax.dot_general(
        left, right, (((1,), (1,)), ((), ())), preferred_element_type=jnp.float32
    )


def plain_dot(left, right):
    return lax.dot_general(
        left, right, (((1,), (0,)), ((), ())), preferred_element_type=jnp.float32
    )


def three_products(dot, left, right):
    left_high, left_low = left
    right_high, right_low = right
    rows = left_high.shape[0]
    both = dot(jnp.concatenate([left_high, left_low], 0), right_high)
    return both[:rows] + both[rows:] + dot(left_high, right_low)


def stacked(high, low):
    return jnp.concatenate([high, low], 0)


def call(kernel, name, out_shape, operands, flops, in_specs=None, scratch=()):
    size = sum(a.size * a.dtype.itemsize for a in operands)
    size += sum(a.size * a.dtype.itemsize for a in jax.tree.leaves(out_shape))
    return pl.pallas_call(
        kernel,
        name=name,
        out_shape=out_shape,
        in_specs=in_specs or [VMEM] * len(operands),
        out_specs=jax.tree.map(lambda _: VMEM, out_shape),
        scratch_shapes=scratch,
        compiler_params=pltpu.CompilerParams(vmem_limit_bytes=VMEM_LIMIT),
        cost_estimate=pl.CostEstimate(flops=flops, bytes_accessed=size, transcendentals=0),
    )(*operands)


def shape_of(shape, dtype=jnp.float32):
    return jax.ShapeDtypeStruct(shape, dtype)


def active_order(pattern_one, pattern_two, position, grid_size, capacity):
    mine = (jnp.arange(grid_size) == position)[None, :]
    one = jnp.sum(jnp.where(mine, pattern_one.reshape(-1, grid_size), 0), axis=1)
    two = jnp.sum(jnp.where(mine, pattern_two.reshape(-1, grid_size), 0), axis=1)
    key = one + two
    index = jnp.arange(key.shape[0])
    ahead = (key[None, :] > key[:, None]) | (
        (key[None, :] == key[:, None]) & (index[None, :] < index[:, None])
    )
    rank = jnp.sum(ahead.astype(jnp.int32), axis=1)
    slots = jnp.arange(capacity)
    order = jnp.sum(jnp.where(rank[None, :] == slots[:, None], index[None, :], 0), axis=1)
    return order.astype(jnp.int32), jnp.sum(one), jnp.sum(two)


def pack_kernel(cap_one, cap_two, order, counts, f_one, inv_one, f_par, f_root, inv_two, out_one, out_two):
    width = inv_one.shape[1]
    for i in range(cap_one):
        out_one[pl.ds(i * B, B), :] = jnp.where(i < counts[0], f_one[order[i]], 0.0)
    out_one[pl.ds(cap_one * B, width), :] = inv_one[...].T
    for i in range(cap_two):
        out_two[pl.ds(i * B, B), :] = jnp.where(i < counts[1], f_root[order[i]], 0.0)
    out_two[pl.ds(cap_two * B, width), :] = inv_two[...].T
    out_two[pl.ds(cap_two * B + width, f_par.shape[0]), :] = f_par[...]


def joined(ref, start, size):
    return jnp.concatenate([ref[k, pl.ds(start, size), :] for k in range(ref.shape[0])], 1)


def solve_one_kernel(cap, gathered, out):
    width = out.shape[0] // 2
    inverse = split(joined(gathered, cap * B, width))

    def step(i, carry):
        start = pl.multiple_of(i * 2 * B, 2 * B)
        rows = split(joined(gathered, start, 2 * B))
        high, low = split(three_products(lanes_dot, inverse, rows))
        out[:width, pl.ds(start, 2 * B)] = high
        out[width:, pl.ds(start, 2 * B)] = low
        return carry

    lax.fori_loop(0, cap // 2, step, 0)


def parent_kernel(cap_two, gathered, out):
    width, share = out.shape
    inverse = split(joined(gathered, cap_two * B, width))
    parent = split(joined(gathered, cap_two * B + width, share))
    out[...] = three_products(lanes_dot, inverse, parent)


def solve_two_kernel(
    cap_one, cap_two, place, gathered_one, gathered_two, parents,
    out_full, out_root, out_lead, out_diag_one, out_diag_two,
    weight_high, weight_low,
):
    grid_size, width, share = parents.shape
    row, col = place[0], place[1]
    for k in range(grid_size):
        total = jnp.zeros((width, share), jnp.float32)
        for m in range(grid_size):
            piece = gathered_one[k, pl.ds(cap_one * B + m * share, share), :]
            total = total + three_products(plain_dot, split(parents[m]), split(piece))
        high, low = split(total)
        weight_high[:, k * share:(k + 1) * share] = high
        weight_low[:, k * share:(k + 1) * share] = low
    weight = (weight_high[...], weight_low[...])
    row_start = cap_one * B + pl.multiple_of(row * share, share)
    col_start = cap_one * B + pl.multiple_of(col * share, share)
    inv_row = split(joined(gathered_one, row_start, share))
    inv_col = split(joined(gathered_one, col_start, share))
    out_lead[...] = three_products(lanes_dot, inv_row, weight)
    out_diag_one[...] = three_products(lanes_dot, inv_col, inv_row)
    row_start = cap_two * B + pl.multiple_of(row * share, share)
    col_start = cap_two * B + pl.multiple_of(col * share, share)
    inv_row = split(joined(gathered_two, row_start, share))
    inv_col = split(joined(gathered_two, col_start, share))
    out_diag_two[...] = three_products(lanes_dot, inv_col, inv_row)
    inverse = split(joined(gathered_two, cap_two * B, width))

    def both(i, carry):
        start = pl.multiple_of(i * 2 * B, 2 * B)
        own = three_products(lanes_dot, inverse, split(joined(gathered_two, start, 2 * B)))
        high, low = split(own)
        out_root[:width, pl.ds(start, 2 * B)] = high
        out_root[width:, pl.ds(start, 2 * B)] = low
        other = three_products(lanes_dot, weight, split(joined(gathered_one, start, 2 * B)))
        high, low = split(own - other)
        out_full[:width, pl.ds(start, 2 * B)] = high
        out_full[width:, pl.ds(start, 2 * B)] = low
        return carry

    def first_only(i, carry):
        start = pl.multiple_of(i * 2 * B, 2 * B)
        other = three_products(lanes_dot, weight, split(joined(gathered_one, start, 2 * B)))
        high, low = split(-other)
        out_full[:width, pl.ds(start, 2 * B)] = high
        out_full[width:, pl.ds(start, 2 * B)] = low
        return carry

    lax.fori_loop(0, cap_two // 2, both, 0)
    lax.fori_loop(cap_two // 2, cap_one // 2, first_only, 0)


def image_kernel(
    blocks, cap, chunk, order_in, order_out, counts, solved, cov_a, cov_b, out, high, low, total
):
    step = pl.program_id(0)
    width = out.shape[0]
    total[...] = jnp.zeros_like(total)

    @pl.when(2 * step < counts[1])
    def _():
        for lead in range(0, cap, chunk):
            size = min(chunk, cap - lead)

            @pl.when(lead < counts[0])
            def _():
                for j in range(size):
                    for half, cov in enumerate((cov_a, cov_b)):
                        piece = cov[pl.ds(order_in[lead + j], B, stride=blocks), :]
                        piece_high, piece_low = split(piece)
                        high[half * B:(half + 1) * B, j * B:(j + 1) * B] = piece_high
                        low[half * B:(half + 1) * B, j * B:(j + 1) * B] = piece_low
                span = slice(lead * B, (lead + size) * B)
                both = lanes_dot(solved[:, span], high[:, :size * B])
                more = lanes_dot(solved[:width, span], low[:, :size * B])
                total[...] += both[:width] + both[width:] + more

    out[...] = total[...]


def image(covariance, solved, order_in, order_out, counts, cap_out, name):
    width = solved.shape[0] // 2
    cap_in = solved.shape[1] // B
    rows, blocks = covariance.shape[0], covariance.shape[1]
    flat = covariance.reshape(rows * blocks, B)
    chunk = 4

    def place(which):
        def index_map(i, order_in, order_out, counts):
            last = jnp.maximum(counts[1] - 1, 0)
            return (order_out[jnp.minimum(2 * i + which, last)], 0)

        return pl.BlockSpec((B * blocks, B), index_map)

    grid_spec = pltpu.PrefetchScalarGridSpec(
        num_scalar_prefetch=3,
        grid=(cap_out // 2,),
        in_specs=[
            pl.BlockSpec(solved.shape, lambda i, *_: (0, 0), pipeline_mode=pl.Buffered(1)),
            place(0),
            place(1),
        ],
        out_specs=pl.BlockSpec((width, 2 * B), lambda i, *_: (0, i)),
        scratch_shapes=[
            pltpu.VMEM((2 * B, chunk * B), jnp.bfloat16),
            pltpu.VMEM((2 * B, chunk * B), jnp.bfloat16),
            pltpu.VMEM((width, 2 * B), jnp.float32),
        ],
    )
    return pl.pallas_call(
        functools.partial(image_kernel, blocks, cap_in, chunk),
        name=name,
        grid_spec=grid_spec,
        out_shape=shape_of((width, cap_out * B)),
        compiler_params=pltpu.CompilerParams(vmem_limit_bytes=VMEM_LIMIT),
        cost_estimate=pl.CostEstimate(
            flops=6 * width * cap_in * B * cap_out * B,
            bytes_accessed=4 * cap_out * B * blocks * B + 8 * width * cap_out * B,
            transcendentals=0,
        ),
    )(order_in, order_out, counts, solved, flat, flat)


def unpack_kernel(blocks, cap, which, order, counts, packed, out):
    share = packed.shape[0]
    out[...] = jnp.zeros_like(out)
    for i in range(min(cap, blocks)):

        @pl.when(i < counts[which])
        def _():
            out[pl.ds(order[i], share, stride=blocks), :] = -packed[:, i * B:(i + 1) * B]


def unpack(packed, order, counts, which, blocks, name):
    share, cap = packed.shape[0], packed.shape[1] // B
    flat = call(
        functools.partial(unpack_kernel, blocks, cap, which),
        name,
        shape_of((share * blocks, B)),
        (order, counts, packed),
        1,
        in_specs=[SMEM, SMEM, VMEM],
    )
    return flat.reshape(share, blocks, 1, B)


def gram_one_kernel(image_rows, solved_one, solved_two, out):
    grid_size, _, share = out.shape
    width = solved_one.shape[0] // 2
    rows = split(image_rows[...])
    for half, solved in enumerate((solved_one, solved_two)):
        product = three_products(lanes_dot, rows, (solved[:width, :], solved[width:, :]))
        for k in range(grid_size):
            out[k, half * share:(half + 1) * share, :] = product[:, k * share:(k + 1) * share]


def gram_two_kernel(image_rows, solved_root, image_parent, parent, out):
    grid_size, share, _ = out.shape
    width = solved_root.shape[0] // 2
    rows = split(image_rows[...])
    product = three_products(lanes_dot, rows, (solved_root[:width, :], solved_root[width:, :]))
    product = product + three_products(
        lanes_dot, split(image_parent[...].T), split(parent[...])
    )
    for k in range(grid_size):
        out[k, :, :] = product[:, k * share:(k + 1) * share]


def swap_grid(block, grid_size):
    pairs = [
        (r * grid_size + c, c * grid_size + r) for r in range(grid_size) for c in range(grid_size)
    ]
    return lax.ppermute(block, ("row", "col"), pairs)


def scatter_sum(pieces, grid_size, position):
    total = lax.dynamic_index_in_dim(pieces, position, 0, keepdims=False)
    for shift in range(1, grid_size):
        target = lax.rem(position + shift, grid_size)
        piece = lax.dynamic_index_in_dim(pieces, target, 0, keepdims=False)
        total = total + lax.ppermute(
            piece, "row", [(i, (i + shift) % grid_size) for i in range(grid_size)]
        )
    return total


def gather_rows(block, grid_size, position):
    gathered = jnp.zeros((grid_size,) + block.shape, block.dtype)
    gathered = lax.dynamic_update_index_in_dim(gathered, block, position, 0)
    for shift in range(1, grid_size):
        other = lax.ppermute(block, "row", [(i, (i + shift) % grid_size) for i in range(grid_size)])
        source = lax.rem(position + grid_size - shift, grid_size)
        gathered = lax.dynamic_update_index_in_dim(gathered, other, source, 0)
    return gathered


def run(
    cap_one, cap_two, root_covariance, factor_one, inverse_one, pattern_one,
    factor_parent, factor_root, inverse_two, pattern_two,
):
    grid_size = lax.axis_size("row")
    row = lax.axis_index("row")
    col = lax.axis_index("col")
    share, width = inverse_one.shape
    blocks = root_covariance.shape[3]
    covariance = root_covariance.reshape(-1, blocks, B)
    row_order, row_one, row_two = active_order(pattern_one, pattern_two, row, grid_size, cap_one)
    col_order, col_one, col_two = active_order(pattern_one, pattern_two, col, grid_size, cap_one)
    place = jnp.stack([row, col]).astype(jnp.int32)
    row_counts = jnp.stack([row_one, row_two])
    col_counts = jnp.stack([col_one, col_two])

    packed_one, packed_two = call(
        functools.partial(pack_kernel, cap_one, cap_two),
        "pack",
        (shape_of((cap_one * B + width, share)), shape_of((cap_two * B + width + share, share))),
        (
            row_order, row_counts, factor_one.reshape(blocks, B, share), inverse_one,
            factor_parent, factor_root.reshape(blocks, B, share), inverse_two,
        ),
        1,
        in_specs=[SMEM, SMEM] + [VMEM] * 5,
    )
    gathered_one = lax.all_gather(packed_one, "col")
    gathered_two = lax.all_gather(packed_two, "col")

    solved_one = call(
        functools.partial(solve_one_kernel, cap_one),
        "solve_one",
        shape_of((2 * width, cap_one * B), jnp.bfloat16),
        (gathered_one,),
        6 * width * width * cap_one * B,
    )
    counts = jnp.stack([row_one, col_one])
    image_one = image(covariance, solved_one, row_order, col_order, counts, cap_one, "image_one")
    image_one = lax.psum_scatter(image_one, "row", scatter_dimension=0, tiled=True)

    parent = call(
        functools.partial(parent_kernel, cap_two),
        "parent",
        shape_of((width, share)),
        (gathered_two,),
        6 * width * width * share,
    )
    parents = gather_rows(parent, grid_size, row)
    solved_two, solved_root, lead, diag_one, diag_two = call(
        functools.partial(solve_two_kernel, cap_one, cap_two),
        "solve_two",
        (
            shape_of((2 * width, cap_one * B), jnp.bfloat16),
            shape_of((2 * width, cap_two * B), jnp.bfloat16),
            shape_of((share, width)),
            shape_of((share, share)),
            shape_of((share, share)),
        ),
        (place, gathered_one, gathered_two, parents),
        6 * width * width * (cap_one + cap_two) * B,
        in_specs=[SMEM] + [VMEM] * 3,
        scratch=[pltpu.VMEM((width, width), jnp.bfloat16)] * 2,
    )
    counts = jnp.stack([row_one, col_two])
    image_two = image(covariance, solved_two, row_order, col_order, counts, cap_two, "image_two")
    image_two = lax.psum_scatter(image_two, "row", scatter_dimension=0, tiled=True)

    rows_one = swap_grid(image_one, grid_size)
    cross_one = unpack(image_one, col_order, col_counts, 0, blocks, "cross_one")
    gram_one = call(
        gram_one_kernel,
        "gram_one",
        shape_of((grid_size, 2 * share, share)),
        (rows_one, solved_one, solved_two),
        12 * share * width * cap_one * B,
    )
    gram_one = scatter_sum(gram_one, grid_size, row)
    block_one = gram_one[:share] + diag_one
    mixed = swap_grid(gram_one[share:], grid_size)
    own_lead = lax.dynamic_slice_in_dim(lead, col * share, share, 1)
    mixed_all = lax.all_gather(mixed, "col")
    parent_out = jnp.concatenate([mixed_all[k] for k in range(grid_size)], 1) - lead

    rows_two = swap_grid(image_two, grid_size)
    cross_two = unpack(image_two, col_order, col_counts, 1, blocks, "cross_two")
    gram_two = call(
        gram_two_kernel,
        "gram_two",
        shape_of((grid_size, share, share)),
        (rows_two, solved_root, own_lead - mixed, parent),
        6 * share * width * cap_two * B,
    )
    block_two = scatter_sum(gram_two, grid_size, row) + diag_two
    return cross_one, block_one, parent_out, cross_two, block_two


def local(*arguments):
    blocks = arguments[0].shape[3]
    full = blocks + blocks % 2
    return run(full, full, *arguments)


def solution(mesh):
    return jax.shard_map(
        local,
        mesh=mesh,
        in_specs=(
            P("grp", "col", None, None, "row", None),
            P("grp", "row", None, "col"),
            P(("grp", "col"), None),
            P("grp"),
            P(("grp", "row"), "col"),
            P("grp", "row", None, "col"),
            P(("grp", "col"), None),
            P("grp"),
        ),
        out_specs=(
            P(("grp", "row"), None, "col", None),
            P(("grp", "col"), "row"),
            P(("grp", "row"), None),
            P(("grp", "row"), None, "col", None),
            P(("grp", "col"), "row"),
        ),
        check_vma=False,
    )
```

```python
import functools

import jax
import jax.numpy as jnp
from jax import lax
from jax.experimental import pallas as pl
from jax.experimental.pallas import tpu as pltpu
from jax.sharding import PartitionSpec as P

B = 128
VMEM_LIMIT = 52 * 1024 * 1024
VMEM = pl.BlockSpec(memory_space=pltpu.VMEM)
SMEM = pl.BlockSpec(memory_space=pltpu.SMEM)


def split(values):
    high = values.astype(jnp.bfloat16)
    low = (values - high.astype(jnp.float32)).astype(jnp.bfloat16)
    return high, low


def lanes_dot(left, right):
    return lax.dot_general(
        left, right, (((1,), (1,)), ((), ())), preferred_element_type=jnp.float32
    )


def plain_dot(left, right):
    return lax.dot_general(
        left, right, (((1,), (0,)), ((), ())), preferred_element_type=jnp.float32
    )


def three_products(dot, left, right):
    left_high, left_low = left
    right_high, right_low = right
    rows = left_high.shape[0]
    both = dot(jnp.concatenate([left_high, left_low], 0), right_high)
    return both[:rows] + both[rows:] + dot(left_high, right_low)


def stacked(high, low):
    return jnp.concatenate([high, low], 0)


def call(kernel, name, out_shape, operands, flops, in_specs=None, scratch=()):
    size = sum(a.size * a.dtype.itemsize for a in operands)
    size += sum(a.size * a.dtype.itemsize for a in jax.tree.leaves(out_shape))
    return pl.pallas_call(
        kernel,
        name=name,
        out_shape=out_shape,
        in_specs=in_specs or [VMEM] * len(operands),
        out_specs=jax.tree.map(lambda _: VMEM, out_shape),
        scratch_shapes=scratch,
        compiler_params=pltpu.CompilerParams(vmem_limit_bytes=VMEM_LIMIT),
        cost_estimate=pl.CostEstimate(flops=flops, bytes_accessed=size, transcendentals=0),
    )(*operands)


def shape_of(shape, dtype=jnp.float32):
    return jax.ShapeDtypeStruct(shape, dtype)


def plan_kernel(capacities, place, pattern_one, pattern_two, row_order, col_order, info):
    blocks = row_order.shape[0]
    grid_size = pattern_one.shape[0] // blocks
    largest_one, largest_two = jnp.int32(0), jnp.int32(0)
    counts_one, counts_two = [], []
    for p in range(grid_size):

        def count(b, carry):
            return (
                carry[0] + pattern_one[b * grid_size + p],
                carry[1] + pattern_two[b * grid_size + p],
            )

        one, two = lax.fori_loop(0, blocks, count, (jnp.int32(0), jnp.int32(0)))
        counts_one.append(one)
        counts_two.append(two)
        largest_one = jnp.maximum(largest_one, one)
        largest_two = jnp.maximum(largest_two, two)
    choice = jnp.int32(len(capacities) - 1)
    for i in reversed(range(len(capacities) - 1)):
        fits = (largest_one <= capacities[i][0]) & (largest_two <= capacities[i][1])
        choice = jnp.where(fits, i, choice)
    info[4] = choice
    for axis, order in enumerate((row_order, col_order)):
        position = place[axis]
        own_one, own_two = jnp.int32(0), jnp.int32(0)
        for p in range(grid_size):
            own_one = jnp.where(position == p, counts_one[p], own_one)
            own_two = jnp.where(position == p, counts_two[p], own_two)
        info[2 * axis] = own_one
        info[2 * axis + 1] = own_two

        def put(b, carry):
            one = pattern_one[b * grid_size + position]
            two = pattern_two[b * grid_size + position]
            slot = jnp.where(two > 0, carry[0], jnp.where(one > 0, carry[1], carry[2]))
            order[slot] = b
            return (carry[0] + two, carry[1] + one - two, carry[2] + 1 - one)

        lax.fori_loop(0, blocks, put, (jnp.int32(0), own_two, own_one))


def pack_kernel(cap_one, cap_two, order, info, f_one, inv_one, f_par, f_root, inv_two, out_one, out_two):
    width = inv_one.shape[1]
    for i in range(cap_one):
        out_one[pl.ds(i * B, B), :] = jnp.where(i < info[0], f_one[order[i]], 0.0)
    out_one[pl.ds(cap_one * B, width), :] = inv_one[...].T
    for i in range(cap_two):
        out_two[pl.ds(i * B, B), :] = jnp.where(i < info[1], f_root[order[i]], 0.0)
    out_two[pl.ds(cap_two * B, width), :] = inv_two[...].T
    out_two[pl.ds(cap_two * B + width, f_par.shape[0]), :] = f_par[...]


def joined(refs, start, size):
    return jnp.concatenate([ref[pl.ds(start, size), :] for ref in refs], 1)


def over_rows(first, last, step, body):
    whole = (last - first) // step

    def turn(i, carry):
        body(pl.multiple_of(first * B + i * (step * B), B), step * B)
        return carry

    lax.fori_loop(0, whole, turn, 0)
    rest = last - first - whole * step
    if rest:
        body((first + whole * step) * B, rest * B)


def solve_one_kernel(cap, *refs):
    gathered, out = refs[:-1], refs[-1]
    width = out.shape[0] // 2
    inverse = split(joined(gathered, cap * B, width))

    def body(start, size):
        rows = split(joined(gathered, start, size))
        high, low = split(three_products(lanes_dot, inverse, rows))
        out[:width, pl.ds(start, size)] = high
        out[width:, pl.ds(start, size)] = low

    over_rows(0, cap, 4, body)


def parent_kernel(cap_two, *refs):
    gathered, out = refs[:-1], refs[-1]
    width, share = out.shape
    inverse = split(joined(gathered, cap_two * B, width))
    parent = split(joined(gathered, cap_two * B + width, share))
    out[...] = three_products(lanes_dot, inverse, parent)


def solve_two_kernel(cap_one, cap_two, place, parents, *refs):
    grid_size, width, share = parents.shape
    gathered_one, gathered_two = refs[:grid_size], refs[grid_size:2 * grid_size]
    out_full, out_root, out_lead, out_diag_one, out_diag_two, weight_high, weight_low = refs[
        2 * grid_size:
    ]
    row, col = place[0], place[1]
    for k in range(grid_size):
        total = jnp.zeros((width, share), jnp.float32)
        for m in range(grid_size):
            piece = gathered_one[k][pl.ds(cap_one * B + m * share, share), :]
            total = total + three_products(plain_dot, split(parents[m]), split(piece))
        high, low = split(total)
        weight_high[:, k * share:(k + 1) * share] = high
        weight_low[:, k * share:(k + 1) * share] = low
    weight = (weight_high[...], weight_low[...])
    row_start = cap_one * B + pl.multiple_of(row * share, share)
    col_start = cap_one * B + pl.multiple_of(col * share, share)
    inv_row = split(joined(gathered_one, row_start, share))
    inv_col = split(joined(gathered_one, col_start, share))
    out_lead[...] = three_products(lanes_dot, inv_row, weight)
    out_diag_one[...] = three_products(lanes_dot, inv_col, inv_row)
    row_start = cap_two * B + pl.multiple_of(row * share, share)
    col_start = cap_two * B + pl.multiple_of(col * share, share)
    inv_row = split(joined(gathered_two, row_start, share))
    inv_col = split(joined(gathered_two, col_start, share))
    out_diag_two[...] = three_products(lanes_dot, inv_col, inv_row)
    inverse = split(joined(gathered_two, cap_two * B, width))

    def both(start, size):
        own = three_products(lanes_dot, inverse, split(joined(gathered_two, start, size)))
        high, low = split(own)
        out_root[:width, pl.ds(start, size)] = high
        out_root[width:, pl.ds(start, size)] = low
        other = three_products(lanes_dot, weight, split(joined(gathered_one, start, size)))
        high, low = split(own - other)
        out_full[:width, pl.ds(start, size)] = high
        out_full[width:, pl.ds(start, size)] = low

    def first_only(start, size):
        other = three_products(lanes_dot, weight, split(joined(gathered_one, start, size)))
        high, low = split(-other)
        out_full[:width, pl.ds(start, size)] = high
        out_full[width:, pl.ds(start, size)] = low

    over_rows(0, cap_two, 4, both)
    over_rows(cap_two, cap_one, 4, first_only)


def image_kernel(
    blocks, cap, chunk, group, order_in, order_out, counts, solved, *refs
):
    covs, (out, high, low, total) = refs[:group], refs[group:]
    step = pl.program_id(0)
    width = out.shape[0]
    total[...] = jnp.zeros_like(total)

    @pl.when(group * step < counts[1])
    def _():
        for lead in range(0, cap, chunk):
            size = min(chunk, cap - lead)

            @pl.when(lead < counts[0])
            def _():
                for j in range(size):
                    for part, cov in enumerate(covs):
                        piece = cov[pl.ds(order_in[lead + j], B, stride=blocks), :]
                        piece_high, piece_low = split(piece)
                        high[part * B:(part + 1) * B, j * B:(j + 1) * B] = piece_high
                        low[part * B:(part + 1) * B, j * B:(j + 1) * B] = piece_low
                span = slice(lead * B, (lead + size) * B)
                both = lanes_dot(solved[:, span], high[:, :size * B])
                more = lanes_dot(solved[:width, span], low[:, :size * B])
                total[...] += both[:width] + both[width:] + more

    out[...] = total[...]


def image(covariance, solved, order_in, order_out, counts, cap_out, name):
    width = solved.shape[0] // 2
    cap_in = solved.shape[1] // B
    rows, blocks = covariance.shape[0], covariance.shape[1]
    flat = covariance.reshape(rows * blocks, B)
    chunk = 4
    group = 4

    def place(which):
        def index_map(i, order_in, order_out, counts):
            last = jnp.maximum(counts[1] - 1, 0)
            return (order_out[jnp.minimum(group * i + which, last)], 0)

        return pl.BlockSpec((B * blocks, B), index_map)

    grid_spec = pltpu.PrefetchScalarGridSpec(
        num_scalar_prefetch=3,
        grid=(pl.cdiv(cap_out, group),),
        in_specs=[
            pl.BlockSpec(solved.shape, lambda i, *_: (0, 0), pipeline_mode=pl.Buffered(1)),
            *[place(which) for which in range(group)],
        ],
        out_specs=pl.BlockSpec((width, group * B), lambda i, *_: (0, i)),
        scratch_shapes=[
            pltpu.VMEM((group * B, chunk * B), jnp.bfloat16),
            pltpu.VMEM((group * B, chunk * B), jnp.bfloat16),
            pltpu.VMEM((width, group * B), jnp.float32),
        ],
    )
    return pl.pallas_call(
        functools.partial(image_kernel, blocks, cap_in, chunk, group),
        name=name,
        grid_spec=grid_spec,
        out_shape=shape_of((width, cap_out * B)),
        compiler_params=pltpu.CompilerParams(vmem_limit_bytes=VMEM_LIMIT),
        cost_estimate=pl.CostEstimate(
            flops=6 * width * cap_in * B * cap_out * B,
            bytes_accessed=4 * cap_out * B * blocks * B + 8 * width * cap_out * B,
            transcendentals=0,
        ),
    )(order_in, order_out, counts, solved, *[flat] * group)


def unpack_kernel(blocks, cap, which, order, counts, packed, out):
    share = packed.shape[0]
    out[...] = jnp.zeros_like(out)
    for i in range(min(cap, blocks)):

        @pl.when(i < counts[which])
        def _():
            out[pl.ds(order[i], share, stride=blocks), :] = -packed[:, i * B:(i + 1) * B]


def unpack(packed, order, counts, which, blocks, name):
    share, cap = packed.shape[0], packed.shape[1] // B
    return call(
        functools.partial(unpack_kernel, blocks, cap, which),
        name,
        shape_of((share * blocks, B)),
        (order, counts, packed),
        1,
        in_specs=[SMEM, SMEM, VMEM],
    )


def gram_one_kernel(image_rows, solved_one, solved_two, out):
    grid_size, _, share = out.shape
    width = solved_one.shape[0] // 2
    rows = split(image_rows[...])
    for half, solved in enumerate((solved_one, solved_two)):
        product = three_products(lanes_dot, rows, (solved[:width, :], solved[width:, :]))
        for k in range(grid_size):
            out[k, half * share:(half + 1) * share, :] = product[:, k * share:(k + 1) * share]


def gram_two_kernel(image_rows, solved_root, image_parent, parent, out):
    grid_size, share, _ = out.shape
    width = solved_root.shape[0] // 2
    rows = split(image_rows[...])
    product = three_products(lanes_dot, rows, (solved_root[:width, :], solved_root[width:, :]))
    product = product + three_products(
        lanes_dot, split(image_parent[...].T), split(parent[...])
    )
    for k in range(grid_size):
        out[k, :, :] = product[:, k * share:(k + 1) * share]


def swap_grid(block, grid_size):
    pairs = [
        (r * grid_size + c, c * grid_size + r) for r in range(grid_size) for c in range(grid_size)
    ]
    return lax.ppermute(block, ("row", "col"), pairs)


def scatter_sum(pieces, grid_size, position):
    total = lax.dynamic_index_in_dim(pieces, position, 0, keepdims=False)
    for shift in range(1, grid_size):
        target = lax.rem(position + shift, grid_size)
        piece = lax.dynamic_index_in_dim(pieces, target, 0, keepdims=False)
        total = total + lax.ppermute(
            piece, "row", [(i, (i + shift) % grid_size) for i in range(grid_size)]
        )
    return total


def gather_rows(block, grid_size, position):
    gathered = jnp.zeros((grid_size,) + block.shape, block.dtype)
    gathered = lax.dynamic_update_index_in_dim(gathered, block, position, 0)
    for shift in range(1, grid_size):
        other = lax.ppermute(block, "row", [(i, (i + shift) % grid_size) for i in range(grid_size)])
        source = lax.rem(position + grid_size - shift, grid_size)
        gathered = lax.dynamic_update_index_in_dim(gathered, other, source, 0)
    return gathered


def flip(block, axis, bit, grid_size):
    return lax.ppermute(block, axis, [(i, i ^ bit) for i in range(grid_size)])


def gather_cols(block, grid_size):
    if grid_size != 4:
        gathered = lax.all_gather(block, "col")
        position = lax.axis_index("col")
        return [
            lax.dynamic_index_in_dim(gathered, position ^ j, 0, keepdims=False)
            for j in range(grid_size)
        ]
    far = flip(block, "col", 2, grid_size)
    near = flip(block, "col", 1, grid_size)
    return [block, near, far, flip(far, "col", 1, grid_size)]


def run(
    cap_one, cap_two, row_order, col_order, info, place, root_covariance, factor_one, inverse_one,
    factor_parent, factor_root, inverse_two,
):
    grid_size = lax.axis_size("row")
    row = lax.axis_index("row")
    col = lax.axis_index("col")
    share, width = inverse_one.shape
    blocks = root_covariance.shape[3]
    covariance = root_covariance.reshape(-1, blocks, B)
    row_info, col_info = info, info[2:4]

    packed_one, packed_two = call(
        functools.partial(pack_kernel, cap_one, cap_two),
        "pack",
        (shape_of((cap_one * B + width, share)), shape_of((cap_two * B + width + share, share))),
        (
            row_order, row_info, factor_one.reshape(blocks, B, share), inverse_one,
            factor_parent, factor_root.reshape(blocks, B, share), inverse_two,
        ),
        1,
        in_specs=[SMEM, SMEM] + [VMEM] * 5,
    )
    gathered_one = gather_cols(packed_one, grid_size)
    gathered_two = gather_cols(packed_two, grid_size)

    solved_one = call(
        functools.partial(solve_one_kernel, cap_one),
        "solve_one",
        shape_of((2 * width, cap_one * B), jnp.bfloat16),
        gathered_one,
        6 * width * width * cap_one * B,
    )
    counts = jnp.stack([info[0], info[2]])
    image_one = image(covariance, solved_one, row_order, col_order, counts, cap_one, "image_one")
    image_one = lax.psum_scatter(image_one, "row", scatter_dimension=0, tiled=True)

    parent = call(
        functools.partial(parent_kernel, cap_two),
        "parent",
        shape_of((width, share)),
        gathered_two,
        6 * width * width * share,
    )
    parents = gather_rows(parent, grid_size, row)
    solved_two, solved_root, lead, diag_one, diag_two = call(
        functools.partial(solve_two_kernel, cap_one, cap_two),
        "solve_two",
        (
            shape_of((2 * width, cap_one * B), jnp.bfloat16),
            shape_of((2 * width, cap_two * B), jnp.bfloat16),
            shape_of((share, width)),
            shape_of((share, share)),
            shape_of((share, share)),
        ),
        (place, parents, *gathered_one, *gathered_two),
        6 * width * width * (cap_one + cap_two) * B,
        in_specs=[SMEM] + [VMEM] * (1 + 2 * grid_size),
        scratch=[pltpu.VMEM((width, width), jnp.bfloat16)] * 2,
    )
    counts = jnp.stack([info[0], info[3]])
    image_two = image(covariance, solved_two, row_order, col_order, counts, cap_two, "image_two")
    image_two = lax.psum_scatter(image_two, "row", scatter_dimension=0, tiled=True)

    rows_one = swap_grid(image_one, grid_size)
    cross_one = unpack(image_one, col_order, col_info, 0, blocks, "cross_one")
    gram_one = call(
        gram_one_kernel,
        "gram_one",
        shape_of((grid_size, 2 * share, share)),
        (rows_one, solved_one, solved_two),
        12 * share * width * cap_one * B,
    )
    image_two, gram_one, cross_one = lax.optimization_barrier((image_two, gram_one, cross_one))
    rows_two = swap_grid(image_two, grid_size)
    gram_one = scatter_sum(gram_one, grid_size, row)
    block_one = gram_one[:share] + diag_one
    mixed = swap_grid(gram_one[share:], grid_size)
    own_lead = lax.dynamic_slice_in_dim(lead, col * share, share, 1)
    parent_out = -lead
    for j, piece in enumerate(gather_cols(mixed, grid_size)):
        start = (col ^ j) * share
        here = lax.dynamic_slice_in_dim(parent_out, start, share, 1)
        parent_out = lax.dynamic_update_slice_in_dim(parent_out, here + piece, start, 1)

    cross_two = unpack(image_two, col_order, col_info, 1, blocks, "cross_two")
    gram_two = call(
        gram_two_kernel,
        "gram_two",
        shape_of((grid_size, share, share)),
        (rows_two, solved_root, own_lead - mixed, parent),
        6 * share * width * cap_two * B,
    )
    block_two = scatter_sum(gram_two, grid_size, row) + diag_two
    return cross_one, block_one, parent_out, cross_two, block_two


def capacities_of(blocks):
    parts = ((0.7, 0.55), (0.75, 0.6), (0.8, 0.65), (0.9, 0.7)) if blocks >= 16 else ()
    return [(round(one * blocks), round(two * blocks)) for one, two in parts] + [(blocks, blocks)]


def local(
    root_covariance, factor_one, inverse_one, pattern_one, factor_parent, factor_root, inverse_two,
    pattern_two,
):
    blocks = root_covariance.shape[3]
    capacities = capacities_of(blocks)
    place = jnp.stack([lax.axis_index("row"), lax.axis_index("col")]).astype(jnp.int32)
    row_order, col_order, info = pl.pallas_call(
        functools.partial(plan_kernel, capacities),
        name="plan",
        out_shape=(
            shape_of((blocks,), jnp.int32), shape_of((blocks,), jnp.int32), shape_of((5,), jnp.int32)
        ),
        in_specs=[SMEM] * 3,
        out_specs=(SMEM,) * 3,
    )(place, pattern_one, pattern_two)
    operands = (
        row_order, col_order, info, place, root_covariance, factor_one, inverse_one,
        factor_parent, factor_root, inverse_two,
    )
    branches = [functools.partial(run, one, two) for one, two in capacities]
    if len(branches) == 1:
        results = branches[0](*operands)
    else:
        results = lax.switch(info[4], branches, *operands)
    cross_one, block_one, parent_out, cross_two, block_two = results
    cross_one = cross_one.reshape(-1, blocks, 1, B)
    cross_two = cross_two.reshape(-1, blocks, 1, B)
    return cross_one, block_one, parent_out, cross_two, block_two


def solution(mesh):
    return jax.shard_map(
        local,
        mesh=mesh,
        in_specs=(
            P("grp", "col", None, None, "row", None),
            P("grp", "row", None, "col"),
            P(("grp", "col"), None),
            P("grp"),
            P(("grp", "row"), "col"),
            P("grp", "row", None, "col"),
            P(("grp", "col"), None),
            P("grp"),
        ),
        out_specs=(
            P(("grp", "row"), None, "col", None),
            P(("grp", "col"), "row"),
            P(("grp", "row"), None),
            P(("grp", "row"), None, "col", None),
            P(("grp", "col"), "row"),
        ),
        check_vma=False,
    )
```

```python
import functools

import jax
import jax.numpy as jnp
from jax import lax
from jax.experimental import pallas as pl
from jax.experimental.pallas import tpu as pltpu
from jax.sharding import PartitionSpec as P

B = 128
VMEM_LIMIT = 52 * 1024 * 1024
GROUP = 4
VMEM = pl.BlockSpec(memory_space=pltpu.VMEM)
SMEM = pl.BlockSpec(memory_space=pltpu.SMEM)


def split(values):
    high = values.astype(jnp.bfloat16)
    low = (values - high.astype(jnp.float32)).astype(jnp.bfloat16)
    return high, low


def lanes_dot(left, right):
    return lax.dot_general(
        left, right, (((1,), (1,)), ((), ())), preferred_element_type=jnp.float32
    )


def plain_dot(left, right):
    return lax.dot_general(
        left, right, (((1,), (0,)), ((), ())), preferred_element_type=jnp.float32
    )


def three_products(dot, left, right):
    left_high, left_low = left
    right_high, right_low = right
    rows = left_high.shape[0]
    both = dot(jnp.concatenate([left_high, left_low], 0), right_high)
    return both[:rows] + both[rows:] + dot(left_high, right_low)


def stacked(high, low):
    return jnp.concatenate([high, low], 0)


def call(kernel, name, out_shape, operands, flops, in_specs=None, scratch=()):
    size = sum(a.size * a.dtype.itemsize for a in operands)
    size += sum(a.size * a.dtype.itemsize for a in jax.tree.leaves(out_shape))
    return pl.pallas_call(
        kernel,
        name=name,
        out_shape=out_shape,
        in_specs=in_specs or [VMEM] * len(operands),
        out_specs=jax.tree.map(lambda _: VMEM, out_shape),
        scratch_shapes=scratch,
        compiler_params=pltpu.CompilerParams(vmem_limit_bytes=VMEM_LIMIT),
        cost_estimate=pl.CostEstimate(flops=flops, bytes_accessed=size, transcendentals=0),
    )(*operands)


def shape_of(shape, dtype=jnp.float32):
    return jax.ShapeDtypeStruct(shape, dtype)


def plan_kernel(capacities, place, pattern_one, pattern_two, row_order, col_order, info):
    blocks = row_order.shape[0]
    grid_size = pattern_one.shape[0] // blocks
    largest_one, largest_two = jnp.int32(0), jnp.int32(0)
    counts_one, counts_two = [], []
    for p in range(grid_size):

        def count(b, carry):
            return (
                carry[0] + pattern_one[b * grid_size + p],
                carry[1] + pattern_two[b * grid_size + p],
            )

        one, two = lax.fori_loop(0, blocks, count, (jnp.int32(0), jnp.int32(0)))
        counts_one.append(one)
        counts_two.append(two)
        largest_one = jnp.maximum(largest_one, one)
        largest_two = jnp.maximum(largest_two, two)
    choice = jnp.int32(len(capacities) - 1)
    for i in reversed(range(len(capacities) - 1)):
        fits = (largest_one <= capacities[i][0]) & (largest_two <= capacities[i][1])
        choice = jnp.where(fits, i, choice)
    info[4] = choice
    for axis, order in enumerate((row_order, col_order)):
        position = place[axis]
        own_one, own_two = jnp.int32(0), jnp.int32(0)
        for p in range(grid_size):
            own_one = jnp.where(position == p, counts_one[p], own_one)
            own_two = jnp.where(position == p, counts_two[p], own_two)
        info[2 * axis] = own_one
        info[2 * axis + 1] = own_two

        def put(b, carry):
            one = pattern_one[b * grid_size + position]
            two = pattern_two[b * grid_size + position]
            slot = jnp.where(two > 0, carry[0], jnp.where(one > 0, carry[1], carry[2]))
            order[slot] = b
            return (carry[0] + two, carry[1] + one - two, carry[2] + 1 - one)

        lax.fori_loop(0, blocks, put, (jnp.int32(0), own_two, own_one))


def pack_one_kernel(cap, order, info, factor, inverse, out, out_bare):
    for i in range(cap):
        block = jnp.where(i < info[0], factor[order[i]], 0.0)
        out[pl.ds(i * B, B), :] = block
        out_bare[pl.ds(i * B, B), :] = block
    out[pl.ds(cap * B, inverse.shape[1]), :] = inverse[...].T


def pack_two_kernel(cap, order, info, place, factor, inverse, *refs):
    parents, out = refs[:-1], refs[-1]
    width = inverse.shape[1]
    share = parents[0].shape[0]
    grid_size = len(parents)
    for i in range(cap):
        out[pl.ds(i * B, B), :] = jnp.where(i < info[1], factor[order[i]], 0.0)
    out[pl.ds(cap * B, width), :] = inverse[...].T
    for shift, parent in enumerate(parents):
        source = lax.rem(place[0] + grid_size - shift, grid_size)
        start = pl.multiple_of(source * share, share)
        out[pl.ds(cap * B + width + start, share), :] = parent[...]


def joined(refs, start, size):
    return jnp.concatenate([ref[pl.ds(start, size), :] for ref in refs], 1)


def over_rows(first, last, step, body):
    whole = (last - first) // step

    def turn(i, carry):
        body(pl.multiple_of(first * B + i * (step * B), B), step * B)
        return carry

    lax.fori_loop(0, whole, turn, 0)
    rest = last - first - whole * step
    if rest:
        body((first + whole * step) * B, rest * B)


def solve_rows(inverse, refs, out, cap):
    width = out.shape[0] // 2

    def body(start, size):
        rows = split(joined(refs, start, size))
        high, low = split(three_products(lanes_dot, inverse, rows))
        out[:width, pl.ds(start, size)] = high
        out[width:, pl.ds(start, size)] = low

    over_rows(0, cap, GROUP, body)


def solve_one_kernel(cap, *refs):
    gathered, out, out_inverse = refs[:-2], refs[-2], refs[-1]
    width = out.shape[0] // 2
    inverse = split(joined(gathered, cap * B, width))
    out_inverse[...] = stacked(*inverse)
    solve_rows(inverse, gathered, out, cap)


def solve_far_kernel(cap, inverse, *refs):
    gathered, out = refs[:-1], refs[-1]
    width = out.shape[0] // 2
    if out.shape[1] > cap * B:
        out[:, cap * B:] = jnp.zeros((2 * width, out.shape[1] - cap * B), out.dtype)
    solve_rows((inverse[:width, :], inverse[width:, :]), gathered, out, cap)


def solve_two_kernel(cap_one, cap_two, grid_size, place, *refs):
    gathered_one, gathered_two = refs[:grid_size], refs[grid_size:2 * grid_size]
    (
        out_full, out_root, out_lead, out_diag_one, out_diag_two, out_parent, weight_high, weight_low
    ) = refs[2 * grid_size:]
    share, width = out_lead.shape
    row, col = place[0], place[1]
    inverse = split(joined(gathered_two, cap_two * B, width))
    parent_start = cap_two * B + width
    parent = split(joined(gathered_two, parent_start, width))
    solved_parent = split(three_products(lanes_dot, inverse, parent))
    row_start = parent_start + pl.multiple_of(row * share, share)
    out_parent[...] = three_products(lanes_dot, inverse, split(joined(gathered_two, row_start, share)))
    for k in range(grid_size):
        piece = split(gathered_one[k][pl.ds(cap_one * B, width), :])
        high, low = split(three_products(plain_dot, solved_parent, piece))
        weight_high[:, k * share:(k + 1) * share] = high
        weight_low[:, k * share:(k + 1) * share] = low
    weight = (weight_high[...], weight_low[...])
    row_start = cap_one * B + pl.multiple_of(row * share, share)
    col_start = cap_one * B + pl.multiple_of(col * share, share)
    inv_row = split(joined(gathered_one, row_start, share))
    inv_col = split(joined(gathered_one, col_start, share))
    out_lead[...] = three_products(lanes_dot, inv_row, weight)
    out_diag_one[...] = three_products(lanes_dot, inv_col, inv_row)
    row_start = cap_two * B + pl.multiple_of(row * share, share)
    col_start = cap_two * B + pl.multiple_of(col * share, share)
    inv_row = split(joined(gathered_two, row_start, share))
    inv_col = split(joined(gathered_two, col_start, share))
    out_diag_two[...] = three_products(lanes_dot, inv_col, inv_row)

    def both(start, size):
        own = three_products(lanes_dot, inverse, split(joined(gathered_two, start, size)))
        high, low = split(own)
        out_root[:width, pl.ds(start, size)] = high
        out_root[width:, pl.ds(start, size)] = low
        other = three_products(lanes_dot, weight, split(joined(gathered_one, start, size)))
        high, low = split(own - other)
        out_full[:width, pl.ds(start, size)] = high
        out_full[width:, pl.ds(start, size)] = low

    def first_only(start, size):
        other = three_products(lanes_dot, weight, split(joined(gathered_one, start, size)))
        high, low = split(-other)
        out_full[:width, pl.ds(start, size)] = high
        out_full[width:, pl.ds(start, size)] = low

    over_rows(0, cap_two, GROUP, both)
    over_rows(cap_two, cap_one, GROUP, first_only)


def image_kernel(
    blocks, cap, chunk, group, order_in, order_out, counts, solved, *refs
):
    covs, (out, high, low, total) = refs[:group], refs[group:]
    step = pl.program_id(0)
    width = out.shape[0]
    total[...] = jnp.zeros_like(total)

    @pl.when(group * step < counts[1])
    def _():
        for lead in range(0, cap, chunk):
            size = min(chunk, cap - lead)

            @pl.when(lead < counts[0])
            def _():
                for j in range(size):
                    for part, cov in enumerate(covs):
                        piece = cov[pl.ds(order_in[lead + j], B, stride=blocks), :]
                        piece_high, piece_low = split(piece)
                        high[part * B:(part + 1) * B, j * B:(j + 1) * B] = piece_high
                        low[part * B:(part + 1) * B, j * B:(j + 1) * B] = piece_low
                span = slice(lead * B, (lead + size) * B)
                both = lanes_dot(solved[:, span], high[:, :size * B])
                more = lanes_dot(solved[:width, span], low[:, :size * B])
                total[...] += both[:width] + both[width:] + more

    out[...] = total[...]


def image(covariance, solved, order_in, order_out, counts, cap_out, name):
    width = solved.shape[0] // 2
    cap_in = solved.shape[1] // B
    rows, blocks = covariance.shape[0], covariance.shape[1]
    flat = covariance.reshape(rows * blocks, B)
    chunk = GROUP
    group = GROUP

    def place(which):
        def index_map(i, order_in, order_out, counts):
            last = jnp.maximum(counts[1] - 1, 0)
            return (order_out[jnp.minimum(group * i + which, last)], 0)

        return pl.BlockSpec((B * blocks, B), index_map)

    grid_spec = pltpu.PrefetchScalarGridSpec(
        num_scalar_prefetch=3,
        grid=(pl.cdiv(cap_out, group),),
        in_specs=[
            pl.BlockSpec(solved.shape, lambda i, *_: (0, 0), pipeline_mode=pl.Buffered(1)),
            *[place(which) for which in range(group)],
        ],
        out_specs=pl.BlockSpec((width, group * B), lambda i, *_: (0, i)),
        scratch_shapes=[
            pltpu.VMEM((group * B, chunk * B), jnp.bfloat16),
            pltpu.VMEM((group * B, chunk * B), jnp.bfloat16),
            pltpu.VMEM((width, group * B), jnp.float32),
        ],
    )
    return pl.pallas_call(
        functools.partial(image_kernel, blocks, cap_in, chunk, group),
        name=name,
        grid_spec=grid_spec,
        out_shape=shape_of((width, cap_out * B)),
        compiler_params=pltpu.CompilerParams(vmem_limit_bytes=VMEM_LIMIT),
        cost_estimate=pl.CostEstimate(
            flops=6 * width * cap_in * B * cap_out * B,
            bytes_accessed=4 * cap_out * B * blocks * B + 8 * width * cap_out * B,
            transcendentals=0,
        ),
    )(order_in, order_out, counts, solved, *[flat] * group)


def mirror_kernel(blocks, cap, group, order_in, order_out, counts, solved, *refs):
    covs, (out, high, low) = refs[:group], refs[group:]
    step = pl.program_id(0)
    width = out.shape[0]

    @pl.when(step == 0)
    def _():
        out[...] = jnp.zeros_like(out)

    @pl.when(group * step < counts[0])
    def _():
        for lead in range(0, cap, group):
            size = min(group, cap - lead)

            @pl.when(lead < counts[1])
            def _():
                for j in range(size):
                    for part, cov in enumerate(covs):
                        piece = cov[pl.ds(order_out[lead + j], B, stride=blocks), :]
                        piece_high, piece_low = split(piece)
                        high[part * B:(part + 1) * B, j * B:(j + 1) * B] = piece_high
                        low[part * B:(part + 1) * B, j * B:(j + 1) * B] = piece_low
                both = plain_dot(solved[...], high[:, :size * B])
                more = plain_dot(solved[:width, :], low[:, :size * B])
                out[:, lead * B:(lead + size) * B] += both[:width] + both[width:] + more


def mirror_image(covariance, solved, order_in, order_out, counts, cap, name):
    width = solved.shape[0] // 2
    rows, blocks = covariance.shape[0], covariance.shape[1]
    flat = covariance.reshape(rows * blocks, B)
    group = GROUP

    def place(which):
        def index_map(i, order_in, order_out, counts):
            last = jnp.maximum(counts[0] - 1, 0)
            return (order_in[jnp.minimum(group * i + which, last)], 0)

        return pl.BlockSpec((B * blocks, B), index_map)

    grid_spec = pltpu.PrefetchScalarGridSpec(
        num_scalar_prefetch=3,
        grid=(solved.shape[1] // (group * B),),
        in_specs=[
            pl.BlockSpec((2 * width, group * B), lambda i, *_: (0, i)),
            *[place(which) for which in range(group)],
        ],
        out_specs=pl.BlockSpec((width, cap * B), lambda i, *_: (0, 0)),
        scratch_shapes=[pltpu.VMEM((group * B, group * B), jnp.bfloat16)] * 2,
    )
    return pl.pallas_call(
        functools.partial(mirror_kernel, blocks, cap, group),
        name=name,
        grid_spec=grid_spec,
        out_shape=shape_of((width, cap * B)),
        compiler_params=pltpu.CompilerParams(vmem_limit_bytes=VMEM_LIMIT),
        cost_estimate=pl.CostEstimate(
            flops=6 * width * cap * B * cap * B,
            bytes_accessed=4 * cap * B * blocks * B + 8 * width * cap * B,
            transcendentals=0,
        ),
    )(order_in, order_out, counts, solved, *[flat] * group)


def unpack_kernel(blocks, cap, which, order, counts, packed, out):
    share = packed.shape[0]
    out[...] = jnp.zeros_like(out)
    for i in range(min(cap, blocks)):

        @pl.when(i < counts[which])
        def _():
            out[pl.ds(order[i], share, stride=blocks), :] = -packed[:, i * B:(i + 1) * B]


def unpack(packed, order, counts, which, blocks, name):
    share, cap = packed.shape[0], packed.shape[1] // B
    return call(
        functools.partial(unpack_kernel, blocks, cap, which),
        name,
        shape_of((share * blocks, B)),
        (order, counts, packed),
        1,
        in_specs=[SMEM, SMEM, VMEM],
    )


def gram_one_kernel(image_rows, solved_one, solved_two, out):
    grid_size, _, share = out.shape
    width = solved_one.shape[0] // 2
    rows = split(image_rows[...])
    for half, solved in enumerate((solved_one, solved_two)):
        product = three_products(lanes_dot, rows, (solved[:width, :], solved[width:, :]))
        for k in range(grid_size):
            out[k, half * share:(half + 1) * share, :] = product[:, k * share:(k + 1) * share]


def gram_two_kernel(image_rows, solved_root, image_parent, parent, out):
    grid_size, share, _ = out.shape
    width = solved_root.shape[0] // 2
    rows = split(image_rows[...])
    product = three_products(lanes_dot, rows, (solved_root[:width, :], solved_root[width:, :]))
    product = product + three_products(
        lanes_dot, split(image_parent[...].T), split(parent[...])
    )
    for k in range(grid_size):
        out[k, :, :] = product[:, k * share:(k + 1) * share]


def swap_grid(block, grid_size):
    pairs = [
        (r * grid_size + c, c * grid_size + r) for r in range(grid_size) for c in range(grid_size)
    ]
    return lax.ppermute(block, ("row", "col"), pairs)


def scatter_sum(pieces, grid_size, position):
    total = lax.dynamic_index_in_dim(pieces, position, 0, keepdims=False)
    for shift in range(1, grid_size):
        target = lax.rem(position + shift, grid_size)
        piece = lax.dynamic_index_in_dim(pieces, target, 0, keepdims=False)
        total = total + lax.ppermute(
            piece, "row", [(i, (i + shift) % grid_size) for i in range(grid_size)]
        )
    return total


def gather_rows(block, grid_size):
    return [block] + [
        lax.ppermute(block, "row", [(i, (i + shift) % grid_size) for i in range(grid_size)])
        for shift in range(1, grid_size)
    ]


def plane_sum(partial, grid_size, col):
    if grid_size != 4:
        return lax.psum_scatter(partial, "col", scatter_dimension=0, tiled=True)
    share = partial.shape[0] // grid_size
    core, chip = col % 2, col // 2
    pieces = partial.reshape(2, 2, share, partial.shape[1])
    away = lax.dynamic_index_in_dim(pieces, 1 - core, 1, keepdims=False)
    stay = lax.dynamic_index_in_dim(pieces, core, 1, keepdims=False)
    pieces = stay + flip(away, "col", 1, grid_size)
    away = lax.dynamic_index_in_dim(pieces, 1 - chip, 0, keepdims=False)
    stay = lax.dynamic_index_in_dim(pieces, chip, 0, keepdims=False)
    return stay + flip(away, "col", 2, grid_size)


def flip(block, axis, bit, grid_size):
    return lax.ppermute(block, axis, [(i, i ^ bit) for i in range(grid_size)])


def gather_cols(block, grid_size):
    if grid_size != 4:
        gathered = lax.all_gather(block, "col")
        position = lax.axis_index("col")
        return [
            lax.dynamic_index_in_dim(gathered, position ^ j, 0, keepdims=False)
            for j in range(grid_size)
        ]
    far = flip(block, "col", 2, grid_size)
    near = flip(block, "col", 1, grid_size)
    return [block, near, far, flip(far, "col", 1, grid_size)]


def run(
    cap_one, cap_two, row_order, col_order, info, place, root_covariance, factor_one, inverse_one,
    factor_parent, factor_root, inverse_two,
):
    grid_size = lax.axis_size("row")
    row = lax.axis_index("row")
    col = lax.axis_index("col")
    share, width = inverse_one.shape
    blocks = root_covariance.shape[3]
    covariance = root_covariance.reshape(-1, blocks, B)
    col_info = info[2:4]

    packed_one, bare_one = call(
        functools.partial(pack_one_kernel, cap_one),
        "pack_one",
        (shape_of((cap_one * B + width, share)), shape_of((cap_one * B, share))),
        (row_order, info, factor_one.reshape(blocks, B, share), inverse_one),
        1,
        in_specs=[SMEM, SMEM, VMEM, VMEM],
    )
    all_rows = lax.all_gather(bare_one, "row")
    gathered_one = gather_cols(packed_one, grid_size)
    packed_two = call(
        functools.partial(pack_two_kernel, cap_two),
        "pack_two",
        shape_of((cap_two * B + 2 * width, share)),
        (
            row_order, info, place, factor_root.reshape(blocks, B, share), inverse_two,
            *gather_rows(factor_parent, grid_size),
        ),
        1,
        in_specs=[SMEM] * 3 + [VMEM] * (2 + grid_size),
    )
    gathered_two = gather_cols(packed_two, grid_size)

    solved_one, lead_inverse = call(
        functools.partial(solve_one_kernel, cap_one),
        "solve_one",
        (
            shape_of((2 * width, cap_one * B), jnp.bfloat16),
            shape_of((2 * width, width), jnp.bfloat16),
        ),
        gathered_one,
        6 * width * width * cap_one * B,
    )
    solved_two, solved_root, lead, diag_one, diag_two, parent = call(
        functools.partial(solve_two_kernel, cap_one, cap_two, grid_size),
        "solve_two",
        (
            shape_of((2 * width, cap_one * B), jnp.bfloat16),
            shape_of((2 * width, cap_two * B), jnp.bfloat16),
            shape_of((share, width)),
            shape_of((share, share)),
            shape_of((share, share)),
            shape_of((width, share)),
        ),
        (place, *gathered_one, *gathered_two),
        6 * width * width * (cap_one + cap_two) * B,
        in_specs=[SMEM] + [VMEM] * (2 * grid_size),
        scratch=[pltpu.VMEM((width, width), jnp.bfloat16)] * 2,
    )
    counts = jnp.stack([info[0], info[3]])
    image_two = image(covariance, solved_two, row_order, col_order, counts, cap_two, "image_two")
    image_two = lax.psum_scatter(image_two, "row", scatter_dimension=0, tiled=True)

    far_rows = []
    for j in range(grid_size):
        piece = lax.dynamic_index_in_dim(all_rows, col ^ j, 0, keepdims=False)
        far_rows.append(flip(piece, "col", j, grid_size) if j else piece)
    solved_far = call(
        functools.partial(solve_far_kernel, cap_one),
        "solve_far",
        shape_of((2 * width, pl.cdiv(cap_one, GROUP) * GROUP * B), jnp.bfloat16),
        (lead_inverse, *far_rows),
        6 * width * width * cap_one * B,
    )
    counts = jnp.stack([info[2], info[0]])
    rows_one = mirror_image(
        covariance, solved_far, col_order, row_order, counts, cap_one, "image_one"
    )
    rows_one = plane_sum(rows_one, grid_size, col)
    image_one = swap_grid(rows_one, grid_size)
    cross_one = unpack(image_one, col_order, col_info, 0, blocks, "cross_one")
    gram_one = call(
        gram_one_kernel,
        "gram_one",
        shape_of((grid_size, 2 * share, share)),
        (rows_one, solved_one, solved_two),
        12 * share * width * cap_one * B,
    )
    rows_two = swap_grid(image_two, grid_size)
    gram_one = scatter_sum(gram_one, grid_size, row)
    block_one = gram_one[:share] + diag_one
    mixed = swap_grid(gram_one[share:], grid_size)
    own_lead = lax.dynamic_slice_in_dim(lead, col * share, share, 1)
    parent_out = -lead
    for j, piece in enumerate(gather_cols(mixed, grid_size)):
        start = (col ^ j) * share
        here = lax.dynamic_slice_in_dim(parent_out, start, share, 1)
        parent_out = lax.dynamic_update_slice_in_dim(parent_out, here + piece, start, 1)

    cross_two = unpack(image_two, col_order, col_info, 1, blocks, "cross_two")
    gram_two = call(
        gram_two_kernel,
        "gram_two",
        shape_of((grid_size, share, share)),
        (rows_two, solved_root, own_lead - mixed, parent),
        6 * share * width * cap_two * B,
    )
    block_two = scatter_sum(gram_two, grid_size, row) + diag_two
    return cross_one, block_one, parent_out, cross_two, block_two


def capacities_of(blocks):
    parts = ((0.7, 0.55), (0.75, 0.6), (0.8, 0.65), (0.9, 0.7)) if blocks >= 16 else ()
    return [(round(one * blocks), round(two * blocks)) for one, two in parts] + [(blocks, blocks)]


def local(
    root_covariance, factor_one, inverse_one, pattern_one, factor_parent, factor_root, inverse_two,
    pattern_two,
):
    blocks = root_covariance.shape[3]
    capacities = capacities_of(blocks)
    place = jnp.stack([lax.axis_index("row"), lax.axis_index("col")]).astype(jnp.int32)
    row_order, col_order, info = pl.pallas_call(
        functools.partial(plan_kernel, capacities),
        name="plan",
        out_shape=(
            shape_of((blocks,), jnp.int32), shape_of((blocks,), jnp.int32), shape_of((5,), jnp.int32)
        ),
        in_specs=[SMEM] * 3,
        out_specs=(SMEM,) * 3,
    )(place, pattern_one, pattern_two)
    operands = (
        row_order, col_order, info, place, root_covariance, factor_one, inverse_one,
        factor_parent, factor_root, inverse_two,
    )
    branches = [functools.partial(run, one, two) for one, two in capacities]
    if len(branches) == 1:
        results = branches[0](*operands)
    else:
        results = lax.switch(info[4], branches, *operands)
    cross_one, block_one, parent_out, cross_two, block_two = results
    cross_one = cross_one.reshape(-1, blocks, 1, B)
    cross_two = cross_two.reshape(-1, blocks, 1, B)
    return cross_one, block_one, parent_out, cross_two, block_two


def solution(mesh):
    return jax.shard_map(
        local,
        mesh=mesh,
        in_specs=(
            P("grp", "col", None, None, "row", None),
            P("grp", "row", None, "col"),
            P(("grp", "col"), None),
            P("grp"),
            P(("grp", "row"), "col"),
            P("grp", "row", None, "col"),
            P(("grp", "col"), None),
            P("grp"),
        ),
        out_specs=(
            P(("grp", "row"), None, "col", None),
            P(("grp", "col"), "row"),
            P(("grp", "row"), None),
            P(("grp", "row"), None, "col", None),
            P(("grp", "col"), "row"),
        ),
        check_vma=False,
    )
```

```python
import functools

import jax
import jax.numpy as jnp
from jax import lax
from jax.experimental import pallas as pl
from jax.experimental.pallas import tpu as pltpu
from jax.sharding import PartitionSpec as P

B = 128
VMEM_LIMIT = 52 * 1024 * 1024
GROUP = 4
VMEM = pl.BlockSpec(memory_space=pltpu.VMEM)
SMEM = pl.BlockSpec(memory_space=pltpu.SMEM)


def split(values):
    high = values.astype(jnp.bfloat16)
    low = (values - high.astype(jnp.float32)).astype(jnp.bfloat16)
    return high, low


def lanes_dot(left, right):
    return lax.dot_general(
        left, right, (((1,), (1,)), ((), ())), preferred_element_type=jnp.float32
    )


def plain_dot(left, right):
    return lax.dot_general(
        left, right, (((1,), (0,)), ((), ())), preferred_element_type=jnp.float32
    )


def three_products(dot, left, right):
    left_high, left_low = left
    right_high, right_low = right
    rows = left_high.shape[0]
    both = dot(jnp.concatenate([left_high, left_low], 0), right_high)
    return both[:rows] + both[rows:] + dot(left_high, right_low)


def stacked(high, low):
    return jnp.concatenate([high, low], 0)


def call(kernel, name, out_shape, operands, flops, in_specs=None, scratch=()):
    size = sum(a.size * a.dtype.itemsize for a in operands)
    size += sum(a.size * a.dtype.itemsize for a in jax.tree.leaves(out_shape))
    return pl.pallas_call(
        kernel,
        name=name,
        out_shape=out_shape,
        in_specs=in_specs or [VMEM] * len(operands),
        out_specs=jax.tree.map(lambda _: VMEM, out_shape),
        scratch_shapes=scratch,
        compiler_params=pltpu.CompilerParams(vmem_limit_bytes=VMEM_LIMIT),
        cost_estimate=pl.CostEstimate(flops=flops, bytes_accessed=size, transcendentals=0),
    )(*operands)


def shape_of(shape, dtype=jnp.float32):
    return jax.ShapeDtypeStruct(shape, dtype)


def plan_kernel(capacities, place, pattern_one, pattern_two, row_order, col_order, info):
    blocks = row_order.shape[0]
    grid_size = pattern_one.shape[0] // blocks
    largest_one, largest_two = jnp.int32(0), jnp.int32(0)
    counts_one, counts_two = [], []
    for p in range(grid_size):

        def count(b, carry):
            return (
                carry[0] + pattern_one[b * grid_size + p],
                carry[1] + pattern_two[b * grid_size + p],
            )

        one, two = lax.fori_loop(0, blocks, count, (jnp.int32(0), jnp.int32(0)))
        counts_one.append(one)
        counts_two.append(two)
        largest_one = jnp.maximum(largest_one, one)
        largest_two = jnp.maximum(largest_two, two)
    choice = jnp.int32(len(capacities) - 1)
    for i in reversed(range(len(capacities) - 1)):
        fits = (largest_one <= capacities[i][0]) & (largest_two <= capacities[i][1])
        choice = jnp.where(fits, i, choice)
    info[4] = choice
    for axis, order in enumerate((row_order, col_order)):
        position = place[axis]
        own_one, own_two = jnp.int32(0), jnp.int32(0)
        for p in range(grid_size):
            own_one = jnp.where(position == p, counts_one[p], own_one)
            own_two = jnp.where(position == p, counts_two[p], own_two)
        info[2 * axis] = own_one
        info[2 * axis + 1] = own_two

        def put(b, carry):
            one = pattern_one[b * grid_size + position]
            two = pattern_two[b * grid_size + position]
            slot = jnp.where(two > 0, carry[0], jnp.where(one > 0, carry[1], carry[2]))
            order[slot] = b
            return (carry[0] + two, carry[1] + one - two, carry[2] + 1 - one)

        lax.fori_loop(0, blocks, put, (jnp.int32(0), own_two, own_one))


def pack_one_kernel(cap, order, info, factor, inverse_one, inverse_two, out, out_bare):
    width = inverse_one.shape[1]
    for i in range(cap):
        block = jnp.where(i < info[0], factor[order[i]], 0.0)
        out[pl.ds(i * B, B), :] = block
        out_bare[pl.ds(i * B, B), :] = block
    out[pl.ds(cap * B, width), :] = inverse_one[...].T
    out[pl.ds(cap * B + width, width), :] = inverse_two[...].T


def pack_two_kernel(cap, order, info, factor, out):
    for i in range(cap):
        out[pl.ds(i * B, B), :] = jnp.where(i < info[1], factor[order[i]], 0.0)


def place_kernel(place, *refs):
    pieces, out = refs[:-1], refs[-1]
    share = pieces[0].shape[0]
    grid_size = len(pieces)
    for shift, piece in enumerate(pieces):
        source = lax.rem(place[0] + grid_size - shift, grid_size)
        out[pl.ds(pl.multiple_of(source * share, share), share), :] = piece[...]


def joined(refs, start, size):
    return jnp.concatenate([ref[pl.ds(start, size), :] for ref in refs], 1)


def over_rows(first, last, step, body):
    whole = (last - first) // step

    def turn(i, carry):
        body(pl.multiple_of(first * B + i * (step * B), B), step * B)
        return carry

    lax.fori_loop(0, whole, turn, 0)
    rest = last - first - whole * step
    if rest:
        body((first + whole * step) * B, rest * B)


def solve_rows(inverse, refs, out, cap):
    width = out.shape[0] // 2

    def body(start, size):
        rows = split(joined(refs, start, size))
        high, low = split(three_products(lanes_dot, inverse, rows))
        out[:width, pl.ds(start, size)] = high
        out[width:, pl.ds(start, size)] = low

    over_rows(0, cap, GROUP, body)


def solve_one_kernel(cap, grid_size, place, *refs):
    gathered, parents = refs[:grid_size], refs[grid_size:2 * grid_size]
    (
        out, out_lag, out_inverse_one, out_inverse_two, out_lead, out_diag_one, out_diag_two,
        out_parent, weight_high, weight_low,
    ) = refs[2 * grid_size:]
    share, width = out_lead.shape
    row, col = place[0], place[1]
    first, second = cap * B, cap * B + width
    inverse = split(joined(gathered, first, width))
    out_inverse_one[...] = stacked(*inverse)
    inverse_two = split(joined(gathered, second, width))
    out_inverse_two[...] = stacked(*inverse_two)
    solved_parent = split(
        three_products(lanes_dot, inverse_two, split(joined(parents, 0, width)))
    )
    row_start = pl.multiple_of(row * share, share)
    col_start = pl.multiple_of(col * share, share)
    out_parent[...] = three_products(
        lanes_dot, inverse_two, split(joined(parents, row_start, share))
    )
    for k in range(grid_size):
        piece = split(gathered[k][pl.ds(first, width), :])
        high, low = split(three_products(plain_dot, solved_parent, piece))
        weight_high[:, k * share:(k + 1) * share] = high
        weight_low[:, k * share:(k + 1) * share] = low
    weight = (weight_high[...], weight_low[...])
    for start, diag in ((first, out_diag_one), (second, out_diag_two)):
        inv_row = split(joined(gathered, start + row_start, share))
        inv_col = split(joined(gathered, start + col_start, share))
        diag[...] = three_products(lanes_dot, inv_col, inv_row)
        if start == first:
            out_lead[...] = three_products(lanes_dot, inv_row, weight)

    def body(start, size):
        rows = split(joined(gathered, start, size))
        high, low = split(three_products(lanes_dot, inverse, rows))
        out[:width, pl.ds(start, size)] = high
        out[width:, pl.ds(start, size)] = low
        out_lag[:, pl.ds(start, size)] = three_products(lanes_dot, weight, rows)

    over_rows(0, cap, GROUP, body)


def solve_far_kernel(cap, inverse, *refs):
    gathered, out = refs[:-1], refs[-1]
    width = out.shape[0] // 2
    if out.shape[1] > cap * B:
        out[:, cap * B:] = jnp.zeros((2 * width, out.shape[1] - cap * B), out.dtype)
    solve_rows((inverse[:width, :], inverse[width:, :]), gathered, out, cap)


def solve_two_kernel(cap_one, cap_two, inverse, lag, *refs):
    gathered, (out_full, out_root) = refs[:-2], refs[-2:]
    width = lag.shape[0]
    halves = (inverse[:width, :], inverse[width:, :])

    def both(start, size):
        own = three_products(lanes_dot, halves, split(joined(gathered, start, size)))
        high, low = split(own)
        out_root[:width, pl.ds(start, size)] = high
        out_root[width:, pl.ds(start, size)] = low
        high, low = split(own - lag[:, pl.ds(start, size)])
        out_full[:width, pl.ds(start, size)] = high
        out_full[width:, pl.ds(start, size)] = low

    over_rows(0, cap_two, GROUP, both)
    if cap_one > cap_two:
        high, low = split(-lag[:, cap_two * B:])
        out_full[:width, cap_two * B:] = high
        out_full[width:, cap_two * B:] = low


def image_kernel(
    blocks, cap, chunk, group, order_in, order_out, counts, solved, *refs
):
    covs, (out, high, low, total) = refs[:group], refs[group:]
    step = pl.program_id(0)
    width = out.shape[0]
    total[...] = jnp.zeros_like(total)

    @pl.when(group * step < counts[1])
    def _():
        for lead in range(0, cap, chunk):
            size = min(chunk, cap - lead)

            @pl.when(lead < counts[0])
            def _():
                for j in range(size):
                    for part, cov in enumerate(covs):
                        piece = cov[pl.ds(order_in[lead + j], B, stride=blocks), :]
                        piece_high, piece_low = split(piece)
                        high[part * B:(part + 1) * B, j * B:(j + 1) * B] = piece_high
                        low[part * B:(part + 1) * B, j * B:(j + 1) * B] = piece_low
                span = slice(lead * B, (lead + size) * B)
                both = lanes_dot(solved[:, span], high[:, :size * B])
                more = lanes_dot(solved[:width, span], low[:, :size * B])
                total[...] += both[:width] + both[width:] + more

    out[...] = total[...]


def image(covariance, solved, order_in, order_out, counts, cap_out, name):
    width = solved.shape[0] // 2
    cap_in = solved.shape[1] // B
    rows, blocks = covariance.shape[0], covariance.shape[1]
    flat = covariance.reshape(rows * blocks, B)
    chunk = GROUP
    group = GROUP

    def place(which):
        def index_map(i, order_in, order_out, counts):
            last = jnp.maximum(counts[1] - 1, 0)
            return (order_out[jnp.minimum(group * i + which, last)], 0)

        return pl.BlockSpec((B * blocks, B), index_map)

    grid_spec = pltpu.PrefetchScalarGridSpec(
        num_scalar_prefetch=3,
        grid=(pl.cdiv(cap_out, group),),
        in_specs=[
            pl.BlockSpec(solved.shape, lambda i, *_: (0, 0), pipeline_mode=pl.Buffered(1)),
            *[place(which) for which in range(group)],
        ],
        out_specs=pl.BlockSpec((width, group * B), lambda i, *_: (0, i)),
        scratch_shapes=[
            pltpu.VMEM((group * B, chunk * B), jnp.bfloat16),
            pltpu.VMEM((group * B, chunk * B), jnp.bfloat16),
            pltpu.VMEM((width, group * B), jnp.float32),
        ],
    )
    return pl.pallas_call(
        functools.partial(image_kernel, blocks, cap_in, chunk, group),
        name=name,
        grid_spec=grid_spec,
        out_shape=shape_of((width, cap_out * B)),
        compiler_params=pltpu.CompilerParams(vmem_limit_bytes=VMEM_LIMIT),
        cost_estimate=pl.CostEstimate(
            flops=6 * width * cap_in * B * cap_out * B,
            bytes_accessed=4 * cap_out * B * blocks * B + 8 * width * cap_out * B,
            transcendentals=0,
        ),
    )(order_in, order_out, counts, solved, *[flat] * group)


def mirror_kernel(blocks, cap, group, lead_in, order_in, order_out, counts, solved, *refs):
    covs, (out, high, low) = refs[:group], refs[-3:]
    step = pl.program_id(0)
    width = out.shape[0]

    @pl.when(step == 0)
    def _():
        out[...] = refs[group][...] if len(refs) > group + 3 else jnp.zeros_like(out)

    @pl.when(lead_in + group * step < counts[0])
    def _():
        for lead in range(0, cap, group):
            size = min(group, cap - lead)

            @pl.when(lead < counts[1])
            def _():
                for j in range(size):
                    for part, cov in enumerate(covs):
                        piece = cov[pl.ds(order_out[lead + j], B, stride=blocks), :]
                        piece_high, piece_low = split(piece)
                        high[part * B:(part + 1) * B, j * B:(j + 1) * B] = piece_high
                        low[part * B:(part + 1) * B, j * B:(j + 1) * B] = piece_low
                both = plain_dot(solved[...], high[:, :size * B])
                more = plain_dot(solved[:width, :], low[:, :size * B])
                out[:, lead * B:(lead + size) * B] += both[:width] + both[width:] + more


def mirror_image(covariance, solved, order_in, order_out, counts, cap, lead_in, before, name):
    width = solved.shape[0] // 2
    rows, blocks = covariance.shape[0], covariance.shape[1]
    flat = covariance.reshape(rows * blocks, B)
    group = GROUP
    steps = solved.shape[1] // (group * B)

    def place(which):
        def index_map(i, order_in, order_out, counts):
            last = jnp.maximum(counts[0] - 1, 0)
            return (order_in[jnp.minimum(lead_in + group * i + which, last)], 0)

        return pl.BlockSpec((B * blocks, B), index_map)

    whole = pl.BlockSpec((width, cap * B), lambda i, *_: (0, 0), pipeline_mode=pl.Buffered(1))
    extra = () if before is None else (before,)
    grid_spec = pltpu.PrefetchScalarGridSpec(
        num_scalar_prefetch=3,
        grid=(steps,),
        in_specs=[
            pl.BlockSpec((2 * width, group * B), lambda i, *_: (0, i)),
            *[place(which) for which in range(group)],
            *[whole for _ in extra],
        ],
        out_specs=pl.BlockSpec((width, cap * B), lambda i, *_: (0, 0)),
        scratch_shapes=[pltpu.VMEM((group * B, group * B), jnp.bfloat16)] * 2,
    )
    return pl.pallas_call(
        functools.partial(mirror_kernel, blocks, cap, group, lead_in),
        name=name,
        grid_spec=grid_spec,
        out_shape=shape_of((width, cap * B)),
        compiler_params=pltpu.CompilerParams(vmem_limit_bytes=VMEM_LIMIT),
        cost_estimate=pl.CostEstimate(
            flops=6 * width * cap * B * solved.shape[1],
            bytes_accessed=4 * steps * group * B * blocks * B + 8 * width * cap * B,
            transcendentals=0,
        ),
    )(order_in, order_out, counts, solved, *[flat] * group, *extra)


def unpack_kernel(blocks, cap, which, order, counts, packed, out):
    share = packed.shape[0]
    out[...] = jnp.zeros_like(out)
    for i in range(min(cap, blocks)):

        @pl.when(i < counts[which])
        def _():
            out[pl.ds(order[i], share, stride=blocks), :] = -packed[:, i * B:(i + 1) * B]


def unpack(packed, order, counts, which, blocks, name):
    share, cap = packed.shape[0], packed.shape[1] // B
    return call(
        functools.partial(unpack_kernel, blocks, cap, which),
        name,
        shape_of((share * blocks, B)),
        (order, counts, packed),
        1,
        in_specs=[SMEM, SMEM, VMEM],
    )


def gram_one_kernel(image_rows, solved_one, solved_two, out):
    grid_size, _, share = out.shape
    width = solved_one.shape[0] // 2
    rows = split(image_rows[...])
    for half, solved in enumerate((solved_one, solved_two)):
        product = three_products(lanes_dot, rows, (solved[:width, :], solved[width:, :]))
        for k in range(grid_size):
            out[k, half * share:(half + 1) * share, :] = product[:, k * share:(k + 1) * share]


def gram_two_kernel(image_rows, solved_root, image_parent, parent, out):
    grid_size, share, _ = out.shape
    width = solved_root.shape[0] // 2
    rows = split(image_rows[...])
    product = three_products(lanes_dot, rows, (solved_root[:width, :], solved_root[width:, :]))
    product = product + three_products(
        lanes_dot, split(image_parent[...].T), split(parent[...])
    )
    for k in range(grid_size):
        out[k, :, :] = product[:, k * share:(k + 1) * share]


def swap_grid(block, grid_size):
    pairs = [
        (r * grid_size + c, c * grid_size + r) for r in range(grid_size) for c in range(grid_size)
    ]
    return lax.ppermute(block, ("row", "col"), pairs)


def scatter_pieces(pieces, grid_size, position):
    return [
        lax.dynamic_index_in_dim(pieces, lax.rem(position + shift, grid_size), 0, keepdims=False)
        for shift in range(grid_size)
    ]


def scatter_sum(pieces, grid_size):
    total = pieces[0]
    for shift in range(1, grid_size):
        total = total + lax.ppermute(
            pieces[shift], "row", [(i, (i + shift) % grid_size) for i in range(grid_size)]
        )
    return total


def gather_rows(block, grid_size):
    return [block] + [
        lax.ppermute(block, "row", [(i, (i + shift) % grid_size) for i in range(grid_size)])
        for shift in range(1, grid_size)
    ]


def plane_sum(partial, grid_size, col, other):
    if grid_size != 4:
        return lax.psum_scatter(partial, "col", scatter_dimension=0, tiled=True), other
    share = partial.shape[0] // grid_size
    core, chip = col % 2, col // 2
    pieces = partial.reshape(2, 2, share, partial.shape[1])
    away = lax.dynamic_index_in_dim(pieces, 1 - core, 1, keepdims=False)
    stay = lax.dynamic_index_in_dim(pieces, core, 1, keepdims=False)
    pieces = stay + flip(away, "col", 1, grid_size)
    pieces, other = lax.optimization_barrier((pieces, other))
    away = lax.dynamic_index_in_dim(pieces, 1 - chip, 0, keepdims=False)
    stay = lax.dynamic_index_in_dim(pieces, chip, 0, keepdims=False)
    return stay + flip(away, "col", 2, grid_size), other


def flip(block, axis, bit, grid_size):
    return lax.ppermute(block, axis, [(i, i ^ bit) for i in range(grid_size)])


def gather_cols(block, grid_size, after=None):
    if grid_size != 4:
        gathered = lax.all_gather(block, "col")
        position = lax.axis_index("col")
        return [
            lax.dynamic_index_in_dim(gathered, position ^ j, 0, keepdims=False)
            for j in range(grid_size)
        ]
    if after is not None:
        block, after[2] = lax.optimization_barrier((block, after[2]))
    far = flip(block, "col", 2, grid_size)
    near = flip(block, "col", 1, grid_size)
    return [block, near, far, flip(far, "col", 1, grid_size)]


def run(
    cap_one, cap_two, row_order, col_order, info, place, root_covariance, factor_one, inverse_one,
    factor_parent, factor_root, inverse_two,
):
    grid_size = lax.axis_size("row")
    row = lax.axis_index("row")
    col = lax.axis_index("col")
    share, width = inverse_one.shape
    blocks = root_covariance.shape[3]
    covariance = root_covariance.reshape(-1, blocks, B)
    col_info = info[2:4]

    packed_one, bare_one = call(
        functools.partial(pack_one_kernel, cap_one),
        "pack_one",
        (shape_of((cap_one * B + 2 * width, share)), shape_of((cap_one * B, share))),
        (row_order, info, factor_one.reshape(blocks, B, share), inverse_one, inverse_two),
        1,
        in_specs=[SMEM, SMEM, VMEM, VMEM, VMEM],
    )
    all_rows = lax.all_gather(bare_one, "row")
    gathered_one = gather_cols(packed_one, grid_size)
    parent_rows = call(
        place_kernel,
        "parent_rows",
        shape_of((width, share)),
        (place, *gather_rows(factor_parent, grid_size)),
        1,
        in_specs=[SMEM] + [VMEM] * grid_size,
    )
    gathered_parent = gather_cols(parent_rows, grid_size)
    packed_two = call(
        functools.partial(pack_two_kernel, cap_two),
        "pack_two",
        shape_of((cap_two * B, share)),
        (row_order, info, factor_root.reshape(blocks, B, share)),
        1,
        in_specs=[SMEM] * 2 + [VMEM],
    )
    gathered_two = gather_cols(packed_two, grid_size, gathered_one)

    solved_one, lag, lead_inverse, inverse_two, lead, diag_one, diag_two, parent = call(
        functools.partial(solve_one_kernel, cap_one, grid_size),
        "solve_one",
        (
            shape_of((2 * width, cap_one * B), jnp.bfloat16),
            shape_of((width, cap_one * B)),
            shape_of((2 * width, width), jnp.bfloat16),
            shape_of((2 * width, width), jnp.bfloat16),
            shape_of((share, width)),
            shape_of((share, share)),
            shape_of((share, share)),
            shape_of((width, share)),
        ),
        (place, *gathered_one, *gathered_parent),
        12 * width * width * cap_one * B,
        in_specs=[SMEM] + [VMEM] * (2 * grid_size),
        scratch=[pltpu.VMEM((width, width), jnp.bfloat16)] * 2,
    )
    solved_two, solved_root = call(
        functools.partial(solve_two_kernel, cap_one, cap_two),
        "solve_two",
        (
            shape_of((2 * width, cap_one * B), jnp.bfloat16),
            shape_of((2 * width, cap_two * B), jnp.bfloat16),
        ),
        (inverse_two, lag, *gathered_two),
        6 * width * width * cap_two * B,
    )
    far_pieces = [
        lax.dynamic_index_in_dim(all_rows, col ^ j, 0, keepdims=False) for j in range(grid_size)
    ]
    solved_two, far_pieces = lax.optimization_barrier((solved_two, far_pieces))
    counts = jnp.stack([info[0], info[3]])
    image_two = image(covariance, solved_two, row_order, col_order, counts, cap_two, "image_two")
    image_two = lax.psum_scatter(image_two, "row", scatter_dimension=0, tiled=True)

    counts = jnp.stack([info[2], info[0]])
    half = pl.cdiv(pl.cdiv(cap_one, 2), GROUP) * GROUP
    rows_one, previous = None, None
    for lead_in in range(0, cap_one, half):
        size = min(half, cap_one - lead_in)
        pieces = [piece[lead_in * B:(lead_in + size) * B] for piece in far_pieces]
        if previous is not None:
            pieces, previous[2] = lax.optimization_barrier((pieces, previous[2]))
        previous = [flip(piece, "col", j, grid_size) if j else piece for j, piece in enumerate(pieces)]
        solved_far = call(
            functools.partial(solve_far_kernel, size),
            f"solve_far_{lead_in}",
            shape_of((2 * width, pl.cdiv(size, GROUP) * GROUP * B), jnp.bfloat16),
            (lead_inverse, *previous),
            6 * width * width * size * B,
        )
        rows_one = mirror_image(
            covariance, solved_far, col_order, row_order, counts, cap_one, lead_in, rows_one,
            f"image_one_{lead_in}",
        )
    rows_one, image_two = plane_sum(rows_one, grid_size, col, image_two)
    rows_two = swap_grid(image_two, grid_size)
    rows_one, rows_two = lax.optimization_barrier((rows_one, rows_two))
    gram_one = call(
        gram_one_kernel,
        "gram_one",
        shape_of((grid_size, 2 * share, share)),
        (rows_one, solved_one, solved_two),
        12 * share * width * cap_one * B,
    )
    gram_one = scatter_pieces(gram_one, grid_size, row)
    gram_one, rows_one = lax.optimization_barrier((gram_one, rows_one))
    gram_one = scatter_sum(gram_one, grid_size)
    image_one = swap_grid(rows_one, grid_size)
    block_one = gram_one[:share] + diag_one
    mixed = swap_grid(gram_one[share:], grid_size)
    own_lead = lax.dynamic_slice_in_dim(lead, col * share, share, 1)
    parent_out = -lead
    for j, piece in enumerate(gather_cols(mixed, grid_size)):
        start = (col ^ j) * share
        here = lax.dynamic_slice_in_dim(parent_out, start, share, 1)
        parent_out = lax.dynamic_update_slice_in_dim(parent_out, here + piece, start, 1)

    cross_two = unpack(image_two, col_order, col_info, 1, blocks, "cross_two")
    gram_two = call(
        gram_two_kernel,
        "gram_two",
        shape_of((grid_size, share, share)),
        (rows_two, solved_root, own_lead - mixed, parent),
        6 * share * width * cap_two * B,
    )
    gram_two = scatter_pieces(gram_two, grid_size, row)
    block_two = scatter_sum(gram_two, grid_size) + diag_two
    cross_one = unpack(image_one, col_order, col_info, 0, blocks, "cross_one")
    return cross_one, block_one, parent_out, cross_two, block_two


def capacities_of(blocks):
    parts = ((0.7, 0.55), (0.75, 0.6), (0.8, 0.65), (0.9, 0.7)) if blocks >= 16 else ()
    return [(round(one * blocks), round(two * blocks)) for one, two in parts] + [(blocks, blocks)]


def local(
    root_covariance, factor_one, inverse_one, pattern_one, factor_parent, factor_root, inverse_two,
    pattern_two,
):
    blocks = root_covariance.shape[3]
    capacities = capacities_of(blocks)
    place = jnp.stack([lax.axis_index("row"), lax.axis_index("col")]).astype(jnp.int32)
    row_order, col_order, info = pl.pallas_call(
        functools.partial(plan_kernel, capacities),
        name="plan",
        out_shape=(
            shape_of((blocks,), jnp.int32), shape_of((blocks,), jnp.int32), shape_of((5,), jnp.int32)
        ),
        in_specs=[SMEM] * 3,
        out_specs=(SMEM,) * 3,
    )(place, pattern_one, pattern_two)
    operands = (
        row_order, col_order, info, place, root_covariance, factor_one, inverse_one,
        factor_parent, factor_root, inverse_two,
    )
    branches = [functools.partial(run, one, two) for one, two in capacities]
    if len(branches) == 1:
        results = branches[0](*operands)
    else:
        results = lax.switch(info[4], branches, *operands)
    cross_one, block_one, parent_out, cross_two, block_two = results
    cross_one = cross_one.reshape(-1, blocks, 1, B)
    cross_two = cross_two.reshape(-1, blocks, 1, B)
    return cross_one, block_one, parent_out, cross_two, block_two


def solution(mesh):
    return jax.shard_map(
        local,
        mesh=mesh,
        in_specs=(
            P("grp", "col", None, None, "row", None),
            P("grp", "row", None, "col"),
            P(("grp", "col"), None),
            P("grp"),
            P(("grp", "row"), "col"),
            P("grp", "row", None, "col"),
            P(("grp", "col"), None),
            P("grp"),
        ),
        out_specs=(
            P(("grp", "row"), None, "col", None),
            P(("grp", "col"), "row"),
            P(("grp", "row"), None),
            P(("grp", "row"), None, "col", None),
            P(("grp", "col"), "row"),
        ),
        check_vma=False,
    )
```

```python
import functools

import jax
import jax.numpy as jnp
from jax import lax
from jax.experimental import pallas as pl
from jax.experimental.pallas import tpu as pltpu
from jax.sharding import PartitionSpec as P

B = 128
VMEM_LIMIT = 52 * 1024 * 1024
GROUP = 4
VMEM = pl.BlockSpec(memory_space=pltpu.VMEM)
SMEM = pl.BlockSpec(memory_space=pltpu.SMEM)


def split(values):
    high = values.astype(jnp.bfloat16)
    low = (values - high.astype(jnp.float32)).astype(jnp.bfloat16)
    return high, low


def lanes_dot(left, right):
    return lax.dot_general(
        left, right, (((1,), (1,)), ((), ())), preferred_element_type=jnp.float32
    )


def plain_dot(left, right):
    return lax.dot_general(
        left, right, (((1,), (0,)), ((), ())), preferred_element_type=jnp.float32
    )


def three_products(dot, left, right):
    left_high, left_low = left
    right_high, right_low = right
    rows = left_high.shape[0]
    both = dot(jnp.concatenate([left_high, left_low], 0), right_high)
    return both[:rows] + both[rows:] + dot(left_high, right_low)


def stacked(high, low):
    return jnp.concatenate([high, low], 0)


def call(kernel, name, out_shape, operands, flops, in_specs=None, scratch=()):
    size = sum(a.size * a.dtype.itemsize for a in operands)
    size += sum(a.size * a.dtype.itemsize for a in jax.tree.leaves(out_shape))
    return pl.pallas_call(
        kernel,
        name=name,
        out_shape=out_shape,
        in_specs=in_specs or [VMEM] * len(operands),
        out_specs=jax.tree.map(lambda _: VMEM, out_shape),
        scratch_shapes=scratch,
        compiler_params=pltpu.CompilerParams(vmem_limit_bytes=VMEM_LIMIT),
        cost_estimate=pl.CostEstimate(flops=flops, bytes_accessed=size, transcendentals=0),
    )(*operands)


def shape_of(shape, dtype=jnp.float32):
    return jax.ShapeDtypeStruct(shape, dtype)


def plan_kernel(capacities, place, pattern_one, pattern_two, row_order, col_order, info):
    blocks = row_order.shape[0]
    grid_size = pattern_one.shape[0] // blocks
    largest_one, largest_two = jnp.int32(0), jnp.int32(0)
    counts_one, counts_two = [], []
    for p in range(grid_size):

        def count(b, carry):
            return (
                carry[0] + pattern_one[b * grid_size + p],
                carry[1] + pattern_two[b * grid_size + p],
            )

        one, two = lax.fori_loop(0, blocks, count, (jnp.int32(0), jnp.int32(0)))
        counts_one.append(one)
        counts_two.append(two)
        largest_one = jnp.maximum(largest_one, one)
        largest_two = jnp.maximum(largest_two, two)
    choice = jnp.int32(len(capacities) - 1)
    for i in reversed(range(len(capacities) - 1)):
        fits = (largest_one <= capacities[i][0]) & (largest_two <= capacities[i][1])
        choice = jnp.where(fits, i, choice)
    info[4] = choice
    for axis, order in enumerate((row_order, col_order)):
        position = place[axis]
        own_one, own_two = jnp.int32(0), jnp.int32(0)
        for p in range(grid_size):
            own_one = jnp.where(position == p, counts_one[p], own_one)
            own_two = jnp.where(position == p, counts_two[p], own_two)
        info[2 * axis] = own_one
        info[2 * axis + 1] = own_two

        def put(b, carry):
            one = pattern_one[b * grid_size + position]
            two = pattern_two[b * grid_size + position]
            slot = jnp.where(two > 0, carry[0], jnp.where(one > 0, carry[1], carry[2]))
            order[slot] = b
            return (carry[0] + two, carry[1] + one - two, carry[2] + 1 - one)

        lax.fori_loop(0, blocks, put, (jnp.int32(0), own_two, own_one))


def pack_one_kernel(cap, order, info, factor, inverse_one, inverse_two, out, *out_parts):
    width = inverse_one.shape[1]
    part_cap = out_parts[0].shape[0] // B
    for i in range(cap):
        block = jnp.where(i < info[0], factor[order[i]], 0.0)
        out[pl.ds(i * B, B), :] = block
        out_parts[i // part_cap][pl.ds(i % part_cap * B, B), :] = block
    out[pl.ds(cap * B, width), :] = inverse_one[...].T
    out[pl.ds(cap * B + width, width), :] = inverse_two[...].T


def pack_two_kernel(cap, order, info, factor, out):
    for i in range(cap):
        out[pl.ds(i * B, B), :] = jnp.where(i < info[1], factor[order[i]], 0.0)


def place_kernel(place, *refs):
    pieces, out = refs[:-1], refs[-1]
    share = pieces[0].shape[0]
    grid_size = len(pieces)
    for shift, piece in enumerate(pieces):
        source = lax.rem(place[0] + grid_size - shift, grid_size)
        out[pl.ds(pl.multiple_of(source * share, share), share), :] = piece[...]


def joined(refs, start, size):
    return jnp.concatenate([ref[pl.ds(start, size), :] for ref in refs], 1)


def over_rows(first, last, step, body):
    whole = (last - first) // step

    def turn(i, carry):
        body(pl.multiple_of(first * B + i * (step * B), B), step * B)
        return carry

    lax.fori_loop(0, whole, turn, 0)
    rest = last - first - whole * step
    if rest:
        body((first + whole * step) * B, rest * B)


def solve_rows(inverse, refs, out, cap):
    width = out.shape[0] // 2

    def body(start, size):
        rows = split(joined(refs, start, size))
        high, low = split(three_products(lanes_dot, inverse, rows))
        out[:width, pl.ds(start, size)] = high
        out[width:, pl.ds(start, size)] = low

    over_rows(0, cap, GROUP, body)


def solve_one_kernel(cap, grid_size, place, *refs):
    gathered, parents = refs[:grid_size], refs[grid_size:2 * grid_size]
    (
        out, out_lag, out_inverse_one, out_inverse_two, out_lead, out_diag_one, out_diag_two,
        out_parent, weight_high, weight_low,
    ) = refs[2 * grid_size:]
    share, width = out_lead.shape
    row, col = place[0], place[1]
    first, second = cap * B, cap * B + width
    inverse = split(joined(gathered, first, width))
    out_inverse_one[...] = stacked(*inverse)
    inverse_two = split(joined(gathered, second, width))
    out_inverse_two[...] = stacked(*inverse_two)
    solved_parent = split(
        three_products(lanes_dot, inverse_two, split(joined(parents, 0, width)))
    )
    row_start = pl.multiple_of(row * share, share)
    col_start = pl.multiple_of(col * share, share)
    out_parent[...] = three_products(
        lanes_dot, inverse_two, split(joined(parents, row_start, share))
    )
    for k in range(grid_size):
        piece = split(gathered[k][pl.ds(first, width), :])
        high, low = split(three_products(plain_dot, solved_parent, piece))
        weight_high[:, k * share:(k + 1) * share] = high
        weight_low[:, k * share:(k + 1) * share] = low
    weight = (weight_high[...], weight_low[...])
    for start, diag in ((first, out_diag_one), (second, out_diag_two)):
        inv_row = split(joined(gathered, start + row_start, share))
        inv_col = split(joined(gathered, start + col_start, share))
        diag[...] = three_products(lanes_dot, inv_col, inv_row)
        if start == first:
            out_lead[...] = three_products(lanes_dot, inv_row, weight)

    def body(start, size):
        rows = split(joined(gathered, start, size))
        high, low = split(three_products(lanes_dot, inverse, rows))
        out[:width, pl.ds(start, size)] = high
        out[width:, pl.ds(start, size)] = low
        out_lag[:, pl.ds(start, size)] = three_products(lanes_dot, weight, rows)

    over_rows(0, cap, GROUP, body)


def solve_far_kernel(cap, inverse, *refs):
    gathered, out = refs[:-1], refs[-1]
    width = out.shape[0] // 2
    if out.shape[1] > cap * B:
        out[:, cap * B:] = jnp.zeros((2 * width, out.shape[1] - cap * B), out.dtype)
    solve_rows((inverse[:width, :], inverse[width:, :]), gathered, out, cap)


def solve_two_kernel(cap_one, cap_two, inverse, lag, *refs):
    gathered, (out_full, out_root) = refs[:-2], refs[-2:]
    width = lag.shape[0]
    halves = (inverse[:width, :], inverse[width:, :])

    def both(start, size):
        own = three_products(lanes_dot, halves, split(joined(gathered, start, size)))
        high, low = split(own)
        out_root[:width, pl.ds(start, size)] = high
        out_root[width:, pl.ds(start, size)] = low
        high, low = split(own - lag[:, pl.ds(start, size)])
        out_full[:width, pl.ds(start, size)] = high
        out_full[width:, pl.ds(start, size)] = low

    over_rows(0, cap_two, GROUP, both)
    if cap_one > cap_two:
        high, low = split(-lag[:, cap_two * B:])
        out_full[:width, cap_two * B:] = high
        out_full[width:, cap_two * B:] = low


def image_kernel(
    blocks, cap, chunk, group, order_in, order_out, counts, solved, *refs
):
    covs, (out, high, low, total) = refs[:group], refs[group:]
    step = pl.program_id(0)
    width = out.shape[0]
    total[...] = jnp.zeros_like(total)

    @pl.when(group * step < counts[1])
    def _():
        for lead in range(0, cap, chunk):
            size = min(chunk, cap - lead)

            @pl.when(lead < counts[0])
            def _():
                for j in range(size):
                    for part, cov in enumerate(covs):
                        piece = cov[pl.ds(order_in[lead + j], B, stride=blocks), :]
                        piece_high, piece_low = split(piece)
                        high[part * B:(part + 1) * B, j * B:(j + 1) * B] = piece_high
                        low[part * B:(part + 1) * B, j * B:(j + 1) * B] = piece_low
                span = slice(lead * B, (lead + size) * B)
                both = lanes_dot(solved[:, span], high[:, :size * B])
                more = lanes_dot(solved[:width, span], low[:, :size * B])
                total[...] += both[:width] + both[width:] + more

    out[...] = total[...]


def image(covariance, solved, order_in, order_out, counts, cap_out, name):
    width = solved.shape[0] // 2
    cap_in = solved.shape[1] // B
    rows, blocks = covariance.shape[0], covariance.shape[1]
    flat = covariance.reshape(rows * blocks, B)
    chunk = GROUP
    group = GROUP

    def place(which):
        def index_map(i, order_in, order_out, counts):
            last = jnp.maximum(counts[1] - 1, 0)
            return (order_out[jnp.minimum(group * i + which, last)], 0)

        return pl.BlockSpec((B * blocks, B), index_map)

    grid_spec = pltpu.PrefetchScalarGridSpec(
        num_scalar_prefetch=3,
        grid=(pl.cdiv(cap_out, group),),
        in_specs=[
            pl.BlockSpec(solved.shape, lambda i, *_: (0, 0), pipeline_mode=pl.Buffered(1)),
            *[place(which) for which in range(group)],
        ],
        out_specs=pl.BlockSpec((width, group * B), lambda i, *_: (0, i)),
        scratch_shapes=[
            pltpu.VMEM((group * B, chunk * B), jnp.bfloat16),
            pltpu.VMEM((group * B, chunk * B), jnp.bfloat16),
            pltpu.VMEM((width, group * B), jnp.float32),
        ],
    )
    return pl.pallas_call(
        functools.partial(image_kernel, blocks, cap_in, chunk, group),
        name=name,
        grid_spec=grid_spec,
        out_shape=shape_of((width, cap_out * B)),
        compiler_params=pltpu.CompilerParams(vmem_limit_bytes=VMEM_LIMIT),
        cost_estimate=pl.CostEstimate(
            flops=6 * width * cap_in * B * cap_out * B,
            bytes_accessed=4 * cap_out * B * blocks * B + 8 * width * cap_out * B,
            transcendentals=0,
        ),
    )(order_in, order_out, counts, solved, *[flat] * group)


def mirror_kernel(blocks, cap, group, lead_in, order_in, order_out, counts, solved, *refs):
    covs, (out, high, low) = refs[:group], refs[-3:]
    step = pl.program_id(0)
    width = out.shape[0]

    @pl.when(step == 0)
    def _():
        out[...] = refs[group][...] if len(refs) > group + 3 else jnp.zeros_like(out)

    @pl.when(lead_in + group * step < counts[0])
    def _():
        for lead in range(0, cap, group):
            size = min(group, cap - lead)

            @pl.when(lead < counts[1])
            def _():
                for j in range(size):
                    for part, cov in enumerate(covs):
                        piece = cov[pl.ds(order_out[lead + j], B, stride=blocks), :]
                        piece_high, piece_low = split(piece)
                        high[part * B:(part + 1) * B, j * B:(j + 1) * B] = piece_high
                        low[part * B:(part + 1) * B, j * B:(j + 1) * B] = piece_low
                both = plain_dot(solved[...], high[:, :size * B])
                more = plain_dot(solved[:width, :], low[:, :size * B])
                out[:, lead * B:(lead + size) * B] += both[:width] + both[width:] + more


def mirror_image(covariance, solved, order_in, order_out, counts, cap, lead_in, before, name):
    width = solved.shape[0] // 2
    rows, blocks = covariance.shape[0], covariance.shape[1]
    flat = covariance.reshape(rows * blocks, B)
    group = GROUP
    steps = solved.shape[1] // (group * B)

    def place(which):
        def index_map(i, order_in, order_out, counts):
            last = jnp.maximum(counts[0] - 1, 0)
            return (order_in[jnp.minimum(lead_in + group * i + which, last)], 0)

        return pl.BlockSpec((B * blocks, B), index_map)

    whole = pl.BlockSpec((width, cap * B), lambda i, *_: (0, 0), pipeline_mode=pl.Buffered(1))
    extra = () if before is None else (before,)
    grid_spec = pltpu.PrefetchScalarGridSpec(
        num_scalar_prefetch=3,
        grid=(steps,),
        in_specs=[
            pl.BlockSpec((2 * width, group * B), lambda i, *_: (0, i)),
            *[place(which) for which in range(group)],
            *[whole for _ in extra],
        ],
        out_specs=pl.BlockSpec((width, cap * B), lambda i, *_: (0, 0)),
        scratch_shapes=[pltpu.VMEM((group * B, group * B), jnp.bfloat16)] * 2,
    )
    return pl.pallas_call(
        functools.partial(mirror_kernel, blocks, cap, group, lead_in),
        name=name,
        grid_spec=grid_spec,
        out_shape=shape_of((width, cap * B)),
        compiler_params=pltpu.CompilerParams(vmem_limit_bytes=VMEM_LIMIT),
        cost_estimate=pl.CostEstimate(
            flops=6 * width * cap * B * solved.shape[1],
            bytes_accessed=4 * steps * group * B * blocks * B + 8 * width * cap * B,
            transcendentals=0,
        ),
    )(order_in, order_out, counts, solved, *[flat] * group, *extra)


def unpack_kernel(blocks, which, order, counts, *refs):
    parts, out = refs[:-1], refs[-1]
    share = parts[0].shape[0]
    out[...] = jnp.zeros_like(out)
    slot = 0
    for packed in parts:
        for i in range(packed.shape[1] // B):
            if slot < blocks:

                @pl.when(slot < counts[which])
                def _():
                    out[pl.ds(order[slot], share, stride=blocks), :] = -packed[:, i * B:(i + 1) * B]

            slot += 1


def unpack(parts, order, counts, which, blocks, name):
    return call(
        functools.partial(unpack_kernel, blocks, which),
        name,
        shape_of((parts[0].shape[0] * blocks, B)),
        (order, counts, *parts),
        1,
        in_specs=[SMEM, SMEM] + [VMEM] * len(parts),
    )


def parent_out_kernel(place, lead, *refs):
    pieces, out = refs[:-1], refs[-1]
    share = pieces[0].shape[0]
    for k in range(len(pieces)):
        for j, piece in enumerate(pieces):

            @pl.when(place[1] ^ j == k)
            def _():
                span = slice(k * share, (k + 1) * share)
                out[:, span] = piece[...] - lead[:, span]


def gram_one_kernel(image_rows, solved_one, solved_two, out):
    grid_size, _, share = out.shape
    width = solved_one.shape[0] // 2
    rows = split(image_rows[...])
    for half, solved in enumerate((solved_one, solved_two)):
        product = three_products(lanes_dot, rows, (solved[:width, :], solved[width:, :]))
        for k in range(grid_size):
            out[k, half * share:(half + 1) * share, :] = product[:, k * share:(k + 1) * share]


def gram_two_kernel(image_rows, solved_root, image_parent, parent, out):
    grid_size, share, _ = out.shape
    width = solved_root.shape[0] // 2
    rows = split(image_rows[...])
    product = three_products(lanes_dot, rows, (solved_root[:width, :], solved_root[width:, :]))
    product = product + three_products(
        lanes_dot, split(image_parent[...].T), split(parent[...])
    )
    for k in range(grid_size):
        out[k, :, :] = product[:, k * share:(k + 1) * share]


def swap_grid(block, grid_size):
    pairs = [
        (r * grid_size + c, c * grid_size + r) for r in range(grid_size) for c in range(grid_size)
    ]
    return lax.ppermute(block, ("row", "col"), pairs)


def scatter_pieces(pieces, grid_size, position):
    return [
        lax.dynamic_index_in_dim(pieces, lax.rem(position + shift, grid_size), 0, keepdims=False)
        for shift in range(grid_size)
    ]


def scatter_sum(pieces, grid_size):
    total = pieces[0]
    for shift in range(1, grid_size):
        total = total + lax.ppermute(
            pieces[shift], "row", [(i, (i + shift) % grid_size) for i in range(grid_size)]
        )
    return total


def gather_rows(block, grid_size):
    return [block] + [
        lax.ppermute(block, "row", [(i, (i + shift) % grid_size) for i in range(grid_size)])
        for shift in range(1, grid_size)
    ]


def plane_sum(partial, grid_size, col, other):
    if grid_size != 4:
        return lax.psum_scatter(partial, "col", scatter_dimension=0, tiled=True), other
    share = partial.shape[0] // grid_size
    core, chip = col % 2, col // 2
    pieces = partial.reshape(2, 2, share, partial.shape[1])
    away = lax.dynamic_index_in_dim(pieces, 1 - core, 1, keepdims=False)
    stay = lax.dynamic_index_in_dim(pieces, core, 1, keepdims=False)
    pieces = stay + flip(away, "col", 1, grid_size)
    pieces, other = lax.optimization_barrier((pieces, other))
    away = lax.dynamic_index_in_dim(pieces, 1 - chip, 0, keepdims=False)
    stay = lax.dynamic_index_in_dim(pieces, chip, 0, keepdims=False)
    return stay + flip(away, "col", 2, grid_size), other


def flip(block, axis, bit, grid_size):
    return lax.ppermute(block, axis, [(i, i ^ bit) for i in range(grid_size)])


def gather_cols(block, grid_size, between=None):
    if grid_size != 4:
        gathered = lax.all_gather(block, "col")
        position = lax.axis_index("col")
        return [
            lax.dynamic_index_in_dim(gathered, position ^ j, 0, keepdims=False)
            for j in range(grid_size)
        ], between
    far = flip(block, "col", 2, grid_size)
    near = flip(block, "col", 1, grid_size)
    if between is not None:
        far, between = lax.optimization_barrier((far, between))
    return [block, near, far, flip(far, "col", 1, grid_size)], between


def exchange(gathered, grid_size, col):
    pieces = [
        lax.dynamic_index_in_dim(gathered, col ^ j, 0, keepdims=False) for j in range(grid_size)
    ]
    return [flip(piece, "col", j, grid_size) if j else piece for j, piece in enumerate(pieces)]


def run(
    cap_one, cap_two, row_order, col_order, info, place, root_covariance, factor_one, inverse_one,
    factor_parent, factor_root, inverse_two,
):
    grid_size = lax.axis_size("row")
    row = lax.axis_index("row")
    col = lax.axis_index("col")
    share, width = inverse_one.shape
    blocks = root_covariance.shape[3]
    covariance = root_covariance.reshape(-1, blocks, B)
    col_info = info[2:4]

    half = pl.cdiv(pl.cdiv(cap_one, 2), GROUP) * GROUP
    parts = [(lead_in, min(half, cap_one - lead_in)) for lead_in in range(0, cap_one, half)]
    packed_one, *bare_parts = call(
        functools.partial(pack_one_kernel, cap_one),
        "pack_one",
        (
            shape_of((cap_one * B + 2 * width, share)),
            *[shape_of((size * B, share)) for _, size in parts],
        ),
        (row_order, info, factor_one.reshape(blocks, B, share), inverse_one, inverse_two),
        1,
        in_specs=[SMEM, SMEM, VMEM, VMEM, VMEM],
    )
    all_rows = [lax.all_gather(part, "row") for part in bare_parts]
    parent_rows = call(
        place_kernel,
        "parent_rows",
        shape_of((width, share)),
        (place, *gather_rows(factor_parent, grid_size)),
        1,
        in_specs=[SMEM] + [VMEM] * grid_size,
    )
    packed_two = call(
        functools.partial(pack_two_kernel, cap_two),
        "pack_two",
        shape_of((cap_two * B, share)),
        (row_order, info, factor_root.reshape(blocks, B, share)),
        1,
        in_specs=[SMEM] * 2 + [VMEM],
    )
    gathered_one, (parent_rows, packed_two) = gather_cols(
        packed_one, grid_size, (parent_rows, packed_two)
    )
    gathered_parent, _ = gather_cols(parent_rows, grid_size)
    gathered_two, _ = gather_cols(packed_two, grid_size)

    solved_one, lag, lead_inverse, inverse_two, lead, diag_one, diag_two, parent = call(
        functools.partial(solve_one_kernel, cap_one, grid_size),
        "solve_one",
        (
            shape_of((2 * width, cap_one * B), jnp.bfloat16),
            shape_of((width, cap_one * B)),
            shape_of((2 * width, width), jnp.bfloat16),
            shape_of((2 * width, width), jnp.bfloat16),
            shape_of((share, width)),
            shape_of((share, share)),
            shape_of((share, share)),
            shape_of((width, share)),
        ),
        (place, *gathered_one, *gathered_parent),
        12 * width * width * cap_one * B,
        in_specs=[SMEM] + [VMEM] * (2 * grid_size),
        scratch=[pltpu.VMEM((width, width), jnp.bfloat16)] * 2,
    )
    solved_two, solved_root = call(
        functools.partial(solve_two_kernel, cap_one, cap_two),
        "solve_two",
        (
            shape_of((2 * width, cap_one * B), jnp.bfloat16),
            shape_of((2 * width, cap_two * B), jnp.bfloat16),
        ),
        (inverse_two, lag, *gathered_two),
        6 * width * width * cap_two * B,
    )
    far_rows = exchange(all_rows[0], grid_size, col)
    solved_two, far_rows = lax.optimization_barrier((solved_two, far_rows))
    counts = jnp.stack([info[0], info[3]])
    image_two = image(covariance, solved_two, row_order, col_order, counts, cap_two, "image_two")
    all_rows[-1], image_two = lax.optimization_barrier((all_rows[-1], image_two))
    image_two = lax.psum_scatter(image_two, "row", scatter_dimension=0, tiled=True)

    counts = jnp.stack([info[2], info[0]])
    rows_one = None
    for lead_in, size in parts:
        if lead_in:
            far_rows = exchange(all_rows[1], grid_size, col)
        solved_far = call(
            functools.partial(solve_far_kernel, size),
            f"solve_far_{lead_in}",
            shape_of((2 * width, pl.cdiv(size, GROUP) * GROUP * B), jnp.bfloat16),
            (lead_inverse, *far_rows),
            6 * width * width * size * B,
        )
        rows_one = mirror_image(
            covariance, solved_far, col_order, row_order, counts, cap_one, lead_in, rows_one,
            f"image_one_{lead_in}",
        )
    rows_one, image_two = plane_sum(rows_one, grid_size, col, image_two)
    rows_two = swap_grid(image_two, grid_size)
    rows_one, rows_two = lax.optimization_barrier((rows_one, rows_two))
    gram_one = call(
        gram_one_kernel,
        "gram_one",
        shape_of((grid_size, 2 * share, share)),
        (rows_one, solved_one, solved_two),
        12 * share * width * cap_one * B,
    )
    gram_one = scatter_pieces(gram_one, grid_size, row)
    gram_one, rows_one = lax.optimization_barrier((gram_one, rows_one))
    early = half * B
    image_one = [swap_grid(rows_one[:, :early], grid_size)]
    gram_one = scatter_sum(gram_one, grid_size)
    gram_one, image_one[0], rows_one = lax.optimization_barrier((gram_one, image_one[0], rows_one))
    if early < cap_one * B:
        image_one.append(swap_grid(rows_one[:, early:], grid_size))
    block_one = gram_one[:share] + diag_one
    mixed = swap_grid(gram_one[share:], grid_size)
    own_lead = lax.dynamic_slice_in_dim(lead, col * share, share, 1)
    parent_out = call(
        parent_out_kernel,
        "parent_out",
        shape_of((share, width)),
        (place, lead, *gather_cols(mixed, grid_size)[0]),
        1,
        in_specs=[SMEM] + [VMEM] * (1 + grid_size),
    )

    cross_two = unpack([image_two], col_order, col_info, 1, blocks, "cross_two")
    gram_two = call(
        gram_two_kernel,
        "gram_two",
        shape_of((grid_size, share, share)),
        (rows_two, solved_root, own_lead - mixed, parent),
        6 * share * width * cap_two * B,
    )
    gram_two = scatter_pieces(gram_two, grid_size, row)
    block_two = scatter_sum(gram_two, grid_size) + diag_two
    cross_one = unpack(image_one, col_order, col_info, 0, blocks, "cross_one")
    return cross_one, block_one, parent_out, cross_two, block_two


def capacities_of(blocks):
    parts = ((0.7, 0.55), (0.75, 0.6), (0.8, 0.65), (0.9, 0.7)) if blocks >= 16 else ()
    return [(round(one * blocks), round(two * blocks)) for one, two in parts] + [(blocks, blocks)]


def local(
    root_covariance, factor_one, inverse_one, pattern_one, factor_parent, factor_root, inverse_two,
    pattern_two,
):
    blocks = root_covariance.shape[3]
    capacities = capacities_of(blocks)
    place = jnp.stack([lax.axis_index("row"), lax.axis_index("col")]).astype(jnp.int32)
    row_order, col_order, info = pl.pallas_call(
        functools.partial(plan_kernel, capacities),
        name="plan",
        out_shape=(
            shape_of((blocks,), jnp.int32), shape_of((blocks,), jnp.int32), shape_of((5,), jnp.int32)
        ),
        in_specs=[SMEM] * 3,
        out_specs=(SMEM,) * 3,
    )(place, pattern_one, pattern_two)
    operands = (
        row_order, col_order, info, place, root_covariance, factor_one, inverse_one,
        factor_parent, factor_root, inverse_two,
    )
    branches = [functools.partial(run, one, two) for one, two in capacities]
    if len(branches) == 1:
        results = branches[0](*operands)
    else:
        results = lax.switch(info[4], branches, *operands)
    cross_one, block_one, parent_out, cross_two, block_two = results
    cross_one = cross_one.reshape(-1, blocks, 1, B)
    cross_two = cross_two.reshape(-1, blocks, 1, B)
    return cross_one, block_one, parent_out, cross_two, block_two


def solution(mesh):
    return jax.shard_map(
        local,
        mesh=mesh,
        in_specs=(
            P("grp", "col", None, None, "row", None),
            P("grp", "row", None, "col"),
            P(("grp", "col"), None),
            P("grp"),
            P(("grp", "row"), "col"),
            P("grp", "row", None, "col"),
            P(("grp", "col"), None),
            P("grp"),
        ),
        out_specs=(
            P(("grp", "row"), None, "col", None),
            P(("grp", "col"), "row"),
            P(("grp", "row"), None),
            P(("grp", "row"), None, "col", None),
            P(("grp", "col"), "row"),
        ),
        check_vma=False,
    )
```

```python
import functools

import jax
import jax.numpy as jnp
from jax import lax
from jax.experimental import pallas as pl
from jax.experimental.pallas import tpu as pltpu
from jax.sharding import PartitionSpec as P

B = 128
VMEM_LIMIT = 52 * 1024 * 1024
GROUP = 4
VMEM = pl.BlockSpec(memory_space=pltpu.VMEM)
SMEM = pl.BlockSpec(memory_space=pltpu.SMEM)


def split(values):
    high = values.astype(jnp.bfloat16)
    low = (values - high.astype(jnp.float32)).astype(jnp.bfloat16)
    return high, low


def lanes_dot(left, right):
    return lax.dot_general(
        left, right, (((1,), (1,)), ((), ())), preferred_element_type=jnp.float32
    )


def plain_dot(left, right):
    return lax.dot_general(
        left, right, (((1,), (0,)), ((), ())), preferred_element_type=jnp.float32
    )


def three_products(dot, left, right):
    left_high, left_low = left
    right_high, right_low = right
    rows = left_high.shape[0]
    both = dot(jnp.concatenate([left_high, left_low], 0), right_high)
    return both[:rows] + both[rows:] + dot(left_high, right_low)


def stacked(high, low):
    return jnp.concatenate([high, low], 0)


def call(kernel, name, out_shape, operands, flops, in_specs=None, scratch=()):
    size = sum(a.size * a.dtype.itemsize for a in operands)
    size += sum(a.size * a.dtype.itemsize for a in jax.tree.leaves(out_shape))
    return pl.pallas_call(
        kernel,
        name=name,
        out_shape=out_shape,
        in_specs=in_specs or [VMEM] * len(operands),
        out_specs=jax.tree.map(lambda _: VMEM, out_shape),
        scratch_shapes=scratch,
        compiler_params=pltpu.CompilerParams(vmem_limit_bytes=VMEM_LIMIT),
        cost_estimate=pl.CostEstimate(
            flops=flops, bytes_accessed=size, transcendentals=0
        ),
    )(*operands)


def shape_of(shape, dtype=jnp.float32):
    return jax.ShapeDtypeStruct(shape, dtype)


def plan_kernel(capacities, place, pattern_one, pattern_two, row_order, col_order, info):
    blocks = row_order.shape[0]
    grid_size = pattern_one.shape[0] // blocks
    largest_one, largest_two = jnp.int32(0), jnp.int32(0)
    counts_one, counts_two = [], []
    for p in range(grid_size):

        def count(b, carry):
            return (
                carry[0] + pattern_one[b * grid_size + p],
                carry[1] + pattern_two[b * grid_size + p],
            )

        one, two = lax.fori_loop(0, blocks, count, (jnp.int32(0), jnp.int32(0)))
        counts_one.append(one)
        counts_two.append(two)
        largest_one = jnp.maximum(largest_one, one)
        largest_two = jnp.maximum(largest_two, two)
    choice = jnp.int32(len(capacities) - 1)
    for i in reversed(range(len(capacities) - 1)):
        fits = (largest_one <= capacities[i][0]) & (largest_two <= capacities[i][1])
        choice = jnp.where(fits, i, choice)
    info[4] = choice
    info[5] = largest_one
    for axis, order in enumerate((row_order, col_order)):
        position = place[axis]
        own_one, own_two = jnp.int32(0), jnp.int32(0)
        for p in range(grid_size):
            own_one = jnp.where(position == p, counts_one[p], own_one)
            own_two = jnp.where(position == p, counts_two[p], own_two)
        info[2 * axis] = own_one
        info[2 * axis + 1] = own_two

        def put(b, carry):
            one = pattern_one[b * grid_size + position]
            two = pattern_two[b * grid_size + position]
            slot = jnp.where(two > 0, carry[0], jnp.where(one > 0, carry[1], carry[2]))
            order[slot] = b
            return (carry[0] + two, carry[1] + one - two, carry[2] + 1 - one)

        lax.fori_loop(0, blocks, put, (jnp.int32(0), own_two, own_one))


def pack_one_kernel(cap, order, info, factor, inverse_one, inverse_two, out, *out_parts):
    width = inverse_one.shape[1]
    part_cap = out_parts[0].shape[0] // B
    for i in range(cap):
        block = jnp.where(i < info[0], factor[order[i]], 0.0)
        out[pl.ds(i * B, B), :] = block
        out_parts[i // part_cap][pl.ds(i % part_cap * B, B), :] = block
    out[pl.ds(cap * B, width), :] = inverse_one[...].T
    out[pl.ds(cap * B + width, width), :] = inverse_two[...].T


def pack_two_kernel(cap, order, info, factor, out):
    for i in range(cap):
        out[pl.ds(i * B, B), :] = jnp.where(i < info[1], factor[order[i]], 0.0)


def place_kernel(place, *refs):
    pieces, out = refs[:-1], refs[-1]
    share = pieces[0].shape[0]
    grid_size = len(pieces)
    for shift, piece in enumerate(pieces):
        source = lax.rem(place[0] + grid_size - shift, grid_size)
        out[pl.ds(pl.multiple_of(source * share, share), share), :] = piece[...]


def joined(refs, start, size):
    return jnp.concatenate([ref[pl.ds(start, size), :] for ref in refs], 1)


def over_rows(first, last, step, body):
    whole = (last - first) // step

    def turn(i, carry):
        body(pl.multiple_of(first * B + i * (step * B), B), step * B)
        return carry

    lax.fori_loop(0, whole, turn, 0)
    rest = last - first - whole * step
    if rest:
        body((first + whole * step) * B, rest * B)


def solve_rows(inverse, refs, out, cap):
    width = out.shape[0] // 2

    def body(start, size):
        rows = split(joined(refs, start, size))
        high, low = split(three_products(lanes_dot, inverse, rows))
        out[:width, pl.ds(start, size)] = high
        out[width:, pl.ds(start, size)] = low

    over_rows(0, cap, GROUP, body)


def solve_one_kernel(cap, grid_size, place, *refs):
    gathered, parents = refs[:grid_size], refs[grid_size:2 * grid_size]
    (
        out, out_lag, out_inverse_one, out_inverse_two, out_lead, out_diag_one, out_diag_two,
        out_parent, weight_high, weight_low,
    ) = refs[2 * grid_size:]
    share, width = out_lead.shape
    row, col = place[0], place[1]
    first, second = cap * B, cap * B + width
    inverse = split(joined(gathered, first, width))
    out_inverse_one[...] = stacked(*inverse)
    inverse_two = split(joined(gathered, second, width))
    out_inverse_two[...] = stacked(*inverse_two)
    solved_parent = split(
        three_products(lanes_dot, inverse_two, split(joined(parents, 0, width)))
    )
    row_start = pl.multiple_of(row * share, share)
    col_start = pl.multiple_of(col * share, share)
    out_parent[...] = three_products(
        lanes_dot, inverse_two, split(joined(parents, row_start, share))
    )
    for k in range(grid_size):
        piece = split(gathered[k][pl.ds(first, width), :])
        high, low = split(three_products(plain_dot, solved_parent, piece))
        weight_high[:, k * share:(k + 1) * share] = high
        weight_low[:, k * share:(k + 1) * share] = low
    weight = (weight_high[...], weight_low[...])
    for start, diag in ((first, out_diag_one), (second, out_diag_two)):
        inv_row = split(joined(gathered, start + row_start, share))
        inv_col = split(joined(gathered, start + col_start, share))
        diag[...] = three_products(lanes_dot, inv_col, inv_row)
        if start == first:
            out_lead[...] = three_products(lanes_dot, inv_row, weight)

    def body(start, size):
        rows = split(joined(gathered, start, size))
        high, low = split(three_products(lanes_dot, inverse, rows))
        out[:width, pl.ds(start, size)] = high
        out[width:, pl.ds(start, size)] = low
        out_lag[:, pl.ds(start, size)] = three_products(lanes_dot, weight, rows)

    over_rows(0, cap, GROUP, body)


def solve_far_kernel(cap, inverse, *refs):
    gathered, out = refs[:-1], refs[-1]
    width = out.shape[0] // 2
    if out.shape[1] > cap * B:
        out[:, cap * B:] = jnp.zeros((2 * width, out.shape[1] - cap * B), out.dtype)
    solve_rows((inverse[:width, :], inverse[width:, :]), gathered, out, cap)


def solve_two_kernel(cap_one, cap_two, inverse, lag, *refs):
    gathered, (out_full, out_root) = refs[:-2], refs[-2:]
    width = lag.shape[0]
    halves = (inverse[:width, :], inverse[width:, :])

    def both(start, size):
        own = three_products(lanes_dot, halves, split(joined(gathered, start, size)))
        high, low = split(own)
        out_root[:width, pl.ds(start, size)] = high
        out_root[width:, pl.ds(start, size)] = low
        high, low = split(own - lag[:, pl.ds(start, size)])
        out_full[:width, pl.ds(start, size)] = high
        out_full[width:, pl.ds(start, size)] = low

    over_rows(0, cap_two, GROUP, both)
    if cap_one > cap_two:
        high, low = split(-lag[:, cap_two * B:])
        out_full[:width, cap_two * B:] = high
        out_full[width:, cap_two * B:] = low


def image_kernel(
    blocks, cap, chunk, group, order_in, order_out, counts, solved, *refs
):
    covs, (out, high, low, total) = refs[:group], refs[group:]
    step = pl.program_id(0)
    width = out.shape[0]
    total[...] = jnp.zeros_like(total)

    @pl.when(group * step < counts[1])
    def _():
        for lead in range(0, cap, chunk):
            size = min(chunk, cap - lead)

            @pl.when(lead < counts[0])
            def _():
                for j in range(size):
                    for part, cov in enumerate(covs):
                        piece = cov[pl.ds(order_in[lead + j], B, stride=blocks), :]
                        piece_high, piece_low = split(piece)
                        high[part * B:(part + 1) * B, j * B:(j + 1) * B] = piece_high
                        low[part * B:(part + 1) * B, j * B:(j + 1) * B] = piece_low
                span = slice(lead * B, (lead + size) * B)
                both = lanes_dot(solved[:, span], high[:, :size * B])
                more = lanes_dot(solved[:width, span], low[:, :size * B])
                total[...] += both[:width] + both[width:] + more

    out[...] = total[...]


def image(covariance, blocks, solved, order_in, order_out, counts, cap_out, name):
    width = solved.shape[0] // 2
    cap_in = solved.shape[1] // B
    chunk = GROUP
    group = GROUP

    def place(which):
        def index_map(i, order_in, order_out, counts):
            last = jnp.maximum(counts[1] - 1, 0)
            return (order_out[jnp.minimum(group * i + which, last)], 0)

        return pl.BlockSpec((B * blocks, B), index_map)

    grid_spec = pltpu.PrefetchScalarGridSpec(
        num_scalar_prefetch=3,
        grid=(pl.cdiv(cap_out, group),),
        in_specs=[
            pl.BlockSpec(solved.shape, lambda i, *_: (0, 0), pipeline_mode=pl.Buffered(1)),
            *[place(which) for which in range(group)],
        ],
        out_specs=pl.BlockSpec((width, group * B), lambda i, *_: (0, i)),
        scratch_shapes=[
            pltpu.VMEM((group * B, chunk * B), jnp.bfloat16),
            pltpu.VMEM((group * B, chunk * B), jnp.bfloat16),
            pltpu.VMEM((width, group * B), jnp.float32),
        ],
    )
    return pl.pallas_call(
        functools.partial(image_kernel, blocks, cap_in, chunk, group),
        name=name,
        grid_spec=grid_spec,
        out_shape=shape_of((width, cap_out * B)),
        compiler_params=pltpu.CompilerParams(vmem_limit_bytes=VMEM_LIMIT),
        cost_estimate=pl.CostEstimate(
            flops=6 * width * cap_in * B * cap_out * B,
            bytes_accessed=(4 * blocks * B + 8 * width) * cap_out * B,
            transcendentals=0,
        ),
    )(order_in, order_out, counts, solved, *[covariance] * group)


def mirror_kernel(blocks, cap, group, lead_in, order_in, order_out, counts, solved, *refs):
    covs, (out, high, low) = refs[:group], refs[-3:]
    step = pl.program_id(0)
    width = out.shape[0]

    @pl.when(step == 0)
    def _():
        out[...] = refs[group][...] if len(refs) > group + 3 else jnp.zeros_like(out)

    @pl.when(lead_in + group * step < counts[0])
    def _():
        for lead in range(0, cap, group):
            size = min(group, cap - lead)

            @pl.when(lead < counts[1])
            def _():
                for j in range(size):
                    for part, cov in enumerate(covs):
                        piece = cov[pl.ds(order_out[lead + j], B, stride=blocks), :]
                        piece_high, piece_low = split(piece)
                        high[part * B:(part + 1) * B, j * B:(j + 1) * B] = piece_high
                        low[part * B:(part + 1) * B, j * B:(j + 1) * B] = piece_low
                both = plain_dot(solved[...], high[:, :size * B])
                more = plain_dot(solved[:width, :], low[:, :size * B])
                out[:, lead * B:(lead + size) * B] += both[:width] + both[width:] + more


def mirror_image(covariance, blocks, solved, order_in, order_out, counts, cap, lead_in, before, name):
    width = solved.shape[0] // 2
    group = GROUP
    steps = solved.shape[1] // (group * B)

    def place(which):
        def index_map(i, order_in, order_out, counts):
            last = jnp.maximum(counts[0] - 1, 0)
            return (order_in[jnp.minimum(lead_in + group * i + which, last)], 0)

        return pl.BlockSpec((B * blocks, B), index_map)

    whole = pl.BlockSpec((width, cap * B), lambda i, *_: (0, 0), pipeline_mode=pl.Buffered(1))
    extra = () if before is None else (before,)
    grid_spec = pltpu.PrefetchScalarGridSpec(
        num_scalar_prefetch=3,
        grid=(steps,),
        in_specs=[
            pl.BlockSpec((2 * width, group * B), lambda i, *_: (0, i)),
            *[place(which) for which in range(group)],
            *[whole for _ in extra],
        ],
        out_specs=pl.BlockSpec((width, cap * B), lambda i, *_: (0, 0)),
        scratch_shapes=[pltpu.VMEM((group * B, group * B), jnp.bfloat16)] * 2,
    )
    return pl.pallas_call(
        functools.partial(mirror_kernel, blocks, cap, group, lead_in),
        name=name,
        grid_spec=grid_spec,
        out_shape=shape_of((width, cap * B)),
        compiler_params=pltpu.CompilerParams(vmem_limit_bytes=VMEM_LIMIT),
        cost_estimate=pl.CostEstimate(
            flops=6 * width * cap * B * solved.shape[1],
            bytes_accessed=4 * (steps * group * B * blocks + 2 * width * cap) * B,
            transcendentals=0,
        ),
    )(order_in, order_out, counts, solved, *[covariance] * group, *extra)


def unpack_kernel(blocks, which, order, counts, *refs):
    parts, out = refs[:-1], refs[-1]
    share = parts[0].shape[0]
    out[...] = jnp.zeros_like(out)
    for i in range(min(blocks, parts[0].shape[1] // B)):

        @pl.when(i < counts[which])
        def _():
            span = slice(i * B, (i + 1) * B)
            block = -parts[0][:, span]
            for part in parts[1:]:
                block = block - part[:, span]
            out[pl.ds(order[i], share, stride=blocks), :] = block


def unpack(parts, order, counts, which, blocks, name):
    return call(
        functools.partial(unpack_kernel, blocks, which),
        name,
        shape_of((parts[0].shape[0] * blocks, B)),
        (order, counts, *parts),
        1,
        in_specs=[SMEM, SMEM] + [VMEM] * len(parts),
    )


def parent_out_kernel(place, lead, *refs):
    pieces, out = refs[:-1], refs[-1]
    share = pieces[0].shape[0]
    for k in range(len(pieces)):
        for j, piece in enumerate(pieces):

            @pl.when(place[1] ^ j == k)
            def _():
                span = slice(k * share, (k + 1) * share)
                out[:, span] = piece[...] - lead[:, span]


def gram_one_kernel(image_rows, solved_one, solved_two, out):
    grid_size, _, share = out.shape
    width = solved_one.shape[0] // 2
    rows = split(image_rows[...])
    for half, solved in enumerate((solved_one, solved_two)):
        product = three_products(lanes_dot, rows, (solved[:width, :], solved[width:, :]))
        for k in range(grid_size):
            out[k, half * share:(half + 1) * share, :] = product[:, k * share:(k + 1) * share]


def gram_two_kernel(image_rows, solved_root, image_parent, parent, out):
    grid_size, share, _ = out.shape
    width = solved_root.shape[0] // 2
    rows = split(image_rows[...])
    product = three_products(lanes_dot, rows, (solved_root[:width, :], solved_root[width:, :]))
    product = product + three_products(
        lanes_dot, split(image_parent[...].T), split(parent[...])
    )
    for k in range(grid_size):
        out[k, :, :] = product[:, k * share:(k + 1) * share]


def swap_grid(block, grid_size):
    pairs = [
        (r * grid_size + c, c * grid_size + r) for r in range(grid_size) for c in range(grid_size)
    ]
    return lax.ppermute(block, ("row", "col"), pairs)


def scatter_pieces(pieces, grid_size, position):
    return [
        lax.dynamic_index_in_dim(pieces, lax.rem(position + shift, grid_size), 0, keepdims=False)
        for shift in range(grid_size)
    ]


def scatter_sum(pieces, grid_size):
    total = pieces[0]
    for shift in range(1, grid_size):
        total = total + lax.ppermute(
            pieces[shift], "row", [(i, (i + shift) % grid_size) for i in range(grid_size)]
        )
    return total


def gather_rows(block, grid_size):
    return [block] + [
        lax.ppermute(block, "row", [(i, (i + shift) % grid_size) for i in range(grid_size)])
        for shift in range(1, grid_size)
    ]


def plane_sum(partial, grid_size, col):
    if grid_size != 4:
        return lax.psum_scatter(partial, "col", scatter_dimension=0, tiled=True)
    share = partial.shape[0] // grid_size
    core, chip = col % 2, col // 2
    pieces = partial.reshape(2, 2, share, partial.shape[1])
    away = lax.dynamic_index_in_dim(pieces, 1 - core, 1, keepdims=False)
    stay = lax.dynamic_index_in_dim(pieces, core, 1, keepdims=False)
    pieces = stay + flip(away, "col", 1, grid_size)
    away = lax.dynamic_index_in_dim(pieces, 1 - chip, 0, keepdims=False)
    stay = lax.dynamic_index_in_dim(pieces, chip, 0, keepdims=False)
    return stay + flip(away, "col", 2, grid_size)


def swap_start(block, grid_size):
    if grid_size != 4:
        return block
    pairs = []
    for r in range(4):
        for c in range(4):
            if r // 2 != c // 2:
                pairs.append((4 * r + c, 4 * r + 2 * (r // 2) + c % 2))
    return lax.ppermute(block, ("row", "col"), pairs)


def swap_finish(block, moved, grid_size):
    if grid_size != 4:
        return [swap_grid(moved, grid_size)]
    direct, onward = [], []
    for r in range(4):
        for c in range(4):
            if r // 2 == c // 2:
                direct.append((4 * r + c, 4 * c + r))
            else:
                onward.append((4 * r + 2 * (r // 2) + c % 2, 4 * c + r))
    return [
        lax.ppermute(block, ("row", "col"), direct), lax.ppermute(moved, ("row", "col"), onward)
    ]


def flip(block, axis, bit, grid_size):
    return lax.ppermute(block, axis, [(i, i ^ bit) for i in range(grid_size)])


def gather_cols(block, grid_size, between=None):
    if grid_size != 4:
        gathered = lax.all_gather(block, "col")
        position = lax.axis_index("col")
        return [
            lax.dynamic_index_in_dim(gathered, position ^ j, 0, keepdims=False)
            for j in range(grid_size)
        ], between
    far = flip(block, "col", 2, grid_size)
    near = flip(block, "col", 1, grid_size)
    if between is not None:
        far, between = lax.optimization_barrier((far, between))
    return [block, near, far, flip(far, "col", 1, grid_size)], between


def exchange(gathered, grid_size, col):
    pieces = [
        lax.dynamic_index_in_dim(gathered, col ^ j, 0, keepdims=False) for j in range(grid_size)
    ]
    return [flip(piece, "col", j, grid_size) if j else piece for j, piece in enumerate(pieces)]


def run(
    cap_one, cap_two, row_order, col_order, info, place, root_covariance, factor_one, inverse_one,
    factor_parent, factor_root, inverse_two,
):
    grid_size = lax.axis_size("row")
    row = lax.axis_index("row")
    col = lax.axis_index("col")
    share, width = inverse_one.shape
    blocks = root_covariance.shape[3]
    covariance = root_covariance.reshape(-1, B)
    col_info = info[2:4]

    half = pl.cdiv(pl.cdiv(cap_one, 2), GROUP) * GROUP
    parts = [(lead_in, min(half, cap_one - lead_in)) for lead_in in range(0, cap_one, half)]
    packed_one, *bare_parts = call(
        functools.partial(pack_one_kernel, cap_one),
        "pack_one",
        (
            shape_of((cap_one * B + 2 * width, share)),
            *[shape_of((size * B, share)) for _, size in parts],
        ),
        (row_order, info, factor_one.reshape(blocks, B, share), inverse_one, inverse_two),
        1,
        in_specs=[SMEM, SMEM, VMEM, VMEM, VMEM],
    )
    all_rows = [lax.all_gather(part, "row") for part in bare_parts]
    parent_rows = call(
        place_kernel,
        "parent_rows",
        shape_of((width, share)),
        (place, *gather_rows(factor_parent, grid_size)),
        1,
        in_specs=[SMEM] + [VMEM] * grid_size,
    )
    packed_two = call(
        functools.partial(pack_two_kernel, cap_two),
        "pack_two",
        shape_of((cap_two * B, share)),
        (row_order, info, factor_root.reshape(blocks, B, share)),
        1,
        in_specs=[SMEM] * 2 + [VMEM],
    )
    gathered_one, (parent_rows, packed_two) = gather_cols(
        packed_one, grid_size, (parent_rows, packed_two)
    )
    gathered_parent, packed_two = gather_cols(parent_rows, grid_size, packed_two)
    gathered_two, _ = gather_cols(packed_two, grid_size)

    solved_one, lag, lead_inverse, inverse_two, lead, diag_one, diag_two, parent = call(
        functools.partial(solve_one_kernel, cap_one, grid_size),
        "solve_one",
        (
            shape_of((2 * width, cap_one * B), jnp.bfloat16),
            shape_of((width, cap_one * B)),
            shape_of((2 * width, width), jnp.bfloat16),
            shape_of((2 * width, width), jnp.bfloat16),
            shape_of((share, width)),
            shape_of((share, share)),
            shape_of((share, share)),
            shape_of((width, share)),
        ),
        (place, *gathered_one, *gathered_parent),
        12 * width * width * cap_one * B,
        in_specs=[SMEM] + [VMEM] * (2 * grid_size),
        scratch=[pltpu.VMEM((width, width), jnp.bfloat16)] * 2,
    )
    solved_two, solved_root = call(
        functools.partial(solve_two_kernel, cap_one, cap_two),
        "solve_two",
        (
            shape_of((2 * width, cap_one * B), jnp.bfloat16),
            shape_of((2 * width, cap_two * B), jnp.bfloat16),
        ),
        (inverse_two, lag, *gathered_two),
        6 * width * width * cap_two * B,
    )
    far_rows = exchange(all_rows[0], grid_size, col)
    solved_two, far_rows = lax.optimization_barrier((solved_two, far_rows))
    counts = jnp.stack([info[0], info[3]])
    image_two = image(covariance, blocks, solved_two, row_order, col_order, counts, cap_two, "image_two")
    all_rows[-1], image_two = lax.optimization_barrier((all_rows[-1], image_two))
    image_two = lax.psum_scatter(image_two, "row", scatter_dimension=0, tiled=True)

    def level_one(far_rows, last_rows, solved_one, solved_two, lead_inverse):
        counts = jnp.stack([info[2], info[0]])
        rows_one = None
        for lead_in, size in parts:
            if lead_in:
                far_rows = exchange(last_rows, grid_size, col)
            solved_far = call(
                functools.partial(solve_far_kernel, size),
                f"solve_far_{lead_in}",
                shape_of((2 * width, pl.cdiv(size, GROUP) * GROUP * B), jnp.bfloat16),
                (lead_inverse, *far_rows),
                6 * width * width * size * B,
            )
            rows_one = mirror_image(
                covariance, blocks, solved_far, col_order, row_order, counts, cap_one, lead_in, rows_one,
                f"image_one_{lead_in}",
            )
        rows_one = plane_sum(rows_one, grid_size, col)
        gram_one = call(
            gram_one_kernel,
            "gram_one",
            shape_of((grid_size, 2 * share, share)),
            (rows_one, solved_one, solved_two),
            12 * share * width * cap_one * B,
        )
        gram_one = scatter_pieces(gram_one, grid_size, row)
        return gram_one, rows_one

    def empty(*operands):
        return (
            [jnp.zeros((2 * share, share), jnp.float32) for _ in range(grid_size)],
            jnp.zeros((share, cap_one * B), jnp.float32),
        )

    gram_one, rows_one = lax.cond(
        info[5] > 0, level_one, empty,
        far_rows, all_rows[-1], solved_one, solved_two, lead_inverse,
    )
    moved = swap_start(rows_one, grid_size)
    gram_one, image_two = lax.optimization_barrier((gram_one, image_two))
    rows_two = swap_grid(image_two, grid_size)
    gram_one = scatter_sum(gram_one, grid_size)
    gram_one, moved, rows_one = lax.optimization_barrier((gram_one, moved, rows_one))
    image_one = swap_finish(rows_one, moved, grid_size)
    block_one = gram_one[:share] + diag_one
    mixed = swap_grid(gram_one[share:], grid_size)
    own_lead = lax.dynamic_slice_in_dim(lead, col * share, share, 1)
    parent_out = call(
        parent_out_kernel,
        "parent_out",
        shape_of((share, width)),
        (place, lead, *gather_cols(mixed, grid_size)[0]),
        1,
        in_specs=[SMEM] + [VMEM] * (1 + grid_size),
    )

    cross_two = unpack([image_two], col_order, col_info, 1, blocks, "cross_two")
    gram_two = call(
        gram_two_kernel,
        "gram_two",
        shape_of((grid_size, share, share)),
        (rows_two, solved_root, own_lead - mixed, parent),
        6 * share * width * cap_two * B,
    )
    gram_two = scatter_pieces(gram_two, grid_size, row)
    block_two = scatter_sum(gram_two, grid_size) + diag_two
    cross_one = unpack(image_one, col_order, col_info, 0, blocks, "cross_one")
    return cross_one, block_one, parent_out, cross_two, block_two


def capacities_of(blocks):
    parts = ((0.7, 0.55), (0.75, 0.6), (0.8, 0.65), (0.9, 0.7)) if blocks >= 16 else ()
    return [(round(one * blocks), round(two * blocks)) for one, two in parts] + [(blocks, blocks)]


def local(
    root_covariance, factor_one, inverse_one, pattern_one, factor_parent, factor_root, inverse_two,
    pattern_two,
):
    blocks = root_covariance.shape[3]
    capacities = capacities_of(blocks)
    place = jnp.stack([lax.axis_index("row"), lax.axis_index("col")]).astype(jnp.int32)
    row_order, col_order, info = pl.pallas_call(
        functools.partial(plan_kernel, capacities),
        name="plan",
        out_shape=(
            shape_of((blocks,), jnp.int32), shape_of((blocks,), jnp.int32), shape_of((6,), jnp.int32)
        ),
        in_specs=[SMEM] * 3,
        out_specs=(SMEM,) * 3,
    )(place, pattern_one, pattern_two)
    operands = (
        row_order, col_order, info, place, root_covariance, factor_one, inverse_one,
        factor_parent, factor_root, inverse_two,
    )
    branches = [functools.partial(run, one, two) for one, two in capacities]
    if len(branches) == 1:
        results = branches[0](*operands)
    else:
        results = lax.switch(info[4], branches, *operands)
    cross_one, block_one, parent_out, cross_two, block_two = results
    cross_one = cross_one.reshape(-1, blocks, 1, B)
    cross_two = cross_two.reshape(-1, blocks, 1, B)
    return cross_one, block_one, parent_out, cross_two, block_two


def solution(mesh):
    return jax.shard_map(
        local,
        mesh=mesh,
        in_specs=(
            P("grp", "col", None, None, "row", None),
            P("grp", "row", None, "col"),
            P(("grp", "col"), None),
            P("grp"),
            P(("grp", "row"), "col"),
            P("grp", "row", None, "col"),
            P(("grp", "col"), None),
            P("grp"),
        ),
        out_specs=(
            P(("grp", "row"), None, "col", None),
            P(("grp", "col"), "row"),
            P(("grp", "row"), None),
            P(("grp", "row"), None, "col", None),
            P(("grp", "col"), "row"),
        ),
        check_vma=False,
    )
```

```python
import functools

import jax
import jax.numpy as jnp
from jax import lax
from jax.experimental import pallas as pl
from jax.experimental.pallas import tpu as pltpu
from jax.sharding import PartitionSpec as P

B = 128
VMEM_LIMIT = 52 * 1024 * 1024
GROUP = 4
VMEM = pl.BlockSpec(memory_space=pltpu.VMEM)
SMEM = pl.BlockSpec(memory_space=pltpu.SMEM)


def split(values):
    high = values.astype(jnp.bfloat16)
    low = (values - high.astype(jnp.float32)).astype(jnp.bfloat16)
    return high, low


def lanes_dot(left, right):
    return lax.dot_general(
        left, right, (((1,), (1,)), ((), ())), preferred_element_type=jnp.float32
    )


def plain_dot(left, right):
    return lax.dot_general(
        left, right, (((1,), (0,)), ((), ())), preferred_element_type=jnp.float32
    )


def three_products(dot, left, right):
    left_high, left_low = left
    right_high, right_low = right
    rows = left_high.shape[0]
    both = dot(jnp.concatenate([left_high, left_low], 0), right_high)
    return both[:rows] + both[rows:] + dot(left_high, right_low)


def stacked(high, low):
    return jnp.concatenate([high, low], 0)


def call(kernel, name, out_shape, operands, flops, in_specs=None, scratch=()):
    size = sum(a.size * a.dtype.itemsize for a in operands)
    size += sum(a.size * a.dtype.itemsize for a in jax.tree.leaves(out_shape))
    return pl.pallas_call(
        kernel,
        name=name,
        out_shape=out_shape,
        in_specs=in_specs or [VMEM] * len(operands),
        out_specs=jax.tree.map(lambda _: VMEM, out_shape),
        scratch_shapes=scratch,
        compiler_params=pltpu.CompilerParams(vmem_limit_bytes=VMEM_LIMIT),
        cost_estimate=pl.CostEstimate(
            flops=flops, bytes_accessed=size, transcendentals=0
        ),
    )(*operands)


def shape_of(shape, dtype=jnp.float32):
    return jax.ShapeDtypeStruct(shape, dtype)


def plan_kernel(capacities, place, pattern_one, pattern_two, row_order, col_order, info):
    blocks = row_order.shape[0]
    grid_size = pattern_one.shape[0] // blocks
    largest_one, largest_two = jnp.int32(0), jnp.int32(0)
    counts_one, counts_two = [], []
    for p in range(grid_size):

        def count(b, carry):
            return (
                carry[0] + pattern_one[b * grid_size + p],
                carry[1] + pattern_two[b * grid_size + p],
            )

        one, two = lax.fori_loop(0, blocks, count, (jnp.int32(0), jnp.int32(0)))
        counts_one.append(one)
        counts_two.append(two)
        largest_one = jnp.maximum(largest_one, one)
        largest_two = jnp.maximum(largest_two, two)
    choice = jnp.int32(0)
    for i in range(1, len(capacities)):
        fits = (largest_one <= capacities[i][0]) & (largest_two <= capacities[i][1])
        choice = jnp.where(fits, i, choice)
    info[4] = choice
    info[5] = largest_one
    for axis, order in enumerate((row_order, col_order)):
        position = place[axis]
        own_one, own_two = jnp.int32(0), jnp.int32(0)
        for p in range(grid_size):
            own_one = jnp.where(position == p, counts_one[p], own_one)
            own_two = jnp.where(position == p, counts_two[p], own_two)
        info[2 * axis] = own_one
        info[2 * axis + 1] = own_two

        def put(b, carry):
            one = pattern_one[b * grid_size + position]
            two = pattern_two[b * grid_size + position]
            slot = jnp.where(two > 0, carry[0], jnp.where(one > 0, carry[1], carry[2]))
            order[slot] = b
            return (carry[0] + two, carry[1] + one - two, carry[2] + 1 - one)

        lax.fori_loop(0, blocks, put, (jnp.int32(0), own_two, own_one))


def pack_one_kernel(cap, order, info, factor, inverse_one, inverse_two, out, *out_parts):
    width = inverse_one.shape[1]
    part_cap = out_parts[0].shape[0] // B
    for i in range(cap):
        block = jnp.where(i < info[0], factor[order[i]], 0.0)
        out[pl.ds(i * B, B), :] = block
        out_parts[i // part_cap][pl.ds(i % part_cap * B, B), :] = block
    out[pl.ds(cap * B, width), :] = inverse_one[...].T
    out[pl.ds(cap * B + width, width), :] = inverse_two[...].T


def pack_two_kernel(cap, order, info, factor, out):
    for i in range(cap):
        out[pl.ds(i * B, B), :] = jnp.where(i < info[1], factor[order[i]], 0.0)


def place_kernel(place, *refs):
    pieces, out = refs[:-1], refs[-1]
    share = pieces[0].shape[0]
    grid_size = len(pieces)
    for shift, piece in enumerate(pieces):
        source = lax.rem(place[0] + grid_size - shift, grid_size)
        out[pl.ds(pl.multiple_of(source * share, share), share), :] = piece[...]


def all_rows(cap, body):
    size = min(cap, GROUP)

    def turn(i, carry):
        body(pl.multiple_of(jnp.minimum(i * GROUP, cap - size) * B, B), size * B)
        return carry

    lax.fori_loop(0, pl.cdiv(cap, GROUP), turn, 0)


def joined(refs, start, size):
    return jnp.concatenate([ref[pl.ds(start, size), :] for ref in refs], 1)


def padded(cap):
    return pl.cdiv(cap, GROUP) * GROUP


def over_rows(first, last, step, body):
    whole = (last - first) // step

    def turn(i, carry):
        body(pl.multiple_of(first * B + i * (step * B), B), step * B)
        return carry

    lax.fori_loop(0, whole, turn, 0)
    rest = last - first - whole * step
    if rest:
        body((first + whole * step) * B, rest * B)


def clear_rest(out, cap):
    if out.shape[1] > cap * B:
        out[:, cap * B:] = jnp.zeros((out.shape[0], out.shape[1] - cap * B), out.dtype)


def solve_rows(inverse, refs, out, cap):
    width = out.shape[0] // 2
    clear_rest(out, cap)

    def body(start, size):
        rows = split(joined(refs, start, size))
        high, low = split(three_products(lanes_dot, inverse, rows))
        out[:width, pl.ds(start, size)] = high
        out[width:, pl.ds(start, size)] = low

    all_rows(cap, body)


def solve_one_kernel(cap, grid_size, place, *refs):
    gathered, parents = refs[:grid_size], refs[grid_size:2 * grid_size]
    (
        out, out_lag, out_inverse_one, out_inverse_two, out_lead, out_diag_one, out_diag_two,
        out_parent, weight_high, weight_low,
    ) = refs[2 * grid_size:]
    share, width = out_lead.shape
    row, col = place[0], place[1]
    first, second = cap * B, cap * B + width
    inverse = split(joined(gathered, first, width))
    out_inverse_one[...] = stacked(*inverse)
    inverse_two = split(joined(gathered, second, width))
    out_inverse_two[...] = stacked(*inverse_two)
    solved_parent = split(
        three_products(lanes_dot, inverse_two, split(joined(parents, 0, width)))
    )
    row_start = pl.multiple_of(row * share, share)
    col_start = pl.multiple_of(col * share, share)
    out_parent[...] = three_products(
        lanes_dot, inverse_two, split(joined(parents, row_start, share))
    )
    for k in range(grid_size):
        piece = split(gathered[k][pl.ds(first, width), :])
        high, low = split(three_products(plain_dot, solved_parent, piece))
        weight_high[:, k * share:(k + 1) * share] = high
        weight_low[:, k * share:(k + 1) * share] = low
    weight = (weight_high[...], weight_low[...])
    for start, diag in ((first, out_diag_one), (second, out_diag_two)):
        inv_row = split(joined(gathered, start + row_start, share))
        inv_col = split(joined(gathered, start + col_start, share))
        diag[...] = three_products(lanes_dot, inv_col, inv_row)
        if start == first:
            out_lead[...] = three_products(lanes_dot, inv_row, weight)

    clear_rest(out, cap)

    def body(start, size):
        rows = split(joined(gathered, start, size))
        high, low = split(three_products(lanes_dot, inverse, rows))
        out[:width, pl.ds(start, size)] = high
        out[width:, pl.ds(start, size)] = low
        out_lag[:, pl.ds(start, size)] = three_products(lanes_dot, weight, rows)

    all_rows(cap, body)


def solve_far_kernel(cap, inverse, *refs):
    gathered, out = refs[:-1], refs[-1]
    width = out.shape[0] // 2
    solve_rows((inverse[:width, :], inverse[width:, :]), gathered, out, cap)


def solve_two_kernel(cap_one, cap_two, inverse, lag, *refs):
    gathered, (out_full, out_root) = refs[:-2], refs[-2:]
    width = lag.shape[0]
    halves = (inverse[:width, :], inverse[width:, :])
    clear_rest(out_full, cap_one)
    clear_rest(out_root, cap_two)

    def both(start, size):
        own = three_products(lanes_dot, halves, split(joined(gathered, start, size)))
        high, low = split(own)
        out_root[:width, pl.ds(start, size)] = high
        out_root[width:, pl.ds(start, size)] = low
        high, low = split(own - lag[:, pl.ds(start, size)])
        out_full[:width, pl.ds(start, size)] = high
        out_full[width:, pl.ds(start, size)] = low

    all_rows(cap_two, both)
    if cap_one > cap_two:
        high, low = split(-lag[:, cap_two * B:])
        out_full[:width, cap_two * B:cap_one * B] = high
        out_full[width:, cap_two * B:cap_one * B] = low


def load_blocks(covs, blocks, order, lead, high, low):
    for j in range(GROUP):
        column = order[jnp.minimum(lead + j, blocks - 1)]
        for part, cov in enumerate(covs):
            piece = cov[pl.ds(column, B, stride=blocks), :]
            piece_high, piece_low = split(piece)
            high[part * B:(part + 1) * B, j * B:(j + 1) * B] = piece_high
            low[part * B:(part + 1) * B, j * B:(j + 1) * B] = piece_low


def groups_of(count):
    return (count + GROUP - 1) // GROUP


def image_kernel(blocks, order_in, order_out, counts, solved, *refs):
    covs, (out, high, low) = refs[:GROUP], refs[GROUP:]
    step = pl.program_id(0)
    width = out.shape[0]
    out[...] = jnp.zeros_like(out)

    @pl.when(GROUP * step < counts[1])
    def _():
        def turn(i, carry):
            load_blocks(covs, blocks, order_in, i * GROUP, high, low)
            span = pl.ds(pl.multiple_of(i * GROUP * B, GROUP * B), GROUP * B)
            both = lanes_dot(solved[:, span], high[...])
            more = lanes_dot(solved[:width, span], low[...])
            out[...] += both[:width] + both[width:] + more
            return carry

        lax.fori_loop(0, groups_of(counts[0]), turn, 0)


def image(covariance, blocks, solved, order_in, order_out, counts, cap_out, name):
    width = solved.shape[0] // 2
    cap_in = solved.shape[1] // B
    group = GROUP

    def place(which):
        def index_map(i, order_in, order_out, counts):
            last = jnp.maximum(counts[1] - 1, 0)
            return (order_out[jnp.minimum(group * i + which, last)], 0)

        return pl.BlockSpec((B * blocks, B), index_map)

    grid_spec = pltpu.PrefetchScalarGridSpec(
        num_scalar_prefetch=3,
        grid=(pl.cdiv(cap_out, group),),
        in_specs=[
            pl.BlockSpec(solved.shape, lambda i, *_: (0, 0), pipeline_mode=pl.Buffered(1)),
            *[place(which) for which in range(group)],
        ],
        out_specs=pl.BlockSpec((width, group * B), lambda i, *_: (0, i)),
        scratch_shapes=[
            pltpu.VMEM((group * B, group * B), jnp.bfloat16),
            pltpu.VMEM((group * B, group * B), jnp.bfloat16),
        ],
    )
    return pl.pallas_call(
        functools.partial(image_kernel, blocks),
        name=name,
        grid_spec=grid_spec,
        out_shape=shape_of((width, cap_out * B)),
        compiler_params=pltpu.CompilerParams(vmem_limit_bytes=VMEM_LIMIT),
        cost_estimate=pl.CostEstimate(
            flops=6 * width * cap_in * B * cap_out * B,
            bytes_accessed=(4 * blocks * B + 8 * width) * cap_out * B,
            transcendentals=0,
        ),
    )(order_in, order_out, counts, solved, *[covariance] * group)


def mirror_kernel(blocks, lead_in, order_in, order_out, counts, solved, *refs):
    covs, (out, high, low) = refs[:GROUP], refs[-3:]
    step = pl.program_id(0)
    width = out.shape[0]

    @pl.when(step == 0)
    def _():
        out[...] = refs[GROUP][...] if len(refs) > GROUP + 3 else jnp.zeros_like(out)

    @pl.when(lead_in + GROUP * step < counts[0])
    def _():
        def turn(i, carry):
            load_blocks(covs, blocks, order_out, i * GROUP, high, low)
            span = pl.ds(pl.multiple_of(i * GROUP * B, GROUP * B), GROUP * B)
            both = plain_dot(solved[...], high[...])
            more = plain_dot(solved[:width, :], low[...])
            out[:, span] += both[:width] + both[width:] + more
            return carry

        lax.fori_loop(0, groups_of(counts[1]), turn, 0)


def mirror_image(covariance, blocks, solved, order_in, order_out, counts, cap, lead_in, before, name):
    width = solved.shape[0] // 2
    group = GROUP
    cap = padded(cap)
    steps = solved.shape[1] // (group * B)

    def place(which):
        def index_map(i, order_in, order_out, counts):
            last = jnp.maximum(counts[0] - 1, 0)
            return (order_in[jnp.minimum(lead_in + group * i + which, last)], 0)

        return pl.BlockSpec((B * blocks, B), index_map)

    whole = pl.BlockSpec((width, cap * B), lambda i, *_: (0, 0), pipeline_mode=pl.Buffered(1))
    extra = () if before is None else (before,)
    grid_spec = pltpu.PrefetchScalarGridSpec(
        num_scalar_prefetch=3,
        grid=(steps,),
        in_specs=[
            pl.BlockSpec((2 * width, group * B), lambda i, *_: (0, i)),
            *[place(which) for which in range(group)],
            *[whole for _ in extra],
        ],
        out_specs=pl.BlockSpec((width, cap * B), lambda i, *_: (0, 0)),
        scratch_shapes=[pltpu.VMEM((group * B, group * B), jnp.bfloat16)] * 2,
    )
    return pl.pallas_call(
        functools.partial(mirror_kernel, blocks, lead_in),
        name=name,
        grid_spec=grid_spec,
        out_shape=shape_of((width, cap * B)),
        compiler_params=pltpu.CompilerParams(vmem_limit_bytes=VMEM_LIMIT),
        cost_estimate=pl.CostEstimate(
            flops=6 * width * cap * B * solved.shape[1],
            bytes_accessed=4 * (steps * group * B * blocks + 2 * width * cap) * B,
            transcendentals=0,
        ),
    )(order_in, order_out, counts, solved, *[covariance] * group, *extra)


def unpack_kernel(blocks, which, order, counts, *refs):
    parts, out = refs[:-1], refs[-1]
    share = parts[0].shape[0]
    out[...] = jnp.zeros_like(out)
    for i in range(min(blocks, parts[0].shape[1] // B)):

        @pl.when(i < counts[which])
        def _():
            span = slice(i * B, (i + 1) * B)
            block = -parts[0][:, span]
            for part in parts[1:]:
                block = block - part[:, span]
            out[pl.ds(order[i], share, stride=blocks), :] = block


def unpack(parts, order, counts, which, blocks, name):
    return call(
        functools.partial(unpack_kernel, blocks, which),
        name,
        shape_of((parts[0].shape[0] * blocks, B)),
        (order, counts, *parts),
        1,
        in_specs=[SMEM, SMEM] + [VMEM] * len(parts),
    )


def parent_out_kernel(place, lead, *refs):
    pieces, out = refs[:-1], refs[-1]
    share = pieces[0].shape[0]
    for k in range(len(pieces)):
        for j, piece in enumerate(pieces):

            @pl.when(place[1] ^ j == k)
            def _():
                span = slice(k * share, (k + 1) * share)
                out[:, span] = piece[...] - lead[:, span]


def gram_rows(image_rows, solved, total):
    width = solved.shape[0] // 2

    def body(start, size):
        span = pl.ds(start, size)
        rows = split(image_rows[:, span])
        total[...] += three_products(
            lanes_dot, rows, (solved[:width, span], solved[width:, span])
        )

    over_rows(0, image_rows.shape[1] // B, GROUP, body)


def gram_one_kernel(image_rows, solved_one, solved_two, out, total):
    grid_size, _, share = out.shape
    for half, solved in enumerate((solved_one, solved_two)):
        total[...] = jnp.zeros_like(total)
        gram_rows(image_rows, solved, total)
        for k in range(grid_size):
            out[k, half * share:(half + 1) * share, :] = total[:, k * share:(k + 1) * share]


def gram_two_kernel(image_rows, solved_root, image_parent, parent, out, total):
    grid_size, share, _ = out.shape
    total[...] = three_products(lanes_dot, split(image_parent[...].T), split(parent[...]))
    gram_rows(image_rows, solved_root, total)
    for k in range(grid_size):
        out[k, :, :] = total[:, k * share:(k + 1) * share]


def swap_grid(block, grid_size):
    pairs = [
        (r * grid_size + c, c * grid_size + r) for r in range(grid_size) for c in range(grid_size)
    ]
    return lax.ppermute(block, ("row", "col"), pairs)


def scatter_pieces(pieces, grid_size, position):
    return [
        lax.dynamic_index_in_dim(pieces, lax.rem(position + shift, grid_size), 0, keepdims=False)
        for shift in range(grid_size)
    ]


def scatter_sum(pieces, grid_size):
    total = pieces[0]
    for shift in range(1, grid_size):
        total = total + lax.ppermute(
            pieces[shift], "row", [(i, (i + shift) % grid_size) for i in range(grid_size)]
        )
    return total


def mixed_pieces(pieces, grid_size, position):
    return [
        lax.dynamic_index_in_dim(pieces, lax.rem(position + j, grid_size), 0, keepdims=False)
        for j in range(grid_size)
    ]


def mixed_sum(pieces, grid_size):
    total = None
    for j, piece in enumerate(pieces):
        pairs = [
            (r * grid_size + c, c * grid_size + (r + j) % grid_size)
            for r in range(grid_size)
            for c in range(grid_size)
        ]
        piece = lax.ppermute(piece, ("row", "col"), pairs)
        total = piece if total is None else total + piece
    return total


def gather_rows(block, grid_size):
    return [block] + [
        lax.ppermute(block, "row", [(i, (i + shift) % grid_size) for i in range(grid_size)])
        for shift in range(1, grid_size)
    ]


def plane_sum(partial, cap, grid_size, col):
    if grid_size != 4:
        return lax.psum_scatter(partial[:, :cap * B], "col", scatter_dimension=0, tiled=True)
    share = partial.shape[0] // grid_size
    core, chip = col % 2, col // 2
    pieces = partial.reshape(2, 2, share, partial.shape[1])
    part = (2, 1, share, cap * B)
    away = lax.dynamic_slice(pieces, (0, 1 - core, 0, 0), part)[:, 0]
    stay = lax.dynamic_slice(pieces, (0, core, 0, 0), part)[:, 0]
    pieces = stay + flip(away, "col", 1, grid_size)
    away = lax.dynamic_index_in_dim(pieces, 1 - chip, 0, keepdims=False)
    stay = lax.dynamic_index_in_dim(pieces, chip, 0, keepdims=False)
    return stay + flip(away, "col", 2, grid_size)


def swap_start(block, grid_size):
    if grid_size != 4:
        return block
    pairs = []
    for r in range(4):
        for c in range(4):
            if r // 2 != c // 2:
                pairs.append((4 * r + c, 4 * r + 2 * (r // 2) + c % 2))
    return lax.ppermute(block, ("row", "col"), pairs)


def swap_finish(block, moved, grid_size):
    if grid_size != 4:
        return [swap_grid(moved, grid_size)]
    direct, onward = [], []
    for r in range(4):
        for c in range(4):
            if r // 2 == c // 2:
                direct.append((4 * r + c, 4 * c + r))
            else:
                onward.append((4 * r + 2 * (r // 2) + c % 2, 4 * c + r))
    return [
        lax.ppermute(block, ("row", "col"), direct), lax.ppermute(moved, ("row", "col"), onward)
    ]


def flip(block, axis, bit, grid_size):
    return lax.ppermute(block, axis, [(i, i ^ bit) for i in range(grid_size)])


def gather_cols(block, grid_size, between=None):
    if grid_size != 4:
        gathered = lax.all_gather(block, "col")
        position = lax.axis_index("col")
        return [
            lax.dynamic_index_in_dim(gathered, position ^ j, 0, keepdims=False)
            for j in range(grid_size)
        ], between
    far = flip(block, "col", 2, grid_size)
    near = flip(block, "col", 1, grid_size)
    if between is not None:
        far, between = lax.optimization_barrier((far, between))
    return [block, near, far, flip(far, "col", 1, grid_size)], between


def exchange(gathered, grid_size, col):
    pieces = [
        lax.dynamic_index_in_dim(gathered, col ^ j, 0, keepdims=False) for j in range(grid_size)
    ]
    return [flip(piece, "col", j, grid_size) if j else piece for j, piece in enumerate(pieces)]


def run(
    cap_one, cap_two, row_order, col_order, info, place, root_covariance, factor_one, inverse_one,
    factor_parent, factor_root, inverse_two,
):
    grid_size = lax.axis_size("row")
    row = lax.axis_index("row")
    col = lax.axis_index("col")
    share, width = inverse_one.shape
    blocks = root_covariance.shape[3]
    covariance = root_covariance.reshape(-1, B)
    col_info = info[2:4]

    half = padded(pl.cdiv(cap_one, 2))
    parts = [(lead_in, min(half, cap_one - lead_in)) for lead_in in range(0, cap_one, half)]
    packed_one, *bare_parts = call(
        functools.partial(pack_one_kernel, cap_one),
        "pack_one",
        (
            shape_of((cap_one * B + 2 * width, share)),
            *[shape_of((size * B, share)) for _, size in parts],
        ),
        (row_order, info, factor_one.reshape(blocks, B, share), inverse_one, inverse_two),
        1,
        in_specs=[SMEM, SMEM, VMEM, VMEM, VMEM],
    )
    every_row = [lax.all_gather(part, "row") for part in bare_parts]
    parent_rows = call(
        place_kernel,
        "parent_rows",
        shape_of((width, share)),
        (place, *gather_rows(factor_parent, grid_size)),
        1,
        in_specs=[SMEM] + [VMEM] * grid_size,
    )
    packed_two = call(
        functools.partial(pack_two_kernel, cap_two),
        "pack_two",
        shape_of((cap_two * B, share)),
        (row_order, info, factor_root.reshape(blocks, B, share)),
        1,
        in_specs=[SMEM] * 2 + [VMEM],
    )
    gathered_one, (parent_rows, packed_two) = gather_cols(
        packed_one, grid_size, (parent_rows, packed_two)
    )
    gathered_parent, packed_two = gather_cols(parent_rows, grid_size, packed_two)

    solved_one, lag, lead_inverse, inverse_two, lead, diag_one, diag_two, parent = call(
        functools.partial(solve_one_kernel, cap_one, grid_size),
        "solve_one",
        (
            shape_of((2 * width, padded(cap_one) * B), jnp.bfloat16),
            shape_of((width, cap_one * B)),
            shape_of((2 * width, width), jnp.bfloat16),
            shape_of((2 * width, width), jnp.bfloat16),
            shape_of((share, width)),
            shape_of((share, share)),
            shape_of((share, share)),
            shape_of((width, share)),
        ),
        (place, *gathered_one, *gathered_parent),
        12 * width * width * cap_one * B,
        in_specs=[SMEM] + [VMEM] * (2 * grid_size),
        scratch=[pltpu.VMEM((width, width), jnp.bfloat16)] * 2,
    )
    gathered_two, lag = gather_cols(packed_two, grid_size, lag)
    solved_two, solved_root = call(
        functools.partial(solve_two_kernel, cap_one, cap_two),
        "solve_two",
        (
            shape_of((2 * width, padded(cap_one) * B), jnp.bfloat16),
            shape_of((2 * width, padded(cap_two) * B), jnp.bfloat16),
        ),
        (inverse_two, lag, *gathered_two),
        6 * width * width * cap_two * B,
    )
    far_rows = exchange(every_row[0], grid_size, col)
    solved_two, far_rows = lax.optimization_barrier((solved_two, far_rows))
    counts = jnp.stack([info[0], info[3]])
    image_two = image(covariance, blocks, solved_two, row_order, col_order, counts, cap_two, "image_two")
    every_row[-1], image_two = lax.optimization_barrier((every_row[-1], image_two))
    image_two = lax.psum_scatter(image_two, "row", scatter_dimension=0, tiled=True)

    def level_one(far_rows, last_rows, solved_one, solved_two, lead_inverse):
        counts = jnp.stack([info[2], info[0]])
        rows_one = None
        for lead_in, size in parts:
            if lead_in:
                far_rows = exchange(last_rows, grid_size, col)
            solved_far = call(
                functools.partial(solve_far_kernel, size),
                f"solve_far_{lead_in}",
                shape_of((2 * width, padded(size) * B), jnp.bfloat16),
                (lead_inverse, *far_rows),
                6 * width * width * size * B,
            )
            rows_one = mirror_image(
                covariance, blocks, solved_far, col_order, row_order, counts, cap_one, lead_in, rows_one,
                f"image_one_{lead_in}",
            )
        rows_one = plane_sum(rows_one, cap_one, grid_size, col)
        gram_one = call(
            gram_one_kernel,
            "gram_one",
            shape_of((grid_size, 2 * share, share)),
            (rows_one, solved_one, solved_two),
            12 * share * width * cap_one * B,
            scratch=[pltpu.VMEM((share, width), jnp.float32)],
        )
        return gram_one, rows_one

    def empty(*operands):
        return (
            jnp.zeros((grid_size, 2 * share, share), jnp.float32),
            jnp.zeros((share, cap_one * B), jnp.float32),
        )

    gram_one, rows_one = lax.cond(
        info[5] > 0, level_one, empty,
        far_rows, every_row[-1], solved_one, solved_two, lead_inverse,
    )
    moved = swap_start(rows_one, grid_size)
    lead_pieces = mixed_pieces(gram_one[:, share:], grid_size, row)
    lead_pieces, image_two = lax.optimization_barrier((lead_pieces, image_two))
    rows_two = swap_grid(image_two, grid_size)
    mixed = mixed_sum(lead_pieces, grid_size)
    mixed, moved, rows_one = lax.optimization_barrier((mixed, moved, rows_one))
    image_one = swap_finish(rows_one, moved, grid_size)
    own_lead = lax.dynamic_slice_in_dim(lead, col * share, share, 1)
    gram_two = call(
        gram_two_kernel,
        "gram_two",
        shape_of((grid_size, share, share)),
        (rows_two, solved_root, own_lead - mixed, parent),
        6 * share * width * cap_two * B,
        scratch=[pltpu.VMEM((share, width), jnp.float32)],
    )
    grams = jnp.concatenate([gram_one[:, :share], gram_two], 1)
    pieces, mixed = lax.optimization_barrier((scatter_pieces(grams, grid_size, row), mixed))
    grams = scatter_sum(pieces, grid_size)
    block_one = grams[:share] + diag_one
    block_two = grams[share:] + diag_two
    parent_out = call(
        parent_out_kernel,
        "parent_out",
        shape_of((share, width)),
        (place, lead, *gather_cols(mixed, grid_size)[0]),
        1,
        in_specs=[SMEM] + [VMEM] * (1 + grid_size),
    )
    cross_two = unpack([image_two], col_order, col_info, 1, blocks, "cross_two")
    cross_one = unpack(image_one, col_order, col_info, 0, blocks, "cross_one")
    return cross_one, block_one, parent_out, cross_two, block_two


def capacities_of(blocks):
    parts = ((0.9, 0.7), (0.8, 0.65), (0.75, 0.6), (0.7, 0.55)) if blocks >= 16 else ()
    return [(blocks, blocks)] + [(round(one * blocks), round(two * blocks)) for one, two in parts]


def local(
    root_covariance, factor_one, inverse_one, pattern_one, factor_parent, factor_root, inverse_two,
    pattern_two,
):
    blocks = root_covariance.shape[3]
    capacities = capacities_of(blocks)
    place = jnp.stack([lax.axis_index("row"), lax.axis_index("col")]).astype(jnp.int32)
    row_order, col_order, info = pl.pallas_call(
        functools.partial(plan_kernel, capacities),
        name="plan",
        out_shape=(
            shape_of((blocks,), jnp.int32), shape_of((blocks,), jnp.int32), shape_of((6,), jnp.int32)
        ),
        in_specs=[SMEM] * 3,
        out_specs=(SMEM,) * 3,
    )(place, pattern_one, pattern_two)
    operands = (
        row_order, col_order, info, place, root_covariance, factor_one, inverse_one,
        factor_parent, factor_root, inverse_two,
    )
    branches = [functools.partial(run, one, two) for one, two in capacities]
    if len(branches) == 1:
        results = branches[0](*operands)
    else:
        results = lax.switch(info[4], branches, *operands)
    cross_one, block_one, parent_out, cross_two, block_two = results
    cross_one = cross_one.reshape(-1, blocks, 1, B)
    cross_two = cross_two.reshape(-1, blocks, 1, B)
    return cross_one, block_one, parent_out, cross_two, block_two


def solution(mesh):
    return jax.shard_map(
        local,
        mesh=mesh,
        in_specs=(
            P("grp", "col", None, None, "row", None),
            P("grp", "row", None, "col"),
            P(("grp", "col"), None),
            P("grp"),
            P(("grp", "row"), "col"),
            P("grp", "row", None, "col"),
            P(("grp", "col"), None),
            P("grp"),
        ),
        out_specs=(
            P(("grp", "row"), None, "col", None),
            P(("grp", "col"), "row"),
            P(("grp", "row"), None),
            P(("grp", "row"), None, "col", None),
            P(("grp", "col"), "row"),
        ),
        check_vma=False,
    )
```

```python
import functools

import jax
import jax.numpy as jnp
from jax import lax
from jax.experimental import pallas as pl
from jax.experimental.pallas import tpu as pltpu
from jax.sharding import PartitionSpec as P

B = 128
VMEM_LIMIT = 52 * 1024 * 1024
GROUP = 4
VMEM = pl.BlockSpec(memory_space=pltpu.VMEM)
SMEM = pl.BlockSpec(memory_space=pltpu.SMEM)


def split(values):
    high = values.astype(jnp.bfloat16)
    low = (values - high.astype(jnp.float32)).astype(jnp.bfloat16)
    return high, low


def lanes_dot(left, right):
    return lax.dot_general(
        left, right, (((1,), (1,)), ((), ())), preferred_element_type=jnp.float32
    )


def plain_dot(left, right):
    return lax.dot_general(
        left, right, (((1,), (0,)), ((), ())), preferred_element_type=jnp.float32
    )


def three_products(dot, left, right):
    left_high, left_low = left
    right_high, right_low = right
    rows = left_high.shape[0]
    both = dot(jnp.concatenate([left_high, left_low], 0), right_high)
    return both[:rows] + both[rows:] + dot(left_high, right_low)


def stacked(high, low):
    return jnp.concatenate([high, low], 0)


def call(kernel, name, out_shape, operands, flops, in_specs=None, scratch=()):
    size = sum(a.size * a.dtype.itemsize for a in operands)
    size += sum(a.size * a.dtype.itemsize for a in jax.tree.leaves(out_shape))
    return pl.pallas_call(
        kernel,
        name=name,
        out_shape=out_shape,
        in_specs=in_specs or [VMEM] * len(operands),
        out_specs=jax.tree.map(lambda _: VMEM, out_shape),
        scratch_shapes=scratch,
        compiler_params=pltpu.CompilerParams(vmem_limit_bytes=VMEM_LIMIT),
        cost_estimate=pl.CostEstimate(
            flops=flops, bytes_accessed=size, transcendentals=0
        ),
    )(*operands)


def shape_of(shape, dtype=jnp.float32):
    return jax.ShapeDtypeStruct(shape, dtype)


def plan_kernel(capacities, place, pattern_one, pattern_two, row_order, col_order, info):
    blocks = row_order.shape[0]
    grid_size = pattern_one.shape[0] // blocks
    largest_one, largest_two = jnp.int32(0), jnp.int32(0)
    counts_one, counts_two = [], []
    for p in range(grid_size):

        def count(b, carry):
            return (
                carry[0] + pattern_one[b * grid_size + p],
                carry[1] + pattern_two[b * grid_size + p],
            )

        one, two = lax.fori_loop(0, blocks, count, (jnp.int32(0), jnp.int32(0)))
        counts_one.append(one)
        counts_two.append(two)
        largest_one = jnp.maximum(largest_one, one)
        largest_two = jnp.maximum(largest_two, two)
    choice = jnp.int32(0)
    for i in range(1, len(capacities)):
        fits = (largest_one <= capacities[i][0]) & (largest_two <= capacities[i][1])
        choice = jnp.where(fits, i, choice)
    info[4] = choice
    info[5] = largest_one
    for axis, order in enumerate((row_order, col_order)):
        position = place[axis]
        own_one, own_two = jnp.int32(0), jnp.int32(0)
        for p in range(grid_size):
            own_one = jnp.where(position == p, counts_one[p], own_one)
            own_two = jnp.where(position == p, counts_two[p], own_two)
        info[2 * axis] = own_one
        info[2 * axis + 1] = own_two

        def put(b, carry):
            one = pattern_one[b * grid_size + position]
            two = pattern_two[b * grid_size + position]
            slot = jnp.where(two > 0, carry[0], jnp.where(one > 0, carry[1], carry[2]))
            order[slot] = b
            return (carry[0] + two, carry[1] + one - two, carry[2] + 1 - one)

        lax.fori_loop(0, blocks, put, (jnp.int32(0), own_two, own_one))


def pack_one_kernel(cap, order, info, factor, inverse_one, inverse_two, out, *out_parts):
    width = inverse_one.shape[1]
    part_cap = out_parts[0].shape[0] // B
    for i in range(cap):
        block = jnp.where(i < info[0], factor[order[i]], 0.0)
        out[pl.ds(i * B, B), :] = block
        out_parts[i // part_cap][pl.ds(i % part_cap * B, B), :] = block
    out[pl.ds(cap * B, width), :] = inverse_one[...].T
    out[pl.ds(cap * B + width, width), :] = inverse_two[...].T


def pack_two_kernel(cap, order, info, factor, out):
    for i in range(cap):
        out[pl.ds(i * B, B), :] = jnp.where(i < info[1], factor[order[i]], 0.0)


def place_kernel(place, *refs):
    pieces, out = refs[:-1], refs[-1]
    share = pieces[0].shape[0]
    grid_size = len(pieces)
    for shift, piece in enumerate(pieces):
        source = lax.rem(place[0] + grid_size - shift, grid_size)
        out[pl.ds(pl.multiple_of(source * share, share), share), :] = piece[...]


def all_rows(cap, body):
    size = min(cap, GROUP)

    def turn(i, carry):
        body(pl.multiple_of(jnp.minimum(i * GROUP, cap - size) * B, B), size * B)
        return carry

    lax.fori_loop(0, pl.cdiv(cap, GROUP), turn, 0)


def joined(refs, start, size):
    return jnp.concatenate([ref[pl.ds(start, size), :] for ref in refs], 1)


def padded(cap):
    return pl.cdiv(cap, GROUP) * GROUP


def over_rows(first, last, step, body):
    whole = (last - first) // step

    def turn(i, carry):
        body(pl.multiple_of(first * B + i * (step * B), B), step * B)
        return carry

    lax.fori_loop(0, whole, turn, 0)
    rest = last - first - whole * step
    if rest:
        body((first + whole * step) * B, rest * B)


def clear_rest(out, cap):
    if out.shape[1] > cap * B:
        out[:, cap * B:] = jnp.zeros((out.shape[0], out.shape[1] - cap * B), out.dtype)


def solve_rows(inverse, refs, out, cap):
    width = out.shape[0] // 2
    clear_rest(out, cap)

    def body(start, size):
        rows = split(joined(refs, start, size))
        high, low = split(three_products(lanes_dot, inverse, rows))
        out[:width, pl.ds(start, size)] = high
        out[width:, pl.ds(start, size)] = low

    all_rows(cap, body)


def solve_one_kernel(cap, grid_size, place, *refs):
    gathered, parents = refs[:grid_size], refs[grid_size:2 * grid_size]
    (
        out, out_lag, out_inverse_one, out_inverse_two, out_lead, out_diag_one, out_diag_two,
        out_parent, weight_high, weight_low,
    ) = refs[2 * grid_size:]
    share, width = out_lead.shape
    row, col = place[0], place[1]
    first, second = cap * B, cap * B + width
    inverse = split(joined(gathered, first, width))
    out_inverse_one[...] = stacked(*inverse)
    inverse_two = split(joined(gathered, second, width))
    out_inverse_two[...] = stacked(*inverse_two)
    solved_parent = split(
        three_products(lanes_dot, inverse_two, split(joined(parents, 0, width)))
    )
    row_start = pl.multiple_of(row * share, share)
    col_start = pl.multiple_of(col * share, share)
    out_parent[...] = three_products(
        lanes_dot, inverse_two, split(joined(parents, row_start, share))
    )
    for k in range(grid_size):
        piece = split(gathered[k][pl.ds(first, width), :])
        high, low = split(three_products(plain_dot, solved_parent, piece))
        weight_high[:, k * share:(k + 1) * share] = high
        weight_low[:, k * share:(k + 1) * share] = low
    weight = (weight_high[...], weight_low[...])
    for start, diag in ((first, out_diag_one), (second, out_diag_two)):
        inv_row = split(joined(gathered, start + row_start, share))
        inv_col = split(joined(gathered, start + col_start, share))
        diag[...] = three_products(lanes_dot, inv_col, inv_row)
        if start == first:
            out_lead[...] = three_products(lanes_dot, inv_row, weight)

    clear_rest(out, cap)

    def body(start, size):
        rows = split(joined(gathered, start, size))
        high, low = split(three_products(lanes_dot, inverse, rows))
        out[:width, pl.ds(start, size)] = high
        out[width:, pl.ds(start, size)] = low
        out_lag[:, pl.ds(start, size)] = three_products(lanes_dot, weight, rows)

    all_rows(cap, body)


def solve_far_kernel(cap, inverse, *refs):
    gathered, out = refs[:-1], refs[-1]
    width = out.shape[0] // 2
    solve_rows((inverse[:width, :], inverse[width:, :]), gathered, out, cap)


def solve_two_kernel(cap_one, cap_two, inverse, lag, *refs):
    gathered, (out_full, out_root) = refs[:-2], refs[-2:]
    width = lag.shape[0]
    halves = (inverse[:width, :], inverse[width:, :])
    clear_rest(out_full, cap_one)
    clear_rest(out_root, cap_two)

    def both(start, size):
        own = three_products(lanes_dot, halves, split(joined(gathered, start, size)))
        high, low = split(own)
        out_root[:width, pl.ds(start, size)] = high
        out_root[width:, pl.ds(start, size)] = low
        high, low = split(own - lag[:, pl.ds(start, size)])
        out_full[:width, pl.ds(start, size)] = high
        out_full[width:, pl.ds(start, size)] = low

    all_rows(cap_two, both)
    if cap_one > cap_two:
        high, low = split(-lag[:, cap_two * B:])
        out_full[:width, cap_two * B:cap_one * B] = high
        out_full[width:, cap_two * B:cap_one * B] = low


def load_blocks(covs, blocks, order, lead, high, low):
    for j in range(GROUP):
        column = order[jnp.minimum(lead + j, blocks - 1)]
        for part, cov in enumerate(covs):
            piece = cov[pl.ds(column, B, stride=blocks), :]
            piece_high, piece_low = split(piece)
            high[part * B:(part + 1) * B, j * B:(j + 1) * B] = piece_high
            low[part * B:(part + 1) * B, j * B:(j + 1) * B] = piece_low


def groups_of(count):
    return (count + GROUP - 1) // GROUP


def image_kernel(blocks, order_in, order_out, counts, solved, *refs):
    covs, (out, high, low) = refs[:GROUP], refs[GROUP:]
    step = pl.program_id(0)
    width = out.shape[0]
    out[...] = jnp.zeros_like(out)

    @pl.when(GROUP * step < counts[1])
    def _():
        def turn(i, carry):
            load_blocks(covs, blocks, order_in, i * GROUP, high, low)
            span = pl.ds(pl.multiple_of(i * GROUP * B, GROUP * B), GROUP * B)
            both = lanes_dot(solved[:, span], high[...])
            more = lanes_dot(solved[:width, span], low[...])
            out[...] += both[:width] + both[width:] + more
            return carry

        lax.fori_loop(0, groups_of(counts[0]), turn, 0)


def image(covariance, blocks, solved, order_in, order_out, counts, cap_out, name):
    width = solved.shape[0] // 2
    cap_in = solved.shape[1] // B
    group = GROUP

    def place(which):
        def index_map(i, order_in, order_out, counts):
            last = jnp.maximum(counts[1] - 1, 0)
            return (order_out[jnp.minimum(group * i + which, last)], 0)

        return pl.BlockSpec((B * blocks, B), index_map)

    grid_spec = pltpu.PrefetchScalarGridSpec(
        num_scalar_prefetch=3,
        grid=(pl.cdiv(cap_out, group),),
        in_specs=[
            pl.BlockSpec(solved.shape, lambda i, *_: (0, 0), pipeline_mode=pl.Buffered(1)),
            *[place(which) for which in range(group)],
        ],
        out_specs=pl.BlockSpec((width, group * B), lambda i, *_: (0, i)),
        scratch_shapes=[
            pltpu.VMEM((group * B, group * B), jnp.bfloat16),
            pltpu.VMEM((group * B, group * B), jnp.bfloat16),
        ],
    )
    return pl.pallas_call(
        functools.partial(image_kernel, blocks),
        name=name,
        grid_spec=grid_spec,
        out_shape=shape_of((width, cap_out * B)),
        compiler_params=pltpu.CompilerParams(vmem_limit_bytes=VMEM_LIMIT),
        cost_estimate=pl.CostEstimate(
            flops=6 * width * cap_in * B * cap_out * B,
            bytes_accessed=(4 * blocks * B + 8 * width) * cap_out * B,
            transcendentals=0,
        ),
    )(order_in, order_out, counts, solved, *[covariance] * group)


def mirror_kernel(blocks, lead_in, order_in, order_out, counts, solved, *refs):
    covs, (out, high, low) = refs[:GROUP], refs[-3:]
    step = pl.program_id(0)
    width = out.shape[0]

    @pl.when(step == 0)
    def _():
        out[...] = refs[GROUP][...] if len(refs) > GROUP + 3 else jnp.zeros_like(out)

    @pl.when(lead_in + GROUP * step < counts[0])
    def _():
        def turn(i, carry):
            load_blocks(covs, blocks, order_out, i * GROUP, high, low)
            span = pl.ds(pl.multiple_of(i * GROUP * B, GROUP * B), GROUP * B)
            both = plain_dot(solved[...], high[...])
            more = plain_dot(solved[:width, :], low[...])
            out[:, span] += both[:width] + both[width:] + more
            return carry

        lax.fori_loop(0, groups_of(counts[1]), turn, 0)


def mirror_image(covariance, blocks, solved, order_in, order_out, counts, cap, lead_in, before, name):
    width = solved.shape[0] // 2
    group = GROUP
    cap = padded(cap)
    steps = solved.shape[1] // (group * B)

    def place(which):
        def index_map(i, order_in, order_out, counts):
            last = jnp.maximum(counts[0] - 1, 0)
            return (order_in[jnp.minimum(lead_in + group * i + which, last)], 0)

        return pl.BlockSpec((B * blocks, B), index_map)

    whole = pl.BlockSpec((width, cap * B), lambda i, *_: (0, 0), pipeline_mode=pl.Buffered(1))
    extra = () if before is None else (before,)
    grid_spec = pltpu.PrefetchScalarGridSpec(
        num_scalar_prefetch=3,
        grid=(steps,),
        in_specs=[
            pl.BlockSpec((2 * width, group * B), lambda i, *_: (0, i)),
            *[place(which) for which in range(group)],
            *[whole for _ in extra],
        ],
        out_specs=pl.BlockSpec((width, cap * B), lambda i, *_: (0, 0)),
        scratch_shapes=[pltpu.VMEM((group * B, group * B), jnp.bfloat16)] * 2,
    )
    return pl.pallas_call(
        functools.partial(mirror_kernel, blocks, lead_in),
        name=name,
        grid_spec=grid_spec,
        out_shape=shape_of((width, cap * B)),
        compiler_params=pltpu.CompilerParams(vmem_limit_bytes=VMEM_LIMIT),
        cost_estimate=pl.CostEstimate(
            flops=6 * width * cap * B * solved.shape[1],
            bytes_accessed=4 * (steps * group * B * blocks + 2 * width * cap) * B,
            transcendentals=0,
        ),
    )(order_in, order_out, counts, solved, *[covariance] * group, *extra)


def unpack_kernel(blocks, which, order, counts, *refs):
    parts, out = refs[:-1], refs[-1]
    share = parts[0].shape[0]
    out[...] = jnp.zeros_like(out)
    for i in range(min(blocks, parts[0].shape[1] // B)):

        @pl.when(i < counts[which])
        def _():
            span = slice(i * B, (i + 1) * B)
            block = -parts[0][:, span]
            for part in parts[1:]:
                block = block - part[:, span]
            out[pl.ds(order[i], share, stride=blocks), :] = block


def unpack(parts, order, counts, which, blocks, name):
    return call(
        functools.partial(unpack_kernel, blocks, which),
        name,
        shape_of((parts[0].shape[0] * blocks, B)),
        (order, counts, *parts),
        1,
        in_specs=[SMEM, SMEM] + [VMEM] * len(parts),
    )


def parent_out_kernel(place, lead, *refs):
    pieces, out = refs[:-1], refs[-1]
    share = pieces[0].shape[0]
    for k in range(len(pieces)):
        for j, piece in enumerate(pieces):

            @pl.when(place[1] ^ j == k)
            def _():
                span = slice(k * share, (k + 1) * share)
                out[:, span] = piece[...] - lead[:, span]


def gram_rows(image_rows, solved, total):
    width = solved.shape[0] // 2

    def body(start, size):
        span = pl.ds(start, size)
        rows = split(image_rows[:, span])
        total[...] += three_products(
            lanes_dot, rows, (solved[:width, span], solved[width:, span])
        )

    over_rows(0, image_rows.shape[1] // B, GROUP, body)


def gram_one_kernel(image_rows, solved_one, solved_two, out, total):
    grid_size, _, share = out.shape
    for half, solved in enumerate((solved_one, solved_two)):
        total[...] = jnp.zeros_like(total)
        gram_rows(image_rows, solved, total)
        for k in range(grid_size):
            out[k, half * share:(half + 1) * share, :] = total[:, k * share:(k + 1) * share]


def gram_two_kernel(image_rows, solved_root, image_parent, parent, out, total):
    grid_size, share, _ = out.shape
    total[...] = three_products(lanes_dot, split(image_parent[...].T), split(parent[...]))
    gram_rows(image_rows, solved_root, total)
    for k in range(grid_size):
        out[k, :, :] = total[:, k * share:(k + 1) * share]


def swap_grid(block, grid_size):
    pairs = [
        (r * grid_size + c, c * grid_size + r) for r in range(grid_size) for c in range(grid_size)
    ]
    return lax.ppermute(block, ("row", "col"), pairs)


def scatter_pieces(pieces, grid_size, position):
    return [
        lax.dynamic_index_in_dim(pieces, lax.rem(position + shift, grid_size), 0, keepdims=False)
        for shift in range(grid_size)
    ]


def scatter_sum(pieces, grid_size):
    total = pieces[0]
    for shift in range(1, grid_size):
        total = total + lax.ppermute(
            pieces[shift], "row", [(i, (i + shift) % grid_size) for i in range(grid_size)]
        )
    return total


def mixed_pieces(pieces, grid_size, position):
    return [
        lax.dynamic_index_in_dim(pieces, lax.rem(position + j, grid_size), 0, keepdims=False)
        for j in range(grid_size)
    ]


def mixed_sum(pieces, grid_size):
    total = None
    for j, piece in enumerate(pieces):
        pairs = [
            (r * grid_size + c, c * grid_size + (r + j) % grid_size)
            for r in range(grid_size)
            for c in range(grid_size)
        ]
        piece = lax.ppermute(piece, ("row", "col"), pairs)
        total = piece if total is None else total + piece
    return total


def gather_rows(block, grid_size):
    return [block] + [
        lax.ppermute(block, "row", [(i, (i + shift) % grid_size) for i in range(grid_size)])
        for shift in range(1, grid_size)
    ]


def plane_sum(partial, cap, grid_size, col):
    if grid_size != 4:
        return lax.psum_scatter(partial[:, :cap * B], "col", scatter_dimension=0, tiled=True)
    share = partial.shape[0] // grid_size
    core, chip = col % 2, col // 2
    pieces = partial.reshape(2, 2, share, partial.shape[1])
    part = (2, 1, share, cap * B)
    away = lax.dynamic_slice(pieces, (0, 1 - core, 0, 0), part)[:, 0]
    stay = lax.dynamic_slice(pieces, (0, core, 0, 0), part)[:, 0]
    pieces = stay + flip(away, "col", 1, grid_size)
    away = lax.dynamic_index_in_dim(pieces, 1 - chip, 0, keepdims=False)
    stay = lax.dynamic_index_in_dim(pieces, chip, 0, keepdims=False)
    return stay + flip(away, "col", 2, grid_size)


def swap_start(block, grid_size):
    if grid_size != 4:
        return block
    pairs = []
    for r in range(4):
        for c in range(4):
            if r // 2 != c // 2:
                pairs.append((4 * r + c, 4 * r + 2 * (r // 2) + c % 2))
    return lax.ppermute(block, ("row", "col"), pairs)


def swap_finish(block, moved, grid_size):
    if grid_size != 4:
        return [swap_grid(moved, grid_size)]
    direct, onward = [], []
    for r in range(4):
        for c in range(4):
            if r // 2 == c // 2:
                direct.append((4 * r + c, 4 * c + r))
            else:
                onward.append((4 * r + 2 * (r // 2) + c % 2, 4 * c + r))
    return [
        lax.ppermute(block, ("row", "col"), direct), lax.ppermute(moved, ("row", "col"), onward)
    ]


def flip(block, axis, bit, grid_size):
    return lax.ppermute(block, axis, [(i, i ^ bit) for i in range(grid_size)])


def gather_cols(block, grid_size, between=None):
    if grid_size != 4:
        gathered = lax.all_gather(block, "col")
        position = lax.axis_index("col")
        return [
            lax.dynamic_index_in_dim(gathered, position ^ j, 0, keepdims=False)
            for j in range(grid_size)
        ], between
    far = flip(block, "col", 2, grid_size)
    near = flip(block, "col", 1, grid_size)
    if between is not None:
        far, between = lax.optimization_barrier((far, between))
    return [block, near, far, flip(far, "col", 1, grid_size)], between


def exchange(gathered, grid_size, col):
    pieces = [
        lax.dynamic_index_in_dim(gathered, col ^ j, 0, keepdims=False) for j in range(grid_size)
    ]
    return [flip(piece, "col", j, grid_size) if j else piece for j, piece in enumerate(pieces)]


def run(
    cap_one, cap_two, covariance, row_order, col_order, info, place, factor_one, inverse_one,
    factor_parent, factor_root, inverse_two,
):
    grid_size = lax.axis_size("row")
    row = lax.axis_index("row")
    col = lax.axis_index("col")
    share, width = inverse_one.shape
    blocks = row_order.shape[0]
    col_info = info[2:4]

    half = padded(pl.cdiv(cap_one, 2))
    parts = [(lead_in, min(half, cap_one - lead_in)) for lead_in in range(0, cap_one, half)]
    packed_one, *bare_parts = call(
        functools.partial(pack_one_kernel, cap_one),
        "pack_one",
        (
            shape_of((cap_one * B + 2 * width, share)),
            *[shape_of((size * B, share)) for _, size in parts],
        ),
        (row_order, info, factor_one.reshape(blocks, B, share), inverse_one, inverse_two),
        1,
        in_specs=[SMEM, SMEM, VMEM, VMEM, VMEM],
    )
    every_row = [lax.all_gather(part, "row") for part in bare_parts]
    parent_rows = call(
        place_kernel,
        "parent_rows",
        shape_of((width, share)),
        (place, *gather_rows(factor_parent, grid_size)),
        1,
        in_specs=[SMEM] + [VMEM] * grid_size,
    )
    packed_two = call(
        functools.partial(pack_two_kernel, cap_two),
        "pack_two",
        shape_of((cap_two * B, share)),
        (row_order, info, factor_root.reshape(blocks, B, share)),
        1,
        in_specs=[SMEM] * 2 + [VMEM],
    )
    gathered_one, (parent_rows, packed_two) = gather_cols(
        packed_one, grid_size, (parent_rows, packed_two)
    )
    gathered_parent, packed_two = gather_cols(parent_rows, grid_size, packed_two)

    solved_one, lag, lead_inverse, inverse_two, lead, diag_one, diag_two, parent = call(
        functools.partial(solve_one_kernel, cap_one, grid_size),
        "solve_one",
        (
            shape_of((2 * width, padded(cap_one) * B), jnp.bfloat16),
            shape_of((width, cap_one * B)),
            shape_of((2 * width, width), jnp.bfloat16),
            shape_of((2 * width, width), jnp.bfloat16),
            shape_of((share, width)),
            shape_of((share, share)),
            shape_of((share, share)),
            shape_of((width, share)),
        ),
        (place, *gathered_one, *gathered_parent),
        12 * width * width * cap_one * B,
        in_specs=[SMEM] + [VMEM] * (2 * grid_size),
        scratch=[pltpu.VMEM((width, width), jnp.bfloat16)] * 2,
    )
    gathered_two, lag = gather_cols(packed_two, grid_size, lag)
    solved_two, solved_root = call(
        functools.partial(solve_two_kernel, cap_one, cap_two),
        "solve_two",
        (
            shape_of((2 * width, padded(cap_one) * B), jnp.bfloat16),
            shape_of((2 * width, padded(cap_two) * B), jnp.bfloat16),
        ),
        (inverse_two, lag, *gathered_two),
        6 * width * width * cap_two * B,
    )
    far_rows = exchange(every_row[0], grid_size, col)
    solved_two, far_rows = lax.optimization_barrier((solved_two, far_rows))
    counts = jnp.stack([info[0], info[3]])
    image_two = image(covariance, blocks, solved_two, row_order, col_order, counts, cap_two, "image_two")
    every_row[-1], image_two = lax.optimization_barrier((every_row[-1], image_two))
    image_two = lax.psum_scatter(image_two, "row", scatter_dimension=0, tiled=True)

    def level_one(far_rows, last_rows, solved_one, solved_two, lead_inverse):
        counts = jnp.stack([info[2], info[0]])
        rows_one = None
        for lead_in, size in parts:
            if lead_in:
                far_rows = exchange(last_rows, grid_size, col)
            solved_far = call(
                functools.partial(solve_far_kernel, size),
                f"solve_far_{lead_in}",
                shape_of((2 * width, padded(size) * B), jnp.bfloat16),
                (lead_inverse, *far_rows),
                6 * width * width * size * B,
            )
            rows_one = mirror_image(
                covariance, blocks, solved_far, col_order, row_order, counts, cap_one, lead_in, rows_one,
                f"image_one_{lead_in}",
            )
        rows_one = plane_sum(rows_one, cap_one, grid_size, col)
        gram_one = call(
            gram_one_kernel,
            "gram_one",
            shape_of((grid_size, 2 * share, share)),
            (rows_one, solved_one, solved_two),
            12 * share * width * cap_one * B,
            scratch=[pltpu.VMEM((share, width), jnp.float32)],
        )
        return gram_one, rows_one

    def empty(*operands):
        return (
            jnp.zeros((grid_size, 2 * share, share), jnp.float32),
            jnp.zeros((share, cap_one * B), jnp.float32),
        )

    gram_one, rows_one = lax.cond(
        info[5] > 0, level_one, empty,
        far_rows, every_row[-1], solved_one, solved_two, lead_inverse,
    )
    moved = swap_start(rows_one, grid_size)
    lead_pieces = mixed_pieces(gram_one[:, share:], grid_size, row)
    lead_pieces, image_two = lax.optimization_barrier((lead_pieces, image_two))
    rows_two = swap_grid(image_two, grid_size)
    mixed = mixed_sum(lead_pieces, grid_size)
    mixed, moved, rows_one = lax.optimization_barrier((mixed, moved, rows_one))
    image_one = swap_finish(rows_one, moved, grid_size)
    own_lead = lax.dynamic_slice_in_dim(lead, col * share, share, 1)
    gram_two = call(
        gram_two_kernel,
        "gram_two",
        shape_of((grid_size, share, share)),
        (rows_two, solved_root, own_lead - mixed, parent),
        6 * share * width * cap_two * B,
        scratch=[pltpu.VMEM((share, width), jnp.float32)],
    )
    grams = jnp.concatenate([gram_one[:, :share], gram_two], 1)
    pieces, mixed = lax.optimization_barrier((scatter_pieces(grams, grid_size, row), mixed))
    grams = scatter_sum(pieces, grid_size)
    block_one = grams[:share] + diag_one
    block_two = grams[share:] + diag_two
    parent_out = call(
        parent_out_kernel,
        "parent_out",
        shape_of((share, width)),
        (place, lead, *gather_cols(mixed, grid_size)[0]),
        1,
        in_specs=[SMEM] + [VMEM] * (1 + grid_size),
    )
    cross_two = unpack([image_two], col_order, col_info, 1, blocks, "cross_two")
    cross_one = unpack(image_one, col_order, col_info, 0, blocks, "cross_one")
    return cross_one, block_one, parent_out, cross_two, block_two


def capacities_of(blocks):
    parts = ((0.9, 0.7), (0.8, 0.65), (0.75, 0.6), (0.7, 0.55)) if blocks >= 16 else ()
    return [(blocks, blocks)] + [(round(one * blocks), round(two * blocks)) for one, two in parts]


def once(branch, operands, turn, results):
    covariance, *others = operands
    _, others = lax.optimization_barrier((turn, others))
    return branch(covariance, *others)


def local(
    root_covariance, factor_one, inverse_one, pattern_one, factor_parent, factor_root, inverse_two,
    pattern_two,
):
    blocks = root_covariance.shape[3]
    share, width = inverse_one.shape
    capacities = capacities_of(blocks)
    place = jnp.stack([lax.axis_index("row"), lax.axis_index("col")]).astype(jnp.int32)
    row_order, col_order, info = pl.pallas_call(
        functools.partial(plan_kernel, capacities),
        name="plan",
        out_shape=(
            shape_of((blocks,), jnp.int32), shape_of((blocks,), jnp.int32), shape_of((6,), jnp.int32)
        ),
        in_specs=[SMEM] * 3,
        out_specs=(SMEM,) * 3,
    )(place, pattern_one, pattern_two)
    operands = (
        root_covariance.reshape(-1, B), row_order, col_order, info, place, factor_one, inverse_one,
        factor_parent, factor_root, inverse_two,
    )
    branches = [functools.partial(run, one, two) for one, two in capacities]
    if len(branches) == 1:
        results = branches[0](*operands)
    else:
        results = tuple(jnp.zeros(shape, jnp.float32) for shape in (
            (share * blocks, B), (share, share), (share, width), (share * blocks, B), (share, share)
        ))
        for k, branch in enumerate(branches):
            results = lax.fori_loop(
                0, (info[4] == k).astype(jnp.int32), functools.partial(once, branch, operands), results
            )
    cross_one, block_one, parent_out, cross_two, block_two = results
    cross_one = cross_one.reshape(-1, blocks, 1, B)
    cross_two = cross_two.reshape(-1, blocks, 1, B)
    return cross_one, block_one, parent_out, cross_two, block_two


def solution(mesh):
    return jax.shard_map(
        local,
        mesh=mesh,
        in_specs=(
            P("grp", "col", None, None, "row", None),
            P("grp", "row", None, "col"),
            P(("grp", "col"), None),
            P("grp"),
            P(("grp", "row"), "col"),
            P("grp", "row", None, "col"),
            P(("grp", "col"), None),
            P("grp"),
        ),
        out_specs=(
            P(("grp", "row"), None, "col", None),
            P(("grp", "col"), "row"),
            P(("grp", "row"), None),
            P(("grp", "row"), None, "col", None),
            P(("grp", "col"), "row"),
        ),
        check_vma=False,
    )
```

```python
import functools

import jax
import jax.numpy as jnp
from jax import lax
from jax.experimental import pallas as pl
from jax.experimental.pallas import tpu as pltpu
from jax.sharding import PartitionSpec as P

B = 128
VMEM_LIMIT = 52 * 1024 * 1024
GROUP = 4
VMEM = pl.BlockSpec(memory_space=pltpu.VMEM)
SMEM = pl.BlockSpec(memory_space=pltpu.SMEM)


def split(values):
    high = values.astype(jnp.bfloat16)
    low = (values - high.astype(jnp.float32)).astype(jnp.bfloat16)
    return high, low


def lanes_dot(left, right):
    return lax.dot_general(
        left, right, (((1,), (1,)), ((), ())), preferred_element_type=jnp.float32
    )


def plain_dot(left, right):
    return lax.dot_general(
        left, right, (((1,), (0,)), ((), ())), preferred_element_type=jnp.float32
    )


def three_products(dot, left, right):
    left_high, left_low = left
    right_high, right_low = right
    rows = left_high.shape[0]
    both = dot(jnp.concatenate([left_high, left_low], 0), right_high)
    return both[:rows] + both[rows:] + dot(left_high, right_low)


def stacked(high, low):
    return jnp.concatenate([high, low], 0)


def call(kernel, name, out_shape, operands, flops, in_specs=None, scratch=()):
    size = sum(a.size * a.dtype.itemsize for a in operands)
    size += sum(a.size * a.dtype.itemsize for a in jax.tree.leaves(out_shape))
    return pl.pallas_call(
        kernel,
        name=name,
        out_shape=out_shape,
        in_specs=in_specs or [VMEM] * len(operands),
        out_specs=jax.tree.map(lambda _: VMEM, out_shape),
        scratch_shapes=scratch,
        compiler_params=pltpu.CompilerParams(vmem_limit_bytes=VMEM_LIMIT),
        cost_estimate=pl.CostEstimate(
            flops=flops, bytes_accessed=size, transcendentals=0
        ),
    )(*operands)


def shape_of(shape, dtype=jnp.float32):
    return jax.ShapeDtypeStruct(shape, dtype)


def plan_kernel(capacities, place, pattern_one, pattern_two, row_order, col_order, info):
    blocks = row_order.shape[0]
    grid_size = pattern_one.shape[0] // blocks
    largest_one, largest_two = jnp.int32(0), jnp.int32(0)
    counts_one, counts_two = [], []
    for p in range(grid_size):

        def count(b, carry):
            return (
                carry[0] + pattern_one[b * grid_size + p],
                carry[1] + pattern_two[b * grid_size + p],
            )

        one, two = lax.fori_loop(0, blocks, count, (jnp.int32(0), jnp.int32(0)))
        counts_one.append(one)
        counts_two.append(two)
        largest_one = jnp.maximum(largest_one, one)
        largest_two = jnp.maximum(largest_two, two)
    choice = jnp.int32(0)
    for i in range(1, len(capacities)):
        fits = (largest_one <= capacities[i][0]) & (largest_two <= capacities[i][1])
        choice = jnp.where(fits, i, choice)
    info[4] = choice
    info[5] = largest_one
    for axis, order in enumerate((row_order, col_order)):
        position = place[axis]
        own_one, own_two = jnp.int32(0), jnp.int32(0)
        for p in range(grid_size):
            own_one = jnp.where(position == p, counts_one[p], own_one)
            own_two = jnp.where(position == p, counts_two[p], own_two)
        info[2 * axis] = own_one
        info[2 * axis + 1] = own_two

        def put(b, carry):
            one = pattern_one[b * grid_size + position]
            two = pattern_two[b * grid_size + position]
            slot = jnp.where(two > 0, carry[0], jnp.where(one > 0, carry[1], carry[2]))
            order[slot] = b
            return (carry[0] + two, carry[1] + one - two, carry[2] + 1 - one)

        lax.fori_loop(0, blocks, put, (jnp.int32(0), own_two, own_one))


def pack_one_kernel(cap, order, info, factor, inverse_one, inverse_two, out, out_bare):
    width = inverse_one.shape[1]
    for i in range(cap):
        block = jnp.where(i < info[0], factor[order[i]], 0.0)
        out[pl.ds(i * B, B), :] = block
        out_bare[pl.ds(i * B, B), :] = block
    out[pl.ds(cap * B, width), :] = inverse_one[...].T
    out[pl.ds(cap * B + width, width), :] = inverse_two[...].T


def pack_two_kernel(cap, order, info, factor, out):
    for i in range(cap):
        out[pl.ds(i * B, B), :] = jnp.where(i < info[1], factor[order[i]], 0.0)


def place_kernel(place, *refs):
    pieces, out = refs[:-1], refs[-1]
    share = pieces[0].shape[0]
    grid_size = len(pieces)
    for shift, piece in enumerate(pieces):
        source = lax.rem(place[0] + grid_size - shift, grid_size)
        out[pl.ds(pl.multiple_of(source * share, share), share), :] = piece[...]


def all_rows(cap, body):
    size = min(cap, GROUP)

    def turn(i, carry):
        body(pl.multiple_of(jnp.minimum(i * GROUP, cap - size) * B, B), size * B)
        return carry

    lax.fori_loop(0, pl.cdiv(cap, GROUP), turn, 0)


def joined(refs, start, size):
    return jnp.concatenate([ref[pl.ds(start, size), :] for ref in refs], 1)


def padded(cap):
    return pl.cdiv(cap, GROUP) * GROUP


def over_rows(first, last, step, body):
    whole = (last - first) // step

    def turn(i, carry):
        body(pl.multiple_of(first * B + i * (step * B), B), step * B)
        return carry

    lax.fori_loop(0, whole, turn, 0)
    rest = last - first - whole * step
    if rest:
        body((first + whole * step) * B, rest * B)


def clear_rest(out, cap):
    if out.shape[1] > cap * B:
        out[:, cap * B:] = jnp.zeros((out.shape[0], out.shape[1] - cap * B), out.dtype)


def solve_rows(inverse, refs, out, cap):
    width = out.shape[0] // 2
    clear_rest(out, cap)

    def body(start, size):
        rows = split(joined(refs, start, size))
        high, low = split(three_products(lanes_dot, inverse, rows))
        out[:width, pl.ds(start, size)] = high
        out[width:, pl.ds(start, size)] = low

    all_rows(cap, body)


def solve_one_kernel(cap, grid_size, place, *refs):
    gathered, parents = refs[:grid_size], refs[grid_size:2 * grid_size]
    (
        out, out_lag, out_inverse_one, out_inverse_two, out_lead, out_diag_one, out_diag_two,
        out_parent, weight_high, weight_low,
    ) = refs[2 * grid_size:]
    share, width = out_lead.shape
    row, col = place[0], place[1]
    first, second = cap * B, cap * B + width
    inverse = split(joined(gathered, first, width))
    out_inverse_one[...] = stacked(*inverse)
    inverse_two = split(joined(gathered, second, width))
    out_inverse_two[...] = stacked(*inverse_two)
    solved_parent = split(
        three_products(lanes_dot, inverse_two, split(joined(parents, 0, width)))
    )
    row_start = pl.multiple_of(row * share, share)
    col_start = pl.multiple_of(col * share, share)
    out_parent[...] = three_products(
        lanes_dot, inverse_two, split(joined(parents, row_start, share))
    )
    for k in range(grid_size):
        piece = split(gathered[k][pl.ds(first, width), :])
        high, low = split(three_products(plain_dot, solved_parent, piece))
        weight_high[:, k * share:(k + 1) * share] = high
        weight_low[:, k * share:(k + 1) * share] = low
    weight = (weight_high[...], weight_low[...])
    for start, diag in ((first, out_diag_one), (second, out_diag_two)):
        inv_row = split(joined(gathered, start + row_start, share))
        inv_col = split(joined(gathered, start + col_start, share))
        diag[...] = three_products(lanes_dot, inv_col, inv_row)
        if start == first:
            out_lead[...] = three_products(lanes_dot, inv_row, weight)

    clear_rest(out, cap)

    def body(start, size):
        rows = split(joined(gathered, start, size))
        high, low = split(three_products(lanes_dot, inverse, rows))
        out[:width, pl.ds(start, size)] = high
        out[width:, pl.ds(start, size)] = low
        out_lag[:, pl.ds(start, size)] = three_products(lanes_dot, weight, rows)

    all_rows(cap, body)


def solve_far_kernel(cap, inverse, *refs):
    gathered, out = refs[:-1], refs[-1]
    width = out.shape[0] // 2
    solve_rows((inverse[:width, :], inverse[width:, :]), gathered, out, cap)


def solve_two_kernel(cap_one, cap_two, inverse, lag, *refs):
    gathered, (out_full, out_root) = refs[:-2], refs[-2:]
    width = lag.shape[0]
    halves = (inverse[:width, :], inverse[width:, :])
    clear_rest(out_full, cap_one)
    clear_rest(out_root, cap_two)

    def both(start, size):
        own = three_products(lanes_dot, halves, split(joined(gathered, start, size)))
        high, low = split(own)
        out_root[:width, pl.ds(start, size)] = high
        out_root[width:, pl.ds(start, size)] = low
        high, low = split(own - lag[:, pl.ds(start, size)])
        out_full[:width, pl.ds(start, size)] = high
        out_full[width:, pl.ds(start, size)] = low

    all_rows(cap_two, both)
    if cap_one > cap_two:
        high, low = split(-lag[:, cap_two * B:])
        out_full[:width, cap_two * B:cap_one * B] = high
        out_full[width:, cap_two * B:cap_one * B] = low


def load_blocks(covs, blocks, order, lead, high, low):
    for j in range(GROUP):
        column = order[jnp.minimum(lead + j, blocks - 1)]
        for part, cov in enumerate(covs):
            piece = cov[pl.ds(column, B, stride=blocks), :]
            piece_high, piece_low = split(piece)
            high[part * B:(part + 1) * B, j * B:(j + 1) * B] = piece_high
            low[part * B:(part + 1) * B, j * B:(j + 1) * B] = piece_low


def groups_of(count):
    return (count + GROUP - 1) // GROUP


def image_kernel(blocks, order_in, order_out, counts, solved, *refs):
    covs, (out, high, low) = refs[:GROUP], refs[GROUP:]
    step = pl.program_id(0)
    width = out.shape[0]
    out[...] = jnp.zeros_like(out)

    @pl.when(GROUP * step < counts[1])
    def _():
        def turn(i, carry):
            load_blocks(covs, blocks, order_in, i * GROUP, high, low)
            span = pl.ds(pl.multiple_of(i * GROUP * B, GROUP * B), GROUP * B)
            both = lanes_dot(solved[:, span], high[...])
            more = lanes_dot(solved[:width, span], low[...])
            out[...] += both[:width] + both[width:] + more
            return carry

        lax.fori_loop(0, groups_of(counts[0]), turn, 0)


def image(covariance, blocks, solved, order_in, order_out, counts, cap_out, name):
    width = solved.shape[0] // 2
    cap_in = solved.shape[1] // B
    group = GROUP

    def place(which):
        def index_map(i, order_in, order_out, counts):
            last = jnp.maximum(counts[1] - 1, 0)
            return (order_out[jnp.minimum(group * i + which, last)], 0)

        return pl.BlockSpec((B * blocks, B), index_map)

    grid_spec = pltpu.PrefetchScalarGridSpec(
        num_scalar_prefetch=3,
        grid=(pl.cdiv(cap_out, group),),
        in_specs=[
            pl.BlockSpec(solved.shape, lambda i, *_: (0, 0), pipeline_mode=pl.Buffered(1)),
            *[place(which) for which in range(group)],
        ],
        out_specs=pl.BlockSpec((width, group * B), lambda i, *_: (0, i)),
        scratch_shapes=[
            pltpu.VMEM((group * B, group * B), jnp.bfloat16),
            pltpu.VMEM((group * B, group * B), jnp.bfloat16),
        ],
    )
    return pl.pallas_call(
        functools.partial(image_kernel, blocks),
        name=name,
        grid_spec=grid_spec,
        out_shape=shape_of((width, cap_out * B)),
        compiler_params=pltpu.CompilerParams(vmem_limit_bytes=VMEM_LIMIT),
        cost_estimate=pl.CostEstimate(
            flops=6 * width * cap_in * B * cap_out * B,
            bytes_accessed=(4 * blocks * B + 8 * width) * cap_out * B,
            transcendentals=0,
        ),
    )(order_in, order_out, counts, solved, *[covariance] * group)


def mirror_kernel(blocks, lead_in, order_in, order_out, counts, solved, *refs):
    covs, (out, high, low) = refs[:GROUP], refs[-3:]
    step = pl.program_id(0)
    width = out.shape[0]

    @pl.when(step == 0)
    def _():
        out[...] = refs[GROUP][...] if len(refs) > GROUP + 3 else jnp.zeros_like(out)

    @pl.when(lead_in + GROUP * step < counts[0])
    def _():
        def turn(i, carry):
            load_blocks(covs, blocks, order_out, i * GROUP, high, low)
            span = pl.ds(pl.multiple_of(i * GROUP * B, GROUP * B), GROUP * B)
            both = plain_dot(solved[...], high[...])
            more = plain_dot(solved[:width, :], low[...])
            out[:, span] += both[:width] + both[width:] + more
            return carry

        lax.fori_loop(0, groups_of(counts[1]), turn, 0)


def mirror_image(covariance, blocks, solved, order_in, order_out, counts, cap, lead_in, before, name):
    width = solved.shape[0] // 2
    group = GROUP
    cap = padded(cap)
    steps = solved.shape[1] // (group * B)

    def place(which):
        def index_map(i, order_in, order_out, counts):
            last = jnp.maximum(counts[0] - 1, 0)
            return (order_in[jnp.minimum(lead_in + group * i + which, last)], 0)

        return pl.BlockSpec((B * blocks, B), index_map)

    whole = pl.BlockSpec((width, cap * B), lambda i, *_: (0, 0), pipeline_mode=pl.Buffered(1))
    extra = () if before is None else (before,)
    grid_spec = pltpu.PrefetchScalarGridSpec(
        num_scalar_prefetch=3,
        grid=(steps,),
        in_specs=[
            pl.BlockSpec((2 * width, group * B), lambda i, *_: (0, i)),
            *[place(which) for which in range(group)],
            *[whole for _ in extra],
        ],
        out_specs=pl.BlockSpec((width, cap * B), lambda i, *_: (0, 0)),
        scratch_shapes=[pltpu.VMEM((group * B, group * B), jnp.bfloat16)] * 2,
    )
    return pl.pallas_call(
        functools.partial(mirror_kernel, blocks, lead_in),
        name=name,
        grid_spec=grid_spec,
        out_shape=shape_of((width, cap * B)),
        compiler_params=pltpu.CompilerParams(vmem_limit_bytes=VMEM_LIMIT),
        cost_estimate=pl.CostEstimate(
            flops=6 * width * cap * B * solved.shape[1],
            bytes_accessed=4 * (steps * group * B * blocks + 2 * width * cap) * B,
            transcendentals=0,
        ),
    )(order_in, order_out, counts, solved, *[covariance] * group, *extra)


def unpack_kernel(blocks, which, order, counts, *refs):
    parts, out = refs[:-1], refs[-1]
    share = parts[0].shape[0]
    out[...] = jnp.zeros_like(out)
    for i in range(min(blocks, parts[0].shape[1] // B)):

        @pl.when(i < counts[which])
        def _():
            span = slice(i * B, (i + 1) * B)
            block = -parts[0][:, span]
            for part in parts[1:]:
                block = block - part[:, span]
            out[pl.ds(order[i], share, stride=blocks), :] = block


def unpack(parts, order, counts, which, blocks, name):
    return call(
        functools.partial(unpack_kernel, blocks, which),
        name,
        shape_of((parts[0].shape[0] * blocks, B)),
        (order, counts, *parts),
        1,
        in_specs=[SMEM, SMEM] + [VMEM] * len(parts),
    )


def parent_out_kernel(place, lead, *refs):
    pieces, out = refs[:-1], refs[-1]
    share = pieces[0].shape[0]
    for k in range(len(pieces)):
        for j, piece in enumerate(pieces):

            @pl.when(place[1] ^ j == k)
            def _():
                span = slice(k * share, (k + 1) * share)
                out[:, span] = piece[...] - lead[:, span]


def gram_rows(image_rows, solved, total):
    width = solved.shape[0] // 2

    def body(start, size):
        span = pl.ds(start, size)
        rows = split(image_rows[:, span])
        total[...] += three_products(
            lanes_dot, rows, (solved[:width, span], solved[width:, span])
        )

    over_rows(0, image_rows.shape[1] // B, GROUP, body)


def gram_one_kernel(image_rows, solved_one, solved_two, out, total):
    grid_size, _, share = out.shape
    for half, solved in enumerate((solved_one, solved_two)):
        total[...] = jnp.zeros_like(total)
        gram_rows(image_rows, solved, total)
        for k in range(grid_size):
            out[k, half * share:(half + 1) * share, :] = total[:, k * share:(k + 1) * share]


def gram_two_kernel(image_rows, solved_root, image_parent, parent, out, total):
    grid_size, share, _ = out.shape
    total[...] = three_products(lanes_dot, split(image_parent[...].T), split(parent[...]))
    gram_rows(image_rows, solved_root, total)
    for k in range(grid_size):
        out[k, :, :] = total[:, k * share:(k + 1) * share]


def swap_grid(block, grid_size):
    pairs = [
        (r * grid_size + c, c * grid_size + r) for r in range(grid_size) for c in range(grid_size)
    ]
    return lax.ppermute(block, ("row", "col"), pairs)


def scatter_pieces(pieces, grid_size, position):
    return [
        lax.dynamic_index_in_dim(pieces, lax.rem(position + shift, grid_size), 0, keepdims=False)
        for shift in range(grid_size)
    ]


def scatter_sum(pieces, grid_size):
    total = pieces[0]
    for shift in range(1, grid_size):
        total = total + lax.ppermute(
            pieces[shift], "row", [(i, (i + shift) % grid_size) for i in range(grid_size)]
        )
    return total


def mixed_pieces(pieces, grid_size, position):
    return [
        lax.dynamic_index_in_dim(pieces, lax.rem(position + j, grid_size), 0, keepdims=False)
        for j in range(grid_size)
    ]


def mixed_sum(pieces, grid_size):
    total = None
    for j, piece in enumerate(pieces):
        pairs = [
            (r * grid_size + c, c * grid_size + (r + j) % grid_size)
            for r in range(grid_size)
            for c in range(grid_size)
        ]
        piece = lax.ppermute(piece, ("row", "col"), pairs)
        total = piece if total is None else total + piece
    return total


def gather_rows(block, grid_size):
    return [block] + [
        lax.ppermute(block, "row", [(i, (i + shift) % grid_size) for i in range(grid_size)])
        for shift in range(1, grid_size)
    ]


def plane_chips(grid_size):
    return 2 if grid_size == 4 else grid_size


def core_sum(partial, cap, grid_size, col):
    if grid_size != 4:
        return lax.psum_scatter(partial[:, :cap * B], "col", scatter_dimension=0, tiled=True)
    share = partial.shape[0] // grid_size
    core = col % 2
    pieces = partial.reshape(2, 2, share, partial.shape[1])
    part = (2, 1, share, cap * B)
    away = lax.dynamic_slice(pieces, (0, 1 - core, 0, 0), part)[:, 0]
    stay = lax.dynamic_slice(pieces, (0, core, 0, 0), part)[:, 0]
    return (stay + flip(away, "col", 1, grid_size)).reshape(2 * share, cap * B)


def chip_sum(partial, grid_size, col):
    if grid_size != 4:
        return partial
    chip = col // 2
    pieces = partial.reshape(2, -1, partial.shape[1])
    away = lax.dynamic_index_in_dim(pieces, 1 - chip, 0, keepdims=False)
    stay = lax.dynamic_index_in_dim(pieces, chip, 0, keepdims=False)
    return stay + flip(away, "col", 2, grid_size)


def flip(block, axis, bit, grid_size):
    return lax.ppermute(block, axis, [(i, i ^ bit) for i in range(grid_size)])


def gather_cols(block, grid_size, between=None):
    if grid_size != 4:
        gathered = lax.all_gather(block, "col")
        position = lax.axis_index("col")
        return [
            lax.dynamic_index_in_dim(gathered, position ^ j, 0, keepdims=False)
            for j in range(grid_size)
        ], between
    far = flip(block, "col", 2, grid_size)
    near = flip(block, "col", 1, grid_size)
    if between is not None:
        far, between = lax.optimization_barrier((far, between))
    return [block, near, far, flip(far, "col", 1, grid_size)], between


def exchange(gathered, start, size, grid_size, col):
    share = gathered.shape[2]
    pieces = [
        lax.dynamic_slice(gathered, (col ^ j, start, 0), (1, size, share))[0]
        for j in range(grid_size)
    ]
    return [flip(piece, "col", j, grid_size) if j else piece for j, piece in enumerate(pieces)]


def run(
    cap_one, cap_two, covariance, row_order, col_order, info, place, factor_one, inverse_one,
    factor_parent, factor_root, inverse_two,
):
    grid_size = lax.axis_size("row")
    row = lax.axis_index("row")
    col = lax.axis_index("col")
    share, width = inverse_one.shape
    blocks = row_order.shape[0]
    col_info = info[2:4]

    half = padded(pl.cdiv(cap_one, 2))
    parts = [(lead_in, min(half, cap_one - lead_in)) for lead_in in range(0, cap_one, half)]
    packed_one, bare_one = call(
        functools.partial(pack_one_kernel, cap_one),
        "pack_one",
        (
            shape_of((cap_one * B + 2 * width, share)),
            shape_of((cap_one * B, share)),
        ),
        (row_order, info, factor_one.reshape(blocks, B, share), inverse_one, inverse_two),
        1,
        in_specs=[SMEM, SMEM, VMEM, VMEM, VMEM],
    )
    every_row = lax.all_gather(bare_one, "row")
    parent_rows = call(
        place_kernel,
        "parent_rows",
        shape_of((width, share)),
        (place, *gather_rows(factor_parent, grid_size)),
        1,
        in_specs=[SMEM] + [VMEM] * grid_size,
    )
    packed_two = call(
        functools.partial(pack_two_kernel, cap_two),
        "pack_two",
        shape_of((cap_two * B, share)),
        (row_order, info, factor_root.reshape(blocks, B, share)),
        1,
        in_specs=[SMEM] * 2 + [VMEM],
    )
    gathered_one, (parent_rows, packed_two) = gather_cols(
        packed_one, grid_size, (parent_rows, packed_two)
    )
    gathered_parent, packed_two = gather_cols(parent_rows, grid_size, packed_two)

    solved_one, lag, lead_inverse, inverse_two, lead, diag_one, diag_two, parent = call(
        functools.partial(solve_one_kernel, cap_one, grid_size),
        "solve_one",
        (
            shape_of((2 * width, padded(cap_one) * B), jnp.bfloat16),
            shape_of((width, cap_one * B)),
            shape_of((2 * width, width), jnp.bfloat16),
            shape_of((2 * width, width), jnp.bfloat16),
            shape_of((share, width)),
            shape_of((share, share)),
            shape_of((share, share)),
            shape_of((width, share)),
        ),
        (place, *gathered_one, *gathered_parent),
        12 * width * width * cap_one * B,
        in_specs=[SMEM] + [VMEM] * (2 * grid_size),
        scratch=[pltpu.VMEM((width, width), jnp.bfloat16)] * 2,
    )
    gathered_two, lag = gather_cols(packed_two, grid_size, lag)
    solved_two, solved_root = call(
        functools.partial(solve_two_kernel, cap_one, cap_two),
        "solve_two",
        (
            shape_of((2 * width, padded(cap_one) * B), jnp.bfloat16),
            shape_of((2 * width, padded(cap_two) * B), jnp.bfloat16),
        ),
        (inverse_two, lag, *gathered_two),
        6 * width * width * cap_two * B,
    )
    counts = jnp.stack([info[0], info[3]])
    image_two = image(covariance, blocks, solved_two, row_order, col_order, counts, cap_two, "image_two")
    every_row, image_two = lax.optimization_barrier((every_row, image_two))
    image_two = lax.psum_scatter(image_two, "row", scatter_dimension=0, tiled=True)

    def level_one(every_row, lead_inverse):
        counts = jnp.stack([info[2], info[0]])
        rows_one = None
        for lead_in, size in parts:
            far_rows = exchange(every_row, lead_in * B, size * B, grid_size, col)
            solved_far = call(
                functools.partial(solve_far_kernel, size),
                f"solve_far_{lead_in}",
                shape_of((2 * width, padded(size) * B), jnp.bfloat16),
                (lead_inverse, *far_rows),
                6 * width * width * size * B,
            )
            rows_one = mirror_image(
                covariance, blocks, solved_far, col_order, row_order, counts, cap_one, lead_in,
                rows_one, f"image_one_{lead_in}",
            )
        return core_sum(rows_one, cap_one, grid_size, col)

    def empty(every_row, lead_inverse):
        return jnp.zeros((width // plane_chips(grid_size), cap_one * B), jnp.float32)

    rows_one = lax.cond(info[5] > 0, level_one, empty, every_row, lead_inverse)
    rows_one, image_two = lax.optimization_barrier((rows_one, image_two))
    rows_one = chip_sum(rows_one, grid_size, col)
    rows_two = swap_grid(image_two, grid_size)
    rows_one, rows_two = lax.optimization_barrier((rows_one, rows_two))
    gram_one = call(
        gram_one_kernel,
        "gram_one",
        shape_of((grid_size, 2 * share, share)),
        (rows_one, solved_one, solved_two),
        12 * share * width * cap_one * B,
        scratch=[pltpu.VMEM((share, width), jnp.float32)],
    )
    mixed = mixed_sum(mixed_pieces(gram_one[:, share:], grid_size, row), grid_size)
    own_lead = lax.dynamic_slice_in_dim(lead, col * share, share, 1)
    gram_two = call(
        gram_two_kernel,
        "gram_two",
        shape_of((grid_size, share, share)),
        (rows_two, solved_root, own_lead - mixed, parent),
        6 * share * width * cap_two * B,
        scratch=[pltpu.VMEM((share, width), jnp.float32)],
    )
    grams = jnp.concatenate([gram_one[:, :share], gram_two], 1)
    pieces, mixed = lax.optimization_barrier((scatter_pieces(grams, grid_size, row), mixed))
    grams = scatter_sum(pieces, grid_size)
    mixed_parts = gather_cols(mixed, grid_size)[0]
    mixed_parts, grams, rows_one = lax.optimization_barrier((mixed_parts, grams, rows_one))
    image_one = swap_grid(rows_one, grid_size)
    block_one = grams[:share] + diag_one
    block_two = grams[share:] + diag_two
    parent_out = call(
        parent_out_kernel,
        "parent_out",
        shape_of((share, width)),
        (place, lead, *mixed_parts),
        1,
        in_specs=[SMEM] + [VMEM] * (1 + grid_size),
    )
    cross_two = unpack([image_two], col_order, col_info, 1, blocks, "cross_two")
    cross_one = unpack([image_one], col_order, col_info, 0, blocks, "cross_one")
    return cross_one, block_one, parent_out, cross_two, block_two


def capacities_of(blocks):
    parts = ((0.85, 0.65), (0.75, 0.6)) if blocks >= 16 else ()
    return [(blocks, blocks)] + [(round(one * blocks), round(two * blocks)) for one, two in parts]


def local(
    root_covariance, factor_one, inverse_one, pattern_one, factor_parent, factor_root, inverse_two,
    pattern_two,
):
    blocks = root_covariance.shape[3]
    capacities = capacities_of(blocks)
    place = jnp.stack([lax.axis_index("row"), lax.axis_index("col")]).astype(jnp.int32)
    row_order, col_order, info = pl.pallas_call(
        functools.partial(plan_kernel, capacities),
        name="plan",
        out_shape=(
            shape_of((blocks,), jnp.int32), shape_of((blocks,), jnp.int32), shape_of((6,), jnp.int32)
        ),
        in_specs=[SMEM] * 3,
        out_specs=(SMEM,) * 3,
    )(place, pattern_one, pattern_two)
    operands = (
        root_covariance.reshape(-1, B), row_order, col_order, info, place, factor_one, inverse_one,
        factor_parent, factor_root, inverse_two,
    )
    branches = [functools.partial(run, one, two) for one, two in capacities]
    if len(branches) == 1:
        results = branches[0](*operands)
    else:
        results = lax.switch(info[4], branches, *operands)
    cross_one, block_one, parent_out, cross_two, block_two = results
    cross_one = cross_one.reshape(-1, blocks, 1, B)
    cross_two = cross_two.reshape(-1, blocks, 1, B)
    return cross_one, block_one, parent_out, cross_two, block_two


def solution(mesh):
    return jax.shard_map(
        local,
        mesh=mesh,
        in_specs=(
            P("grp", "col", None, None, "row", None),
            P("grp", "row", None, "col"),
            P(("grp", "col"), None),
            P("grp"),
            P(("grp", "row"), "col"),
            P("grp", "row", None, "col"),
            P(("grp", "col"), None),
            P("grp"),
        ),
        out_specs=(
            P(("grp", "row"), None, "col", None),
            P(("grp", "col"), "row"),
            P(("grp", "row"), None),
            P(("grp", "row"), None, "col", None),
            P(("grp", "col"), "row"),
        ),
        check_vma=False,
    )
```

```python
import functools

import jax
import jax.numpy as jnp
from jax import lax
from jax.experimental import pallas as pl
from jax.experimental.pallas import tpu as pltpu
from jax.sharding import PartitionSpec as P

B = 128
VMEM_LIMIT = 52 * 1024 * 1024
GROUP = 4
VMEM = pl.BlockSpec(memory_space=pltpu.VMEM)
SMEM = pl.BlockSpec(memory_space=pltpu.SMEM)


def split(values):
    high = values.astype(jnp.bfloat16)
    low = (values - high.astype(jnp.float32)).astype(jnp.bfloat16)
    return high, low


def lanes_dot(left, right):
    return lax.dot_general(
        left, right, (((1,), (1,)), ((), ())), preferred_element_type=jnp.float32
    )


def plain_dot(left, right):
    return lax.dot_general(
        left, right, (((1,), (0,)), ((), ())), preferred_element_type=jnp.float32
    )


def three_products(dot, left, right):
    left_high, left_low = left
    right_high, right_low = right
    rows = left_high.shape[0]
    both = dot(jnp.concatenate([left_high, left_low], 0), right_high)
    return both[:rows] + both[rows:] + dot(left_high, right_low)


def stacked(high, low):
    return jnp.concatenate([high, low], 0)


def call(kernel, name, out_shape, operands, flops, in_specs=None, scratch=()):
    size = sum(a.size * a.dtype.itemsize for a in operands)
    size += sum(a.size * a.dtype.itemsize for a in jax.tree.leaves(out_shape))
    return pl.pallas_call(
        kernel,
        name=name,
        out_shape=out_shape,
        in_specs=in_specs or [VMEM] * len(operands),
        out_specs=jax.tree.map(lambda _: VMEM, out_shape),
        scratch_shapes=scratch,
        compiler_params=pltpu.CompilerParams(vmem_limit_bytes=VMEM_LIMIT),
        cost_estimate=pl.CostEstimate(
            flops=flops, bytes_accessed=size, transcendentals=0
        ),
    )(*operands)


def shape_of(shape, dtype=jnp.float32):
    return jax.ShapeDtypeStruct(shape, dtype)


def plan_kernel(capacities, place, pattern_one, pattern_two, row_order, col_order, info):
    blocks = row_order.shape[0]
    grid_size = pattern_one.shape[0] // blocks
    largest_one, largest_two = jnp.int32(0), jnp.int32(0)
    counts_one, counts_two = [], []
    for p in range(grid_size):

        def count(b, carry):
            return (
                carry[0] + pattern_one[b * grid_size + p],
                carry[1] + pattern_two[b * grid_size + p],
            )

        one, two = lax.fori_loop(0, blocks, count, (jnp.int32(0), jnp.int32(0)))
        counts_one.append(one)
        counts_two.append(two)
        largest_one = jnp.maximum(largest_one, one)
        largest_two = jnp.maximum(largest_two, two)
    choice = jnp.int32(0)
    for i in range(1, len(capacities)):
        fits = (largest_one <= capacities[i][0]) & (largest_two <= capacities[i][1])
        choice = jnp.where(fits, i, choice)
    info[4] = choice
    info[5] = largest_one
    for axis, order in enumerate((row_order, col_order)):
        position = place[axis]
        own_one, own_two = jnp.int32(0), jnp.int32(0)
        for p in range(grid_size):
            own_one = jnp.where(position == p, counts_one[p], own_one)
            own_two = jnp.where(position == p, counts_two[p], own_two)
        info[2 * axis] = own_one
        info[2 * axis + 1] = own_two

        def put(b, carry):
            one = pattern_one[b * grid_size + position]
            two = pattern_two[b * grid_size + position]
            slot = jnp.where(two > 0, carry[0], jnp.where(one > 0, carry[1], carry[2]))
            order[slot] = b
            return (carry[0] + two, carry[1] + one - two, carry[2] + 1 - one)

        lax.fori_loop(0, blocks, put, (jnp.int32(0), own_two, own_one))


def pack_one_kernel(cap, order, info, factor, inverse_one, inverse_two, out, out_bare):
    width = inverse_one.shape[1]
    for i in range(cap):
        block = jnp.where(i < info[0], factor[order[i]], 0.0)
        out[pl.ds(i * B, B), :] = block
        out_bare[pl.ds(i * B, B), :] = block
    out[pl.ds(cap * B, width), :] = inverse_one[...].T
    out[pl.ds(cap * B + width, width), :] = inverse_two[...].T


def pack_two_kernel(cap, order, info, factor, out):
    for i in range(cap):
        out[pl.ds(i * B, B), :] = jnp.where(i < info[1], factor[order[i]], 0.0)


def place_kernel(place, *refs):
    pieces, out = refs[:-1], refs[-1]
    share = pieces[0].shape[0]
    grid_size = len(pieces)
    for shift, piece in enumerate(pieces):
        source = lax.rem(place[0] + grid_size - shift, grid_size)
        out[pl.ds(pl.multiple_of(source * share, share), share), :] = piece[...]


def all_rows(cap, body):
    size = min(cap, GROUP)

    def turn(i, carry):
        body(pl.multiple_of(jnp.minimum(i * GROUP, cap - size) * B, B), size * B)
        return carry

    lax.fori_loop(0, pl.cdiv(cap, GROUP), turn, 0)


def joined(refs, start, size):
    return jnp.concatenate([ref[pl.ds(start, size), :] for ref in refs], 1)


def padded(cap):
    return pl.cdiv(cap, GROUP) * GROUP


def over_rows(first, last, step, body):
    whole = (last - first) // step

    def turn(i, carry):
        body(pl.multiple_of(first * B + i * (step * B), B), step * B)
        return carry

    lax.fori_loop(0, whole, turn, 0)
    rest = last - first - whole * step
    if rest:
        body((first + whole * step) * B, rest * B)


def clear_rest(out, cap):
    if out.shape[1] > cap * B:
        out[:, cap * B:] = jnp.zeros((out.shape[0], out.shape[1] - cap * B), out.dtype)


def solve_rows(inverse, refs, out, cap):
    width = out.shape[0] // 2
    clear_rest(out, cap)

    def body(start, size):
        rows = split(joined(refs, start, size))
        high, low = split(three_products(lanes_dot, inverse, rows))
        out[:width, pl.ds(start, size)] = high
        out[width:, pl.ds(start, size)] = low

    all_rows(cap, body)


def solve_one_kernel(cap, grid_size, place, *refs):
    gathered, parents = refs[:grid_size], refs[grid_size:2 * grid_size]
    (
        out, out_lag, out_inverse_one, out_inverse_two, out_lead, out_diag_one, out_diag_two,
        out_parent, parent, solved_parent, weight,
    ) = refs[2 * grid_size:]
    share, width = out_lead.shape
    row, col = place[0], place[1]
    first, second = cap * B, cap * B + width
    part = width // 4

    def halves(ref):
        return ref[:width, :], ref[width:, :]

    def by_parts(target, part_of):
        def turn(i, carry):
            start = pl.multiple_of(i * part, part)
            high, low = split(part_of(start))
            target[pl.ds(start, part), :] = high
            target[pl.ds(width + start, part), :] = low
            return carry

        lax.fori_loop(0, 4, turn, 0)

    def product_of(dot, left, right):
        def part_of(start):
            pair = left[pl.ds(start, part), :], left[pl.ds(width + start, part), :]
            return three_products(dot, pair, halves(right))

        return part_of

    by_parts(out_inverse_one, lambda start: joined(gathered, first + start, part))
    by_parts(out_inverse_two, lambda start: joined(gathered, second + start, part))
    by_parts(parent, lambda start: joined(parents, start, part))
    by_parts(solved_parent, product_of(lanes_dot, out_inverse_two, parent))
    by_parts(weight, product_of(plain_dot, solved_parent, out_inverse_one))
    row_start = pl.multiple_of(row * share, share)
    col_start = pl.multiple_of(col * share, share)
    out_parent[...] = three_products(
        lanes_dot, halves(out_inverse_two), split(joined(parents, row_start, share))
    )
    for start, diag in ((first, out_diag_one), (second, out_diag_two)):
        inv_row = split(joined(gathered, start + row_start, share))
        inv_col = split(joined(gathered, start + col_start, share))
        diag[...] = three_products(lanes_dot, inv_col, inv_row)
        if start == first:
            out_lead[...] = three_products(lanes_dot, inv_row, halves(weight))

    clear_rest(out, cap)

    def body(start, size):
        rows = split(joined(gathered, start, size))
        high, low = split(three_products(lanes_dot, halves(out_inverse_one), rows))
        out[:width, pl.ds(start, size)] = high
        out[width:, pl.ds(start, size)] = low
        out_lag[:, pl.ds(start, size)] = three_products(lanes_dot, halves(weight), rows)

    all_rows(cap, body)


def solve_far_kernel(cap, inverse, *refs):
    gathered, out = refs[:-1], refs[-1]
    width = out.shape[0] // 2
    solve_rows((inverse[:width, :], inverse[width:, :]), gathered, out, cap)


def solve_two_kernel(cap_one, cap_two, inverse, lag, *refs):
    gathered, (out_full, out_root) = refs[:-2], refs[-2:]
    width = lag.shape[0]
    halves = (inverse[:width, :], inverse[width:, :])
    clear_rest(out_full, cap_one)
    clear_rest(out_root, cap_two)

    def both(start, size):
        own = three_products(lanes_dot, halves, split(joined(gathered, start, size)))
        high, low = split(own)
        out_root[:width, pl.ds(start, size)] = high
        out_root[width:, pl.ds(start, size)] = low
        high, low = split(own - lag[:, pl.ds(start, size)])
        out_full[:width, pl.ds(start, size)] = high
        out_full[width:, pl.ds(start, size)] = low

    all_rows(cap_two, both)
    if cap_one > cap_two:
        high, low = split(-lag[:, cap_two * B:])
        out_full[:width, cap_two * B:cap_one * B] = high
        out_full[width:, cap_two * B:cap_one * B] = low


def load_blocks(covs, blocks, order, lead, high, low):
    for j in range(GROUP):
        column = order[jnp.minimum(lead + j, blocks - 1)]
        for part, cov in enumerate(covs):
            piece = cov[pl.ds(column, B, stride=blocks), :]
            piece_high, piece_low = split(piece)
            high[part * B:(part + 1) * B, j * B:(j + 1) * B] = piece_high
            low[part * B:(part + 1) * B, j * B:(j + 1) * B] = piece_low


def groups_of(count):
    return (count + GROUP - 1) // GROUP


def image_kernel(blocks, order_in, order_out, counts, solved, *refs):
    covs, (out, high, low) = refs[:GROUP], refs[GROUP:]
    step = pl.program_id(0)
    width = out.shape[0]
    out[...] = jnp.zeros_like(out)

    @pl.when(GROUP * step < counts[1])
    def _():
        def turn(i, carry):
            load_blocks(covs, blocks, order_in, i * GROUP, high, low)
            span = pl.ds(pl.multiple_of(i * GROUP * B, GROUP * B), GROUP * B)
            both = lanes_dot(solved[:, span], high[...])
            more = lanes_dot(solved[:width, span], low[...])
            out[...] += both[:width] + both[width:] + more
            return carry

        lax.fori_loop(0, groups_of(counts[0]), turn, 0)


def image(covariance, blocks, solved, order_in, order_out, counts, cap_out, name):
    width = solved.shape[0] // 2
    cap_in = solved.shape[1] // B
    group = GROUP

    def place(which):
        def index_map(i, order_in, order_out, counts):
            last = jnp.maximum(counts[1] - 1, 0)
            return (order_out[jnp.minimum(group * i + which, last)], 0)

        return pl.BlockSpec((B * blocks, B), index_map)

    grid_spec = pltpu.PrefetchScalarGridSpec(
        num_scalar_prefetch=3,
        grid=(pl.cdiv(cap_out, group),),
        in_specs=[
            pl.BlockSpec(solved.shape, lambda i, *_: (0, 0), pipeline_mode=pl.Buffered(1)),
            *[place(which) for which in range(group)],
        ],
        out_specs=pl.BlockSpec((width, group * B), lambda i, *_: (0, i)),
        scratch_shapes=[
            pltpu.VMEM((group * B, group * B), jnp.bfloat16),
            pltpu.VMEM((group * B, group * B), jnp.bfloat16),
        ],
    )
    return pl.pallas_call(
        functools.partial(image_kernel, blocks),
        name=name,
        grid_spec=grid_spec,
        out_shape=shape_of((width, cap_out * B)),
        compiler_params=pltpu.CompilerParams(vmem_limit_bytes=VMEM_LIMIT),
        cost_estimate=pl.CostEstimate(
            flops=6 * width * cap_in * B * cap_out * B,
            bytes_accessed=(4 * blocks * B + 8 * width) * cap_out * B,
            transcendentals=0,
        ),
    )(order_in, order_out, counts, solved, *[covariance] * group)


def mirror_kernel(blocks, lead_in, order_in, order_out, counts, solved, *refs):
    covs, (out, high, low) = refs[:GROUP], refs[-3:]
    step = pl.program_id(0)
    width = out.shape[0]

    @pl.when(step == 0)
    def _():
        out[...] = refs[GROUP][...] if len(refs) > GROUP + 3 else jnp.zeros_like(out)

    @pl.when(lead_in + GROUP * step < counts[0])
    def _():
        def turn(i, carry):
            load_blocks(covs, blocks, order_out, i * GROUP, high, low)
            span = pl.ds(pl.multiple_of(i * GROUP * B, GROUP * B), GROUP * B)
            both = plain_dot(solved[...], high[...])
            more = plain_dot(solved[:width, :], low[...])
            out[:, span] += both[:width] + both[width:] + more
            return carry

        lax.fori_loop(0, groups_of(counts[1]), turn, 0)


def mirror_image(covariance, blocks, solved, order_in, order_out, counts, cap, lead_in, before, name):
    width = solved.shape[0] // 2
    group = GROUP
    cap = padded(cap)
    steps = solved.shape[1] // (group * B)

    def place(which):
        def index_map(i, order_in, order_out, counts):
            last = jnp.maximum(counts[0] - 1, 0)
            return (order_in[jnp.minimum(lead_in + group * i + which, last)], 0)

        return pl.BlockSpec((B * blocks, B), index_map)

    whole = pl.BlockSpec((width, cap * B), lambda i, *_: (0, 0), pipeline_mode=pl.Buffered(1))
    extra = () if before is None else (before,)
    grid_spec = pltpu.PrefetchScalarGridSpec(
        num_scalar_prefetch=3,
        grid=(steps,),
        in_specs=[
            pl.BlockSpec((2 * width, group * B), lambda i, *_: (0, i)),
            *[place(which) for which in range(group)],
            *[whole for _ in extra],
        ],
        out_specs=pl.BlockSpec((width, cap * B), lambda i, *_: (0, 0)),
        scratch_shapes=[pltpu.VMEM((group * B, group * B), jnp.bfloat16)] * 2,
    )
    return pl.pallas_call(
        functools.partial(mirror_kernel, blocks, lead_in),
        name=name,
        grid_spec=grid_spec,
        out_shape=shape_of((width, cap * B)),
        compiler_params=pltpu.CompilerParams(vmem_limit_bytes=VMEM_LIMIT),
        cost_estimate=pl.CostEstimate(
            flops=6 * width * cap * B * solved.shape[1],
            bytes_accessed=4 * (steps * group * B * blocks + 2 * width * cap) * B,
            transcendentals=0,
        ),
    )(order_in, order_out, counts, solved, *[covariance] * group, *extra)


def unpack_kernel(blocks, which, order, counts, *refs):
    parts, out = refs[:-1], refs[-1]
    share = parts[0].shape[0]
    out[...] = jnp.zeros_like(out)
    for i in range(min(blocks, parts[0].shape[1] // B)):

        @pl.when(i < counts[which])
        def _():
            span = slice(i * B, (i + 1) * B)
            block = -parts[0][:, span]
            for part in parts[1:]:
                block = block - part[:, span]
            out[pl.ds(order[i], share, stride=blocks), :] = block


def unpack(parts, order, counts, which, blocks, name):
    return call(
        functools.partial(unpack_kernel, blocks, which),
        name,
        shape_of((parts[0].shape[0] * blocks, B)),
        (order, counts, *parts),
        1,
        in_specs=[SMEM, SMEM] + [VMEM] * len(parts),
    )


def parent_out_kernel(place, lead, *refs):
    pieces, out = refs[:-1], refs[-1]
    share = pieces[0].shape[0]
    for k in range(len(pieces)):
        for j, piece in enumerate(pieces):

            @pl.when(place[1] ^ j == k)
            def _():
                span = slice(k * share, (k + 1) * share)
                out[:, span] = piece[...] - lead[:, span]


def gram_rows(image_rows, solved, total):
    width = solved.shape[0] // 2

    def body(start, size):
        span = pl.ds(start, size)
        rows = split(image_rows[:, span])
        total[...] += three_products(
            lanes_dot, rows, (solved[:width, span], solved[width:, span])
        )

    over_rows(0, image_rows.shape[1] // B, GROUP, body)


def gram_one_kernel(image_rows, solved_one, solved_two, out, total):
    grid_size, _, share = out.shape
    for half, solved in enumerate((solved_one, solved_two)):
        total[...] = jnp.zeros_like(total)
        gram_rows(image_rows, solved, total)
        for k in range(grid_size):
            out[k, half * share:(half + 1) * share, :] = total[:, k * share:(k + 1) * share]


def gram_two_kernel(image_rows, solved_root, image_parent, parent, out, total):
    grid_size, share, _ = out.shape
    total[...] = three_products(lanes_dot, split(image_parent[...].T), split(parent[...]))
    gram_rows(image_rows, solved_root, total)
    for k in range(grid_size):
        out[k, :, :] = total[:, k * share:(k + 1) * share]


def swap_grid(block, grid_size):
    pairs = [
        (r * grid_size + c, c * grid_size + r) for r in range(grid_size) for c in range(grid_size)
    ]
    return lax.ppermute(block, ("row", "col"), pairs)


def scatter_pieces(pieces, grid_size, position):
    return [
        lax.dynamic_index_in_dim(pieces, lax.rem(position + shift, grid_size), 0, keepdims=False)
        for shift in range(grid_size)
    ]


def scatter_sum(pieces, grid_size):
    total = pieces[0]
    for shift in range(1, grid_size):
        total = total + lax.ppermute(
            pieces[shift], "row", [(i, (i + shift) % grid_size) for i in range(grid_size)]
        )
    return total


def mixed_pieces(pieces, grid_size, position):
    return [
        lax.dynamic_index_in_dim(pieces, lax.rem(position + j, grid_size), 0, keepdims=False)
        for j in range(grid_size)
    ]


def mixed_sum(pieces, grid_size):
    total = None
    for j, piece in enumerate(pieces):
        pairs = [
            (r * grid_size + c, c * grid_size + (r + j) % grid_size)
            for r in range(grid_size)
            for c in range(grid_size)
        ]
        piece = lax.ppermute(piece, ("row", "col"), pairs)
        total = piece if total is None else total + piece
    return total


def gather_rows(block, grid_size):
    return [block] + [
        lax.ppermute(block, "row", [(i, (i + shift) % grid_size) for i in range(grid_size)])
        for shift in range(1, grid_size)
    ]


def plane_chips(grid_size):
    return 2 if grid_size == 4 else grid_size


def core_sum(partial, cap, grid_size, col):
    if grid_size != 4:
        return lax.psum_scatter(partial[:, :cap * B], "col", scatter_dimension=0, tiled=True)
    share = partial.shape[0] // grid_size
    core = col % 2
    pieces = partial.reshape(2, 2, share, partial.shape[1])
    part = (2, 1, share, cap * B)
    away = lax.dynamic_slice(pieces, (0, 1 - core, 0, 0), part)[:, 0]
    stay = lax.dynamic_slice(pieces, (0, core, 0, 0), part)[:, 0]
    return (stay + flip(away, "col", 1, grid_size)).reshape(2 * share, cap * B)


def chip_sum(partial, grid_size, col):
    if grid_size != 4:
        return partial
    chip = col // 2
    pieces = partial.reshape(2, -1, partial.shape[1])
    away = lax.dynamic_index_in_dim(pieces, 1 - chip, 0, keepdims=False)
    stay = lax.dynamic_index_in_dim(pieces, chip, 0, keepdims=False)
    return stay + flip(away, "col", 2, grid_size)


def flip(block, axis, bit, grid_size):
    return lax.ppermute(block, axis, [(i, i ^ bit) for i in range(grid_size)])


def gather_cols(block, grid_size, between=None):
    if grid_size != 4:
        gathered = lax.all_gather(block, "col")
        position = lax.axis_index("col")
        return [
            lax.dynamic_index_in_dim(gathered, position ^ j, 0, keepdims=False)
            for j in range(grid_size)
        ], between
    far = flip(block, "col", 2, grid_size)
    near = flip(block, "col", 1, grid_size)
    if between is not None:
        far, between = lax.optimization_barrier((far, between))
    return [block, near, far, flip(far, "col", 1, grid_size)], between


def exchange(gathered, start, size, grid_size, col):
    share = gathered.shape[2]
    pieces = [
        lax.dynamic_slice(gathered, (col ^ j, start, 0), (1, size, share))[0]
        for j in range(grid_size)
    ]
    return [flip(piece, "col", j, grid_size) if j else piece for j, piece in enumerate(pieces)]


def run(
    cap_one, cap_two, covariance, row_order, col_order, info, place, factor_one, inverse_one,
    factor_parent, factor_root, inverse_two,
):
    grid_size = lax.axis_size("row")
    row = lax.axis_index("row")
    col = lax.axis_index("col")
    share, width = inverse_one.shape
    blocks = row_order.shape[0]
    col_info = info[2:4]

    half = padded(pl.cdiv(cap_one, 2)) if 5 * cap_one <= 4 * blocks else cap_one
    parts = [(lead_in, min(half, cap_one - lead_in)) for lead_in in range(0, cap_one, half)]
    packed_one, bare_one = call(
        functools.partial(pack_one_kernel, cap_one),
        "pack_one",
        (
            shape_of((cap_one * B + 2 * width, share)),
            shape_of((cap_one * B, share)),
        ),
        (row_order, info, factor_one.reshape(blocks, B, share), inverse_one, inverse_two),
        1,
        in_specs=[SMEM, SMEM, VMEM, VMEM, VMEM],
    )
    every_row = lax.all_gather(bare_one, "row")
    parent_rows = call(
        place_kernel,
        "parent_rows",
        shape_of((width, share)),
        (place, *gather_rows(factor_parent, grid_size)),
        1,
        in_specs=[SMEM] + [VMEM] * grid_size,
    )
    packed_two = call(
        functools.partial(pack_two_kernel, cap_two),
        "pack_two",
        shape_of((cap_two * B, share)),
        (row_order, info, factor_root.reshape(blocks, B, share)),
        1,
        in_specs=[SMEM] * 2 + [VMEM],
    )
    gathered_one, (parent_rows, packed_two) = gather_cols(
        packed_one, grid_size, (parent_rows, packed_two)
    )
    gathered_parent, packed_two = gather_cols(parent_rows, grid_size, packed_two)

    solved_one, lag, lead_inverse, inverse_two, lead, diag_one, diag_two, parent = call(
        functools.partial(solve_one_kernel, cap_one, grid_size),
        "solve_one",
        (
            shape_of((2 * width, padded(cap_one) * B), jnp.bfloat16),
            shape_of((width, cap_one * B)),
            shape_of((2 * width, width), jnp.bfloat16),
            shape_of((2 * width, width), jnp.bfloat16),
            shape_of((share, width)),
            shape_of((share, share)),
            shape_of((share, share)),
            shape_of((width, share)),
        ),
        (place, *gathered_one, *gathered_parent),
        12 * width * width * cap_one * B,
        in_specs=[SMEM] + [VMEM] * (2 * grid_size),
        scratch=[pltpu.VMEM((2 * width, width), jnp.bfloat16)] * 3,
    )
    gathered_two, lag = gather_cols(packed_two, grid_size, lag)
    solved_two, solved_root = call(
        functools.partial(solve_two_kernel, cap_one, cap_two),
        "solve_two",
        (
            shape_of((2 * width, padded(cap_one) * B), jnp.bfloat16),
            shape_of((2 * width, padded(cap_two) * B), jnp.bfloat16),
        ),
        (inverse_two, lag, *gathered_two),
        6 * width * width * cap_two * B,
    )
    counts = jnp.stack([info[0], info[3]])
    image_two = image(covariance, blocks, solved_two, row_order, col_order, counts, cap_two, "image_two")
    every_row, image_two = lax.optimization_barrier((every_row, image_two))
    image_two = lax.psum_scatter(image_two, "row", scatter_dimension=0, tiled=True)

    def level_one(every_row, lead_inverse):
        counts = jnp.stack([info[2], info[0]])
        rows_one, far_rows = None, None
        for lead_in, size in parts:
            if far_rows is not None:
                every_row, far_rows = lax.optimization_barrier((every_row, far_rows))
            far_rows = exchange(every_row, lead_in * B, size * B, grid_size, col)
            solved_far = call(
                functools.partial(solve_far_kernel, size),
                f"solve_far_{lead_in}",
                shape_of((2 * width, padded(size) * B), jnp.bfloat16),
                (lead_inverse, *far_rows),
                6 * width * width * size * B,
            )
            rows_one = mirror_image(
                covariance, blocks, solved_far, col_order, row_order, counts, cap_one, lead_in,
                rows_one, f"image_one_{lead_in}",
            )
        return core_sum(rows_one, cap_one, grid_size, col)

    def empty(every_row, lead_inverse):
        return jnp.zeros((width // plane_chips(grid_size), cap_one * B), jnp.float32)

    rows_one = lax.cond(info[5] > 0, level_one, empty, every_row, lead_inverse)
    rows_one, image_two = lax.optimization_barrier((rows_one, image_two))
    rows_one = chip_sum(rows_one, grid_size, col)
    rows_two = swap_grid(image_two, grid_size)
    rows_one, rows_two = lax.optimization_barrier((rows_one, rows_two))
    gram_one = call(
        gram_one_kernel,
        "gram_one",
        shape_of((grid_size, 2 * share, share)),
        (rows_one, solved_one, solved_two),
        12 * share * width * cap_one * B,
        scratch=[pltpu.VMEM((share, width), jnp.float32)],
    )
    mixed = mixed_sum(mixed_pieces(gram_one[:, share:], grid_size, row), grid_size)
    own_lead = lax.dynamic_slice_in_dim(lead, col * share, share, 1)
    gram_two = call(
        gram_two_kernel,
        "gram_two",
        shape_of((grid_size, share, share)),
        (rows_two, solved_root, own_lead - mixed, parent),
        6 * share * width * cap_two * B,
        scratch=[pltpu.VMEM((share, width), jnp.float32)],
    )
    grams = jnp.concatenate([gram_one[:, :share], gram_two], 1)
    pieces, mixed = lax.optimization_barrier((scatter_pieces(grams, grid_size, row), mixed))
    grams = scatter_sum(pieces, grid_size)
    mixed_parts = gather_cols(mixed, grid_size)[0]
    mixed_parts, grams, rows_one = lax.optimization_barrier((mixed_parts, grams, rows_one))
    image_one = swap_grid(rows_one, grid_size)
    block_one = grams[:share] + diag_one
    block_two = grams[share:] + diag_two
    parent_out = call(
        parent_out_kernel,
        "parent_out",
        shape_of((share, width)),
        (place, lead, *mixed_parts),
        1,
        in_specs=[SMEM] + [VMEM] * (1 + grid_size),
    )
    cross_two = unpack([image_two], col_order, col_info, 1, blocks, "cross_two")
    cross_one = unpack([image_one], col_order, col_info, 0, blocks, "cross_one")
    return cross_one, block_one, parent_out, cross_two, block_two


def capacities_of(blocks):
    parts = ((0.85, 0.65), (0.75, 0.6)) if blocks >= 16 else ()
    return [(blocks, blocks)] + [(round(one * blocks), round(two * blocks)) for one, two in parts]


def local(
    root_covariance, factor_one, inverse_one, pattern_one, factor_parent, factor_root, inverse_two,
    pattern_two,
):
    blocks = root_covariance.shape[3]
    capacities = capacities_of(blocks)
    place = jnp.stack([lax.axis_index("row"), lax.axis_index("col")]).astype(jnp.int32)
    row_order, col_order, info = pl.pallas_call(
        functools.partial(plan_kernel, capacities),
        name="plan",
        out_shape=(
            shape_of((blocks,), jnp.int32), shape_of((blocks,), jnp.int32), shape_of((6,), jnp.int32)
        ),
        in_specs=[SMEM] * 3,
        out_specs=(SMEM,) * 3,
    )(place, pattern_one, pattern_two)
    operands = (
        root_covariance.reshape(-1, B), row_order, col_order, info, place, factor_one, inverse_one,
        factor_parent, factor_root, inverse_two,
    )
    branches = [functools.partial(run, one, two) for one, two in capacities]
    if len(branches) == 1:
        results = branches[0](*operands)
    else:
        results = lax.switch(info[4], branches, *operands)
    cross_one, block_one, parent_out, cross_two, block_two = results
    cross_one = cross_one.reshape(-1, blocks, 1, B)
    cross_two = cross_two.reshape(-1, blocks, 1, B)
    return cross_one, block_one, parent_out, cross_two, block_two


def solution(mesh):
    return jax.shard_map(
        local,
        mesh=mesh,
        in_specs=(
            P("grp", "col", None, None, "row", None),
            P("grp", "row", None, "col"),
            P(("grp", "col"), None),
            P("grp"),
            P(("grp", "row"), "col"),
            P("grp", "row", None, "col"),
            P(("grp", "col"), None),
            P("grp"),
        ),
        out_specs=(
            P(("grp", "row"), None, "col", None),
            P(("grp", "col"), "row"),
            P(("grp", "row"), None),
            P(("grp", "row"), None, "col", None),
            P(("grp", "col"), "row"),
        ),
        check_vma=False,
    )
```

```python
import functools

import jax
import jax.numpy as jnp
from jax import lax
from jax.experimental import pallas as pl
from jax.experimental.pallas import tpu as pltpu
from jax.sharding import PartitionSpec as P

B = 128
VMEM_LIMIT = 52 * 1024 * 1024
GROUP = 4
VMEM = pl.BlockSpec(memory_space=pltpu.VMEM)
SMEM = pl.BlockSpec(memory_space=pltpu.SMEM)


def split(values):
    high = values.astype(jnp.bfloat16)
    low = (values - high.astype(jnp.float32)).astype(jnp.bfloat16)
    return high, low


def lanes_dot(left, right):
    return lax.dot_general(
        left, right, (((1,), (1,)), ((), ())), preferred_element_type=jnp.float32
    )


def plain_dot(left, right):
    return lax.dot_general(
        left, right, (((1,), (0,)), ((), ())), preferred_element_type=jnp.float32
    )


def three_products(dot, left, right):
    left_high, left_low = left
    right_high, right_low = right
    rows = left_high.shape[0]
    both = dot(jnp.concatenate([left_high, left_low], 0), right_high)
    return both[:rows] + both[rows:] + dot(left_high, right_low)


def stacked(high, low):
    return jnp.concatenate([high, low], 0)


def call(kernel, name, out_shape, operands, flops, in_specs=None, scratch=()):
    size = sum(a.size * a.dtype.itemsize for a in operands)
    size += sum(a.size * a.dtype.itemsize for a in jax.tree.leaves(out_shape))
    return pl.pallas_call(
        kernel,
        name=name,
        out_shape=out_shape,
        in_specs=in_specs or [VMEM] * len(operands),
        out_specs=jax.tree.map(lambda _: VMEM, out_shape),
        scratch_shapes=scratch,
        compiler_params=pltpu.CompilerParams(vmem_limit_bytes=VMEM_LIMIT),
        cost_estimate=pl.CostEstimate(
            flops=flops, bytes_accessed=size, transcendentals=0
        ),
    )(*operands)


def shape_of(shape, dtype=jnp.float32):
    return jax.ShapeDtypeStruct(shape, dtype)


def plan_kernel(capacities, place, pattern_one, pattern_two, row_order, col_order, info):
    blocks = row_order.shape[0]
    grid_size = pattern_one.shape[0] // blocks
    largest_one, largest_two = jnp.int32(0), jnp.int32(0)
    counts_one, counts_two = [], []
    for p in range(grid_size):

        def count(b, carry):
            return (
                carry[0] + pattern_one[b * grid_size + p],
                carry[1] + pattern_two[b * grid_size + p],
            )

        one, two = lax.fori_loop(0, blocks, count, (jnp.int32(0), jnp.int32(0)))
        counts_one.append(one)
        counts_two.append(two)
        largest_one = jnp.maximum(largest_one, one)
        largest_two = jnp.maximum(largest_two, two)
    choice = jnp.int32(0)
    for i in range(1, len(capacities)):
        fits = (largest_one <= capacities[i][0]) & (largest_two <= capacities[i][1])
        choice = jnp.where(fits, i, choice)
    info[4] = choice
    info[5] = largest_one
    for axis, order in enumerate((row_order, col_order)):
        position = place[axis]
        own_one, own_two = jnp.int32(0), jnp.int32(0)
        for p in range(grid_size):
            own_one = jnp.where(position == p, counts_one[p], own_one)
            own_two = jnp.where(position == p, counts_two[p], own_two)
        info[2 * axis] = own_one
        info[2 * axis + 1] = own_two

        def put(b, carry):
            one = pattern_one[b * grid_size + position]
            two = pattern_two[b * grid_size + position]
            slot = jnp.where(two > 0, carry[0], jnp.where(one > 0, carry[1], carry[2]))
            order[slot] = b
            return (carry[0] + two, carry[1] + one - two, carry[2] + 1 - one)

        lax.fori_loop(0, blocks, put, (jnp.int32(0), own_two, own_one))


def pack_one_kernel(cap, order, info, factor, inverse_one, inverse_two, out, out_bare):
    width = inverse_one.shape[1]
    for i in range(cap):
        block = jnp.where(i < info[0], factor[order[i]], 0.0)
        out[pl.ds(i * B, B), :] = block
        out_bare[pl.ds(i * B, B), :] = block
    out[pl.ds(cap * B, width), :] = inverse_one[...].T
    out[pl.ds(cap * B + width, width), :] = inverse_two[...].T


def pack_two_kernel(cap, order, info, factor, out):
    for i in range(cap):
        out[pl.ds(i * B, B), :] = jnp.where(i < info[1], factor[order[i]], 0.0)


def place_kernel(place, *refs):
    pieces, out = refs[:-1], refs[-1]
    share = pieces[0].shape[0]
    grid_size = len(pieces)
    for shift, piece in enumerate(pieces):
        source = lax.rem(place[0] + grid_size - shift, grid_size)
        out[pl.ds(pl.multiple_of(source * share, share), share), :] = piece[...]


def all_rows(cap, body):
    size = min(cap, GROUP)

    def turn(i, carry):
        body(pl.multiple_of(jnp.minimum(i * GROUP, cap - size) * B, B), size * B)
        return carry

    lax.fori_loop(0, pl.cdiv(cap, GROUP), turn, 0)


def joined(refs, start, size):
    return jnp.concatenate([ref[pl.ds(start, size), :] for ref in refs], 1)


def padded(cap):
    return pl.cdiv(cap, GROUP) * GROUP


def over_rows(first, last, step, body):
    whole = (last - first) // step

    def turn(i, carry):
        body(pl.multiple_of(first * B + i * (step * B), B), step * B)
        return carry

    lax.fori_loop(0, whole, turn, 0)
    rest = last - first - whole * step
    if rest:
        body((first + whole * step) * B, rest * B)


def clear_rest(out, cap):
    if out.shape[1] > cap * B:
        out[:, cap * B:] = jnp.zeros((out.shape[0], out.shape[1] - cap * B), out.dtype)


def solve_rows(inverse, refs, out, cap):
    width = out.shape[0] // 2
    clear_rest(out, cap)

    def body(start, size):
        rows = split(joined(refs, start, size))
        high, low = split(three_products(lanes_dot, inverse, rows))
        out[:width, pl.ds(start, size)] = high
        out[width:, pl.ds(start, size)] = low

    all_rows(cap, body)


def solve_one_kernel(cap, grid_size, place, *refs):
    gathered, parents = refs[:grid_size], refs[grid_size:2 * grid_size]
    (
        out, out_lag, out_inverse_one, out_inverse_two, out_lead, out_diag_one, out_diag_two,
        out_parent, parent, solved_parent, weight,
    ) = refs[2 * grid_size:]
    share, width = out_lead.shape
    row, col = place[0], place[1]
    first, second = cap * B, cap * B + width
    part = width // 4

    def halves(ref):
        return ref[:width, :], ref[width:, :]

    def by_parts(target, part_of):
        def turn(i, carry):
            start = pl.multiple_of(i * part, part)
            high, low = split(part_of(start))
            target[pl.ds(start, part), :] = high
            target[pl.ds(width + start, part), :] = low
            return carry

        lax.fori_loop(0, 4, turn, 0)

    def product_of(dot, left, right):
        def part_of(start):
            pair = left[pl.ds(start, part), :], left[pl.ds(width + start, part), :]
            return three_products(dot, pair, halves(right))

        return part_of

    by_parts(out_inverse_one, lambda start: joined(gathered, first + start, part))
    by_parts(out_inverse_two, lambda start: joined(gathered, second + start, part))
    by_parts(parent, lambda start: joined(parents, start, part))
    by_parts(solved_parent, product_of(lanes_dot, out_inverse_two, parent))
    by_parts(weight, product_of(plain_dot, solved_parent, out_inverse_one))
    row_start = pl.multiple_of(row * share, share)
    col_start = pl.multiple_of(col * share, share)
    out_parent[...] = three_products(
        lanes_dot, halves(out_inverse_two), split(joined(parents, row_start, share))
    )
    for start, diag in ((first, out_diag_one), (second, out_diag_two)):
        inv_row = split(joined(gathered, start + row_start, share))
        inv_col = split(joined(gathered, start + col_start, share))
        diag[...] = three_products(lanes_dot, inv_col, inv_row)
        if start == first:
            out_lead[...] = three_products(lanes_dot, inv_row, halves(weight))

    clear_rest(out, cap)

    def body(start, size):
        rows = split(joined(gathered, start, size))
        high, low = split(three_products(lanes_dot, halves(out_inverse_one), rows))
        out[:width, pl.ds(start, size)] = high
        out[width:, pl.ds(start, size)] = low
        out_lag[:, pl.ds(start, size)] = three_products(lanes_dot, halves(weight), rows)

    all_rows(cap, body)


def solve_far_kernel(cap, inverse, *refs):
    gathered, out = refs[:-1], refs[-1]
    width = out.shape[0] // 2
    solve_rows((inverse[:width, :], inverse[width:, :]), gathered, out, cap)


def solve_two_kernel(cap_one, cap_two, inverse, lag, *refs):
    gathered, (out_full, out_root) = refs[:-2], refs[-2:]
    width = lag.shape[0]
    halves = (inverse[:width, :], inverse[width:, :])
    clear_rest(out_full, cap_one)
    clear_rest(out_root, cap_two)

    def both(start, size):
        own = three_products(lanes_dot, halves, split(joined(gathered, start, size)))
        high, low = split(own)
        out_root[:width, pl.ds(start, size)] = high
        out_root[width:, pl.ds(start, size)] = low
        high, low = split(own - lag[:, pl.ds(start, size)])
        out_full[:width, pl.ds(start, size)] = high
        out_full[width:, pl.ds(start, size)] = low

    all_rows(cap_two, both)
    if cap_one > cap_two:
        high, low = split(-lag[:, cap_two * B:])
        out_full[:width, cap_two * B:cap_one * B] = high
        out_full[width:, cap_two * B:cap_one * B] = low


def load_blocks(covs, blocks, order, lead, high, low):
    for j in range(GROUP):
        column = order[jnp.minimum(lead + j, blocks - 1)]
        for part, cov in enumerate(covs):
            piece = cov[pl.ds(column, B, stride=blocks), :]
            piece_high, piece_low = split(piece)
            high[part * B:(part + 1) * B, j * B:(j + 1) * B] = piece_high
            low[part * B:(part + 1) * B, j * B:(j + 1) * B] = piece_low


def groups_of(count):
    return (count + GROUP - 1) // GROUP


def image_kernel(blocks, order_in, order_out, counts, solved, *refs):
    covs, (out, high, low) = refs[:GROUP], refs[GROUP:]
    step = pl.program_id(0)
    width = out.shape[0]
    out[...] = jnp.zeros_like(out)

    @pl.when(GROUP * step < counts[1])
    def _():
        def turn(i, carry):
            load_blocks(covs, blocks, order_in, i * GROUP, high, low)
            span = pl.ds(pl.multiple_of(i * GROUP * B, GROUP * B), GROUP * B)
            both = lanes_dot(solved[:, span], high[...])
            more = lanes_dot(solved[:width, span], low[...])
            out[...] += both[:width] + both[width:] + more
            return carry

        lax.fori_loop(0, groups_of(counts[0]), turn, 0)


def image(covariance, blocks, solved, order_in, order_out, counts, cap_out, name):
    width = solved.shape[0] // 2
    cap_in = solved.shape[1] // B
    group = GROUP

    def place(which):
        def index_map(i, order_in, order_out, counts):
            last = jnp.maximum(counts[1] - 1, 0)
            return (order_out[jnp.minimum(group * i + which, last)], 0)

        return pl.BlockSpec((B * blocks, B), index_map)

    grid_spec = pltpu.PrefetchScalarGridSpec(
        num_scalar_prefetch=3,
        grid=(pl.cdiv(cap_out, group),),
        in_specs=[
            pl.BlockSpec(solved.shape, lambda i, *_: (0, 0), pipeline_mode=pl.Buffered(1)),
            *[place(which) for which in range(group)],
        ],
        out_specs=pl.BlockSpec((width, group * B), lambda i, *_: (0, i)),
        scratch_shapes=[
            pltpu.VMEM((group * B, group * B), jnp.bfloat16),
            pltpu.VMEM((group * B, group * B), jnp.bfloat16),
        ],
    )
    return pl.pallas_call(
        functools.partial(image_kernel, blocks),
        name=name,
        grid_spec=grid_spec,
        out_shape=shape_of((width, cap_out * B)),
        compiler_params=pltpu.CompilerParams(vmem_limit_bytes=VMEM_LIMIT),
        cost_estimate=pl.CostEstimate(
            flops=6 * width * cap_in * B * cap_out * B,
            bytes_accessed=(4 * blocks * B + 8 * width) * cap_out * B,
            transcendentals=0,
        ),
    )(order_in, order_out, counts, solved, *[covariance] * group)


def mirror_kernel(blocks, lead_in, order_in, order_out, counts, solved, *refs):
    covs, (out, high, low) = refs[:GROUP], refs[-3:]
    step = pl.program_id(0)
    width = out.shape[0]

    @pl.when(step == 0)
    def _():
        out[...] = refs[GROUP][...] if len(refs) > GROUP + 3 else jnp.zeros_like(out)

    @pl.when(lead_in + GROUP * step < counts[0])
    def _():
        def turn(i, carry):
            load_blocks(covs, blocks, order_out, i * GROUP, high, low)
            span = pl.ds(pl.multiple_of(i * GROUP * B, GROUP * B), GROUP * B)
            both = plain_dot(solved[...], high[...])
            more = plain_dot(solved[:width, :], low[...])
            out[:, span] += both[:width] + both[width:] + more
            return carry

        lax.fori_loop(0, groups_of(counts[1]), turn, 0)


def mirror_image(covariance, blocks, solved, order_in, order_out, counts, cap, lead_in, before, name):
    width = solved.shape[0] // 2
    group = GROUP
    cap = padded(cap)
    steps = solved.shape[1] // (group * B)

    def place(which):
        def index_map(i, order_in, order_out, counts):
            last = jnp.maximum(counts[0] - 1, 0)
            return (order_in[jnp.minimum(lead_in + group * i + which, last)], 0)

        return pl.BlockSpec((B * blocks, B), index_map)

    whole = pl.BlockSpec((width, cap * B), lambda i, *_: (0, 0), pipeline_mode=pl.Buffered(1))
    extra = () if before is None else (before,)
    grid_spec = pltpu.PrefetchScalarGridSpec(
        num_scalar_prefetch=3,
        grid=(steps,),
        in_specs=[
            pl.BlockSpec((2 * width, group * B), lambda i, *_: (0, i)),
            *[place(which) for which in range(group)],
            *[whole for _ in extra],
        ],
        out_specs=pl.BlockSpec((width, cap * B), lambda i, *_: (0, 0)),
        scratch_shapes=[pltpu.VMEM((group * B, group * B), jnp.bfloat16)] * 2,
    )
    return pl.pallas_call(
        functools.partial(mirror_kernel, blocks, lead_in),
        name=name,
        grid_spec=grid_spec,
        out_shape=shape_of((width, cap * B)),
        compiler_params=pltpu.CompilerParams(vmem_limit_bytes=VMEM_LIMIT),
        cost_estimate=pl.CostEstimate(
            flops=6 * width * cap * B * solved.shape[1],
            bytes_accessed=4 * (steps * group * B * blocks + 2 * width * cap) * B,
            transcendentals=0,
        ),
    )(order_in, order_out, counts, solved, *[covariance] * group, *extra)


def unpack_kernel(blocks, which, order, counts, *refs):
    parts, out = refs[:-1], refs[-1]
    share = parts[0].shape[0]
    out[...] = jnp.zeros_like(out)
    for i in range(min(blocks, parts[0].shape[1] // B)):

        @pl.when(i < counts[which])
        def _():
            span = slice(i * B, (i + 1) * B)
            block = -parts[0][:, span]
            for part in parts[1:]:
                block = block - part[:, span]
            out[pl.ds(order[i], share, stride=blocks), :] = block


def unpack(parts, order, counts, which, blocks, name):
    return call(
        functools.partial(unpack_kernel, blocks, which),
        name,
        shape_of((parts[0].shape[0] * blocks, B)),
        (order, counts, *parts),
        1,
        in_specs=[SMEM, SMEM] + [VMEM] * len(parts),
    )


def parent_out_kernel(place, lead, *refs):
    pieces, out = refs[:-1], refs[-1]
    share = pieces[0].shape[0]
    for k in range(len(pieces)):
        for j, piece in enumerate(pieces):

            @pl.when(place[1] ^ j == k)
            def _():
                span = slice(k * share, (k + 1) * share)
                out[:, span] = piece[...] - lead[:, span]


def gram_rows(image_rows, solved, total):
    width = solved.shape[0] // 2

    def body(start, size):
        span = pl.ds(start, size)
        rows = split(image_rows[:, span])
        total[...] += three_products(
            lanes_dot, rows, (solved[:width, span], solved[width:, span])
        )

    over_rows(0, image_rows.shape[1] // B, GROUP, body)


def gram_one_kernel(image_rows, solved_one, solved_two, out, total):
    grid_size, _, share = out.shape
    for half, solved in enumerate((solved_one, solved_two)):
        total[...] = jnp.zeros_like(total)
        gram_rows(image_rows, solved, total)
        for k in range(grid_size):
            out[k, half * share:(half + 1) * share, :] = total[:, k * share:(k + 1) * share]


def gram_two_kernel(image_rows, solved_root, image_parent, parent, out, total):
    grid_size, share, _ = out.shape
    total[...] = three_products(lanes_dot, split(image_parent[...].T), split(parent[...]))
    gram_rows(image_rows, solved_root, total)
    for k in range(grid_size):
        out[k, :, :] = total[:, k * share:(k + 1) * share]


def swap_grid(block, grid_size):
    pairs = [
        (r * grid_size + c, c * grid_size + r) for r in range(grid_size) for c in range(grid_size)
    ]
    return lax.ppermute(block, ("row", "col"), pairs)


def scatter_pieces(pieces, grid_size, position):
    return [
        lax.dynamic_index_in_dim(pieces, lax.rem(position + shift, grid_size), 0, keepdims=False)
        for shift in range(grid_size)
    ]


def scatter_sum(pieces, grid_size):
    total = pieces[0]
    for shift in range(1, grid_size):
        total = total + lax.ppermute(
            pieces[shift], "row", [(i, (i + shift) % grid_size) for i in range(grid_size)]
        )
    return total


def mixed_pieces(pieces, grid_size, position):
    return [
        lax.dynamic_index_in_dim(pieces, lax.rem(position + j, grid_size), 0, keepdims=False)
        for j in range(grid_size)
    ]


def mixed_sum(pieces, grid_size):
    total = None
    for j, piece in enumerate(pieces):
        pairs = [
            (r * grid_size + c, c * grid_size + (r + j) % grid_size)
            for r in range(grid_size)
            for c in range(grid_size)
        ]
        piece = lax.ppermute(piece, ("row", "col"), pairs)
        total = piece if total is None else total + piece
    return total


def gather_rows(block, grid_size):
    return [block] + [
        lax.ppermute(block, "row", [(i, (i + shift) % grid_size) for i in range(grid_size)])
        for shift in range(1, grid_size)
    ]


def plane_chips(grid_size):
    return 2 if grid_size == 4 else grid_size


def core_sum(partial, cap, grid_size, col):
    if grid_size != 4:
        return lax.psum_scatter(partial[:, :cap * B], "col", scatter_dimension=0, tiled=True)
    share = partial.shape[0] // grid_size
    core = col % 2
    pieces = partial.reshape(2, 2, share, partial.shape[1])
    part = (2, 1, share, cap * B)
    away = lax.dynamic_slice(pieces, (0, 1 - core, 0, 0), part)[:, 0]
    stay = lax.dynamic_slice(pieces, (0, core, 0, 0), part)[:, 0]
    return (stay + flip(away, "col", 1, grid_size)).reshape(2 * share, cap * B)


def chip_sum(partial, grid_size, col):
    if grid_size != 4:
        return partial
    chip = col // 2
    pieces = partial.reshape(2, -1, partial.shape[1])
    away = lax.dynamic_index_in_dim(pieces, 1 - chip, 0, keepdims=False)
    stay = lax.dynamic_index_in_dim(pieces, chip, 0, keepdims=False)
    return stay + flip(away, "col", 2, grid_size)


def flip(block, axis, bit, grid_size):
    return lax.ppermute(block, axis, [(i, i ^ bit) for i in range(grid_size)])


def gather_cols(block, grid_size, between=None):
    if grid_size != 4:
        gathered = lax.all_gather(block, "col")
        position = lax.axis_index("col")
        return [
            lax.dynamic_index_in_dim(gathered, position ^ j, 0, keepdims=False)
            for j in range(grid_size)
        ], between
    far = flip(block, "col", 2, grid_size)
    near = flip(block, "col", 1, grid_size)
    if between is not None:
        far, between = lax.optimization_barrier((far, between))
    return [block, near, far, flip(far, "col", 1, grid_size)], between


def exchange(gathered, start, size, grid_size, col):
    share = gathered.shape[2]
    pieces = [
        lax.dynamic_slice(gathered, (col ^ j, start, 0), (1, size, share))[0]
        for j in range(grid_size)
    ]
    return [flip(piece, "col", j, grid_size) if j else piece for j, piece in enumerate(pieces)]


def run(
    cap_one, cap_two, covariance, row_order, col_order, info, place, factor_one, inverse_one,
    factor_parent, factor_root, inverse_two,
):
    grid_size = lax.axis_size("row")
    row = lax.axis_index("row")
    col = lax.axis_index("col")
    share, width = inverse_one.shape
    blocks = row_order.shape[0]
    col_info = info[2:4]

    half = padded(pl.cdiv(cap_one, 2)) if cap_one < blocks else cap_one
    parts = [(lead_in, min(half, cap_one - lead_in)) for lead_in in range(0, cap_one, half)]
    packed_one, bare_one = call(
        functools.partial(pack_one_kernel, cap_one),
        "pack_one",
        (
            shape_of((cap_one * B + 2 * width, share)),
            shape_of((cap_one * B, share)),
        ),
        (row_order, info, factor_one.reshape(blocks, B, share), inverse_one, inverse_two),
        1,
        in_specs=[SMEM, SMEM, VMEM, VMEM, VMEM],
    )
    every_row = lax.all_gather(bare_one, "row")
    parent_rows = call(
        place_kernel,
        "parent_rows",
        shape_of((width, share)),
        (place, *gather_rows(factor_parent, grid_size)),
        1,
        in_specs=[SMEM] + [VMEM] * grid_size,
    )
    packed_two = call(
        functools.partial(pack_two_kernel, cap_two),
        "pack_two",
        shape_of((cap_two * B, share)),
        (row_order, info, factor_root.reshape(blocks, B, share)),
        1,
        in_specs=[SMEM] * 2 + [VMEM],
    )
    gathered_one, (parent_rows, packed_two) = gather_cols(
        packed_one, grid_size, (parent_rows, packed_two)
    )
    gathered_parent, packed_two = gather_cols(parent_rows, grid_size, packed_two)

    solved_one, lag, lead_inverse, inverse_two, lead, diag_one, diag_two, parent = call(
        functools.partial(solve_one_kernel, cap_one, grid_size),
        "solve_one",
        (
            shape_of((2 * width, padded(cap_one) * B), jnp.bfloat16),
            shape_of((width, cap_one * B)),
            shape_of((2 * width, width), jnp.bfloat16),
            shape_of((2 * width, width), jnp.bfloat16),
            shape_of((share, width)),
            shape_of((share, share)),
            shape_of((share, share)),
            shape_of((width, share)),
        ),
        (place, *gathered_one, *gathered_parent),
        12 * width * width * cap_one * B,
        in_specs=[SMEM] + [VMEM] * (2 * grid_size),
        scratch=[pltpu.VMEM((2 * width, width), jnp.bfloat16)] * 3,
    )
    gathered_two, lag = gather_cols(packed_two, grid_size, lag)
    solved_two, solved_root = call(
        functools.partial(solve_two_kernel, cap_one, cap_two),
        "solve_two",
        (
            shape_of((2 * width, padded(cap_one) * B), jnp.bfloat16),
            shape_of((2 * width, padded(cap_two) * B), jnp.bfloat16),
        ),
        (inverse_two, lag, *gathered_two),
        6 * width * width * cap_two * B,
    )
    counts = jnp.stack([info[0], info[3]])
    image_two = image(covariance, blocks, solved_two, row_order, col_order, counts, cap_two, "image_two")
    every_row, image_two = lax.optimization_barrier((every_row, image_two))
    image_two = lax.psum_scatter(image_two, "row", scatter_dimension=0, tiled=True)

    counts = jnp.stack([info[2], info[0]])

    def far_product(far_rows, lead_inverse, lead_in, before):
        size = far_rows[0].shape[0] // B
        solved_far = call(
            functools.partial(solve_far_kernel, size),
            f"solve_far_{lead_in}",
            shape_of((2 * width, padded(size) * B), jnp.bfloat16),
            (lead_inverse, *far_rows),
            6 * width * width * size * B,
        )
        return mirror_image(
            covariance, blocks, solved_far, col_order, row_order, counts, cap_one, lead_in, before,
            f"image_one_{lead_in}",
        )

    def far_part(every_row, part):
        return exchange(every_row, part[0] * B, part[1] * B, grid_size, col)

    def first_part(every_row, lead_inverse):
        far_rows = far_part(every_row, parts[0])
        rest = []
        if len(parts) > 1:
            every_row, _ = lax.optimization_barrier((every_row, far_rows))
            rest = far_part(every_row, parts[1])
        return far_product(far_rows, lead_inverse, 0, None), rest

    def no_first_part(every_row, lead_inverse):
        rest = [jnp.zeros((parts[1][1] * B, share), jnp.float32)] * grid_size if len(parts) > 1 else []
        return jnp.zeros((width, padded(cap_one) * B), jnp.float32), rest

    def last_part(partial, rest, lead_inverse):
        if rest:
            partial = far_product(rest, lead_inverse, parts[1][0], partial)
        return core_sum(partial, cap_one, grid_size, col)

    def no_last_part(partial, rest, lead_inverse):
        return jnp.zeros((width // plane_chips(grid_size), cap_one * B), jnp.float32)

    some = info[5] > 0
    rows_one, rest = lax.cond(some, first_part, no_first_part, every_row, lead_inverse)
    rows_one, rest, image_two = lax.optimization_barrier((rows_one, rest, image_two))
    rows_two = swap_grid(image_two, grid_size)
    rows_one = lax.cond(some, last_part, no_last_part, rows_one, rest, lead_inverse)
    rows_one, rows_two = lax.optimization_barrier((rows_one, rows_two))
    rows_one = chip_sum(rows_one, grid_size, col)
    gram_one = call(
        gram_one_kernel,
        "gram_one",
        shape_of((grid_size, 2 * share, share)),
        (rows_one, solved_one, solved_two),
        12 * share * width * cap_one * B,
        scratch=[pltpu.VMEM((share, width), jnp.float32)],
    )
    mixed = mixed_sum(mixed_pieces(gram_one[:, share:], grid_size, row), grid_size)
    mixed, rows_one = lax.optimization_barrier((mixed, rows_one))
    image_one = swap_grid(rows_one, grid_size)
    own_lead = lax.dynamic_slice_in_dim(lead, col * share, share, 1)
    gram_two = call(
        gram_two_kernel,
        "gram_two",
        shape_of((grid_size, share, share)),
        (rows_two, solved_root, own_lead - mixed, parent),
        6 * share * width * cap_two * B,
        scratch=[pltpu.VMEM((share, width), jnp.float32)],
    )
    grams = jnp.concatenate([gram_one[:, :share], gram_two], 1)
    pieces, mixed = lax.optimization_barrier((scatter_pieces(grams, grid_size, row), mixed))
    grams = scatter_sum(pieces, grid_size)
    mixed_parts = gather_cols(mixed, grid_size)[0]
    block_one = grams[:share] + diag_one
    block_two = grams[share:] + diag_two
    parent_out = call(
        parent_out_kernel,
        "parent_out",
        shape_of((share, width)),
        (place, lead, *mixed_parts),
        1,
        in_specs=[SMEM] + [VMEM] * (1 + grid_size),
    )
    cross_two = unpack([image_two], col_order, col_info, 1, blocks, "cross_two")
    cross_one = unpack([image_one], col_order, col_info, 0, blocks, "cross_one")
    return cross_one, block_one, parent_out, cross_two, block_two


def capacities_of(blocks):
    parts = ((0.85, 0.7), (0.75, 0.6)) if blocks >= 16 else ()
    return [(blocks, blocks)] + [(round(one * blocks), round(two * blocks)) for one, two in parts]


def local(
    root_covariance, factor_one, inverse_one, pattern_one, factor_parent, factor_root, inverse_two,
    pattern_two,
):
    blocks = root_covariance.shape[3]
    capacities = capacities_of(blocks)
    place = jnp.stack([lax.axis_index("row"), lax.axis_index("col")]).astype(jnp.int32)
    row_order, col_order, info = pl.pallas_call(
        functools.partial(plan_kernel, capacities),
        name="plan",
        out_shape=(
            shape_of((blocks,), jnp.int32), shape_of((blocks,), jnp.int32), shape_of((6,), jnp.int32)
        ),
        in_specs=[SMEM] * 3,
        out_specs=(SMEM,) * 3,
    )(place, pattern_one, pattern_two)
    operands = (
        root_covariance.reshape(-1, B), row_order, col_order, info, place, factor_one, inverse_one,
        factor_parent, factor_root, inverse_two,
    )
    branches = [functools.partial(run, one, two) for one, two in capacities]
    if len(branches) == 1:
        results = branches[0](*operands)
    else:
        results = lax.switch(info[4], branches, *operands)
    cross_one, block_one, parent_out, cross_two, block_two = results
    cross_one = cross_one.reshape(-1, blocks, 1, B)
    cross_two = cross_two.reshape(-1, blocks, 1, B)
    return cross_one, block_one, parent_out, cross_two, block_two


def solution(mesh):
    return jax.shard_map(
        local,
        mesh=mesh,
        in_specs=(
            P("grp", "col", None, None, "row", None),
            P("grp", "row", None, "col"),
            P(("grp", "col"), None),
            P("grp"),
            P(("grp", "row"), "col"),
            P("grp", "row", None, "col"),
            P(("grp", "col"), None),
            P("grp"),
        ),
        out_specs=(
            P(("grp", "row"), None, "col", None),
            P(("grp", "col"), "row"),
            P(("grp", "row"), None),
            P(("grp", "row"), None, "col", None),
            P(("grp", "col"), "row"),
        ),
        check_vma=False,
    )
```

```python
import functools

import jax
import jax.numpy as jnp
from jax import lax
from jax.experimental import pallas as pl
from jax.experimental.pallas import tpu as pltpu
from jax.sharding import PartitionSpec as P

B = 128
VMEM_LIMIT = 52 * 1024 * 1024
GROUP = 4
VMEM = pl.BlockSpec(memory_space=pltpu.VMEM)
SMEM = pl.BlockSpec(memory_space=pltpu.SMEM)


def split(values):
    high = values.astype(jnp.bfloat16)
    low = (values - high.astype(jnp.float32)).astype(jnp.bfloat16)
    return high, low


def lanes_dot(left, right):
    return lax.dot_general(
        left, right, (((1,), (1,)), ((), ())), preferred_element_type=jnp.float32
    )


def plain_dot(left, right):
    return lax.dot_general(
        left, right, (((1,), (0,)), ((), ())), preferred_element_type=jnp.float32
    )


def three_products(dot, left, right):
    left_high, left_low = left
    right_high, right_low = right
    rows = left_high.shape[0]
    both = dot(jnp.concatenate([left_high, left_low], 0), right_high)
    return both[:rows] + both[rows:] + dot(left_high, right_low)


def stacked(high, low):
    return jnp.concatenate([high, low], 0)


def call(kernel, name, out_shape, operands, flops, in_specs=None, scratch=()):
    size = sum(a.size * a.dtype.itemsize for a in operands)
    size += sum(a.size * a.dtype.itemsize for a in jax.tree.leaves(out_shape))
    return pl.pallas_call(
        kernel,
        name=name,
        out_shape=out_shape,
        in_specs=in_specs or [VMEM] * len(operands),
        out_specs=jax.tree.map(lambda _: VMEM, out_shape),
        scratch_shapes=scratch,
        compiler_params=pltpu.CompilerParams(vmem_limit_bytes=VMEM_LIMIT),
        cost_estimate=pl.CostEstimate(
            flops=flops, bytes_accessed=size, transcendentals=0
        ),
    )(*operands)


def shape_of(shape, dtype=jnp.float32):
    return jax.ShapeDtypeStruct(shape, dtype)


def plan_kernel(capacities, place, pattern_one, pattern_two, row_order, col_order, info):
    blocks = row_order.shape[0]
    grid_size = pattern_one.shape[0] // blocks
    largest_one, largest_two = jnp.int32(0), jnp.int32(0)
    counts_one, counts_two = [], []
    for p in range(grid_size):

        def count(b, carry):
            return (
                carry[0] + pattern_one[b * grid_size + p],
                carry[1] + pattern_two[b * grid_size + p],
            )

        one, two = lax.fori_loop(0, blocks, count, (jnp.int32(0), jnp.int32(0)))
        counts_one.append(one)
        counts_two.append(two)
        largest_one = jnp.maximum(largest_one, one)
        largest_two = jnp.maximum(largest_two, two)
    choice = jnp.int32(0)
    for i in range(1, len(capacities)):
        fits = (largest_one <= capacities[i][0]) & (largest_two <= capacities[i][1])
        choice = jnp.where(fits, i, choice)
    info[4] = choice
    info[5] = largest_one
    for axis, order in enumerate((row_order, col_order)):
        position = place[axis]
        own_one, own_two = jnp.int32(0), jnp.int32(0)
        for p in range(grid_size):
            own_one = jnp.where(position == p, counts_one[p], own_one)
            own_two = jnp.where(position == p, counts_two[p], own_two)
        info[2 * axis] = own_one
        info[2 * axis + 1] = own_two

        def put(b, carry):
            one = pattern_one[b * grid_size + position]
            two = pattern_two[b * grid_size + position]
            slot = jnp.where(two > 0, carry[0], jnp.where(one > 0, carry[1], carry[2]))
            order[slot] = b
            return (carry[0] + two, carry[1] + one - two, carry[2] + 1 - one)

        lax.fori_loop(0, blocks, put, (jnp.int32(0), own_two, own_one))


def pack_one_kernel(cap, order, info, factor, inverse_one, inverse_two, out, out_bare):
    width = inverse_one.shape[1]
    for i in range(cap):
        block = jnp.where(i < info[0], factor[order[i]], 0.0)
        out[pl.ds(i * B, B), :] = block
        out_bare[pl.ds(i * B, B), :] = block
    out[pl.ds(cap * B, width), :] = inverse_one[...].T
    out[pl.ds(cap * B + width, width), :] = inverse_two[...].T


def pack_two_kernel(cap, order, info, factor, out):
    for i in range(cap):
        out[pl.ds(i * B, B), :] = jnp.where(i < info[1], factor[order[i]], 0.0)


def place_kernel(place, *refs):
    pieces, out = refs[:-1], refs[-1]
    share = pieces[0].shape[0]
    grid_size = len(pieces)
    for shift, piece in enumerate(pieces):
        source = lax.rem(place[0] + grid_size - shift, grid_size)
        out[pl.ds(pl.multiple_of(source * share, share), share), :] = piece[...]


def all_rows(cap, body):
    size = min(cap, GROUP)

    def turn(i, carry):
        body(pl.multiple_of(jnp.minimum(i * GROUP, cap - size) * B, B), size * B)
        return carry

    lax.fori_loop(0, pl.cdiv(cap, GROUP), turn, 0)


def joined(refs, start, size):
    return jnp.concatenate([ref[pl.ds(start, size), :] for ref in refs], 1)


def padded(cap):
    return pl.cdiv(cap, GROUP) * GROUP


def over_rows(first, last, step, body):
    whole = (last - first) // step

    def turn(i, carry):
        body(pl.multiple_of(first * B + i * (step * B), B), step * B)
        return carry

    lax.fori_loop(0, whole, turn, 0)
    rest = last - first - whole * step
    if rest:
        body((first + whole * step) * B, rest * B)


def clear_rest(out, cap):
    if out.shape[1] > cap * B:
        out[:, cap * B:] = jnp.zeros((out.shape[0], out.shape[1] - cap * B), out.dtype)


def solve_rows(inverse, refs, out, cap):
    width = out.shape[0] // 2
    clear_rest(out, cap)

    def body(start, size):
        rows = split(joined(refs, start, size))
        high, low = split(three_products(lanes_dot, inverse, rows))
        out[:width, pl.ds(start, size)] = high
        out[width:, pl.ds(start, size)] = low

    all_rows(cap, body)


def solve_one_kernel(cap, grid_size, place, *refs):
    gathered, parents = refs[:grid_size], refs[grid_size:2 * grid_size]
    (
        out, out_lag, out_inverse_one, out_inverse_two, out_lead, out_diag_one, out_diag_two,
        out_parent, parent, solved_parent, weight,
    ) = refs[2 * grid_size:]
    share, width = out_lead.shape
    row, col = place[0], place[1]
    first, second = cap * B, cap * B + width
    part = width // 4

    def halves(ref):
        return ref[:width, :], ref[width:, :]

    def by_parts(target, part_of):
        def turn(i, carry):
            start = pl.multiple_of(i * part, part)
            high, low = split(part_of(start))
            target[pl.ds(start, part), :] = high
            target[pl.ds(width + start, part), :] = low
            return carry

        lax.fori_loop(0, 4, turn, 0)

    def product_of(dot, left, right):
        def part_of(start):
            pair = left[pl.ds(start, part), :], left[pl.ds(width + start, part), :]
            return three_products(dot, pair, halves(right))

        return part_of

    by_parts(out_inverse_one, lambda start: joined(gathered, first + start, part))
    by_parts(out_inverse_two, lambda start: joined(gathered, second + start, part))
    by_parts(parent, lambda start: joined(parents, start, part))
    by_parts(solved_parent, product_of(lanes_dot, out_inverse_two, parent))
    by_parts(weight, product_of(plain_dot, solved_parent, out_inverse_one))
    row_start = pl.multiple_of(row * share, share)
    col_start = pl.multiple_of(col * share, share)
    out_parent[...] = three_products(
        lanes_dot, halves(out_inverse_two), split(joined(parents, row_start, share))
    )
    for start, diag in ((first, out_diag_one), (second, out_diag_two)):
        inv_row = split(joined(gathered, start + row_start, share))
        inv_col = split(joined(gathered, start + col_start, share))
        diag[...] = three_products(lanes_dot, inv_col, inv_row)
        if start == first:
            out_lead[...] = three_products(lanes_dot, inv_row, halves(weight))

    clear_rest(out, cap)

    def body(start, size):
        rows = split(joined(gathered, start, size))
        high, low = split(three_products(lanes_dot, halves(out_inverse_one), rows))
        out[:width, pl.ds(start, size)] = high
        out[width:, pl.ds(start, size)] = low
        out_lag[:, pl.ds(start, size)] = three_products(lanes_dot, halves(weight), rows)

    all_rows(cap, body)


def solve_far_kernel(cap, inverse, *refs):
    gathered, out = refs[:-1], refs[-1]
    width = out.shape[0] // 2
    solve_rows((inverse[:width, :], inverse[width:, :]), gathered, out, cap)


def solve_two_kernel(cap_one, cap_two, inverse, lag, *refs):
    gathered, (out_full, out_root) = refs[:-2], refs[-2:]
    width = lag.shape[0]
    halves = (inverse[:width, :], inverse[width:, :])
    clear_rest(out_full, cap_one)
    clear_rest(out_root, cap_two)

    def both(start, size):
        own = three_products(lanes_dot, halves, split(joined(gathered, start, size)))
        high, low = split(own)
        out_root[:width, pl.ds(start, size)] = high
        out_root[width:, pl.ds(start, size)] = low
        high, low = split(own - lag[:, pl.ds(start, size)])
        out_full[:width, pl.ds(start, size)] = high
        out_full[width:, pl.ds(start, size)] = low

    all_rows(cap_two, both)
    if cap_one > cap_two:
        high, low = split(-lag[:, cap_two * B:])
        out_full[:width, cap_two * B:cap_one * B] = high
        out_full[width:, cap_two * B:cap_one * B] = low


def load_blocks(covs, blocks, order, lead, high, low):
    for j in range(GROUP):
        column = order[jnp.minimum(lead + j, blocks - 1)]
        for part, cov in enumerate(covs):
            piece = cov[pl.ds(column, B, stride=blocks), :]
            piece_high, piece_low = split(piece)
            high[part * B:(part + 1) * B, j * B:(j + 1) * B] = piece_high
            low[part * B:(part + 1) * B, j * B:(j + 1) * B] = piece_low


def groups_of(count):
    return (count + GROUP - 1) // GROUP


def image_kernel(blocks, order_in, order_out, counts, solved, *refs):
    covs, (out, high, low) = refs[:GROUP], refs[GROUP:]
    step = pl.program_id(0)
    width = out.shape[0]
    out[...] = jnp.zeros_like(out)

    @pl.when(GROUP * step < counts[1])
    def _():
        def turn(i, carry):
            load_blocks(covs, blocks, order_in, i * GROUP, high, low)
            span = pl.ds(pl.multiple_of(i * GROUP * B, GROUP * B), GROUP * B)
            both = lanes_dot(solved[:, span], high[...])
            more = lanes_dot(solved[:width, span], low[...])
            out[...] += both[:width] + both[width:] + more
            return carry

        lax.fori_loop(0, groups_of(counts[0]), turn, 0)


def image(covariance, blocks, solved, order_in, order_out, counts, cap_out, name):
    width = solved.shape[0] // 2
    cap_in = solved.shape[1] // B
    group = GROUP

    def place(which):
        def index_map(i, order_in, order_out, counts):
            last = jnp.maximum(counts[1] - 1, 0)
            return (order_out[jnp.minimum(group * i + which, last)], 0)

        return pl.BlockSpec((B * blocks, B), index_map)

    grid_spec = pltpu.PrefetchScalarGridSpec(
        num_scalar_prefetch=3,
        grid=(pl.cdiv(cap_out, group),),
        in_specs=[
            pl.BlockSpec(solved.shape, lambda i, *_: (0, 0), pipeline_mode=pl.Buffered(1)),
            *[place(which) for which in range(group)],
        ],
        out_specs=pl.BlockSpec((width, group * B), lambda i, *_: (0, i)),
        scratch_shapes=[
            pltpu.VMEM((group * B, group * B), jnp.bfloat16),
            pltpu.VMEM((group * B, group * B), jnp.bfloat16),
        ],
    )
    return pl.pallas_call(
        functools.partial(image_kernel, blocks),
        name=name,
        grid_spec=grid_spec,
        out_shape=shape_of((width, cap_out * B)),
        compiler_params=pltpu.CompilerParams(vmem_limit_bytes=VMEM_LIMIT),
        cost_estimate=pl.CostEstimate(
            flops=6 * width * cap_in * B * cap_out * B,
            bytes_accessed=(4 * blocks * B + 8 * width) * cap_out * B,
            transcendentals=0,
        ),
    )(order_in, order_out, counts, solved, *[covariance] * group)


def mirror_kernel(blocks, lead_in, order_in, order_out, counts, solved, *refs):
    covs, (out, high, low) = refs[:GROUP], refs[-3:]
    step = pl.program_id(0)
    width = out.shape[0]

    @pl.when(step == 0)
    def _():
        out[...] = refs[GROUP][...] if len(refs) > GROUP + 3 else jnp.zeros_like(out)

    @pl.when(lead_in + GROUP * step < counts[0])
    def _():
        def turn(i, carry):
            load_blocks(covs, blocks, order_out, i * GROUP, high, low)
            span = pl.ds(pl.multiple_of(i * GROUP * B, GROUP * B), GROUP * B)
            both = plain_dot(solved[...], high[...])
            more = plain_dot(solved[:width, :], low[...])
            out[:, span] += both[:width] + both[width:] + more
            return carry

        lax.fori_loop(0, groups_of(counts[1]), turn, 0)


def mirror_image(covariance, blocks, solved, order_in, order_out, counts, cap, lead_in, before, name):
    width = solved.shape[0] // 2
    group = GROUP
    cap = padded(cap)
    steps = solved.shape[1] // (group * B)

    def place(which):
        def index_map(i, order_in, order_out, counts):
            last = jnp.maximum(counts[0] - 1, 0)
            return (order_in[jnp.minimum(lead_in + group * i + which, last)], 0)

        return pl.BlockSpec((B * blocks, B), index_map)

    whole = pl.BlockSpec((width, cap * B), lambda i, *_: (0, 0), pipeline_mode=pl.Buffered(1))
    extra = () if before is None else (before,)
    grid_spec = pltpu.PrefetchScalarGridSpec(
        num_scalar_prefetch=3,
        grid=(steps,),
        in_specs=[
            pl.BlockSpec((2 * width, group * B), lambda i, *_: (0, i)),
            *[place(which) for which in range(group)],
            *[whole for _ in extra],
        ],
        out_specs=pl.BlockSpec((width, cap * B), lambda i, *_: (0, 0)),
        scratch_shapes=[pltpu.VMEM((group * B, group * B), jnp.bfloat16)] * 2,
    )
    return pl.pallas_call(
        functools.partial(mirror_kernel, blocks, lead_in),
        name=name,
        grid_spec=grid_spec,
        out_shape=shape_of((width, cap * B)),
        compiler_params=pltpu.CompilerParams(vmem_limit_bytes=VMEM_LIMIT),
        cost_estimate=pl.CostEstimate(
            flops=6 * width * cap * B * solved.shape[1],
            bytes_accessed=4 * (steps * group * B * blocks + 2 * width * cap) * B,
            transcendentals=0,
        ),
    )(order_in, order_out, counts, solved, *[covariance] * group, *extra)


def unpack_kernel(blocks, which, order, counts, *refs):
    parts, out = refs[:-1], refs[-1]
    share = parts[0].shape[0]
    out[...] = jnp.zeros_like(out)
    for i in range(min(blocks, parts[0].shape[1] // B)):

        @pl.when(i < counts[which])
        def _():
            span = slice(i * B, (i + 1) * B)
            block = -parts[0][:, span]
            for part in parts[1:]:
                block = block - part[:, span]
            out[pl.ds(order[i], share, stride=blocks), :] = block


def unpack(parts, order, counts, which, blocks, name):
    return call(
        functools.partial(unpack_kernel, blocks, which),
        name,
        shape_of((parts[0].shape[0] * blocks, B)),
        (order, counts, *parts),
        1,
        in_specs=[SMEM, SMEM] + [VMEM] * len(parts),
    )


def parent_out_kernel(place, lead, *refs):
    pieces, out = refs[:-1], refs[-1]
    share = pieces[0].shape[0]
    for k in range(len(pieces)):
        for j, piece in enumerate(pieces):

            @pl.when(place[1] ^ j == k)
            def _():
                span = slice(k * share, (k + 1) * share)
                out[:, span] = piece[...] - lead[:, span]


def gram_rows(image_rows, solved, total):
    width = solved.shape[0] // 2

    def body(start, size):
        span = pl.ds(start, size)
        rows = split(image_rows[:, span])
        total[...] += three_products(
            lanes_dot, rows, (solved[:width, span], solved[width:, span])
        )

    over_rows(0, image_rows.shape[1] // B, GROUP, body)


def gram_one_kernel(image_rows, solved_one, solved_two, out, total):
    grid_size, _, share = out.shape
    for half, solved in enumerate((solved_one, solved_two)):
        total[...] = jnp.zeros_like(total)
        gram_rows(image_rows, solved, total)
        for k in range(grid_size):
            out[k, half * share:(half + 1) * share, :] = total[:, k * share:(k + 1) * share]


def gram_two_kernel(image_rows, solved_root, image_parent, parent, out, total):
    grid_size, share, _ = out.shape
    total[...] = three_products(lanes_dot, split(image_parent[...].T), split(parent[...]))
    gram_rows(image_rows, solved_root, total)
    for k in range(grid_size):
        out[k, :, :] = total[:, k * share:(k + 1) * share]


def swap_grid(block, grid_size):
    pairs = [
        (r * grid_size + c, c * grid_size + r) for r in range(grid_size) for c in range(grid_size)
    ]
    return lax.ppermute(block, ("row", "col"), pairs)


def scatter_pieces(pieces, grid_size, position):
    return [
        lax.dynamic_index_in_dim(pieces, lax.rem(position + shift, grid_size), 0, keepdims=False)
        for shift in range(grid_size)
    ]


def scatter_sum(pieces, grid_size):
    total = pieces[0]
    for shift in range(1, grid_size):
        total = total + lax.ppermute(
            pieces[shift], "row", [(i, (i + shift) % grid_size) for i in range(grid_size)]
        )
    return total


def mixed_pieces(pieces, grid_size, position):
    return [
        lax.dynamic_index_in_dim(pieces, lax.rem(position + j, grid_size), 0, keepdims=False)
        for j in range(grid_size)
    ]


def mixed_sum(pieces, grid_size):
    total = None
    for j, piece in enumerate(pieces):
        pairs = [
            (r * grid_size + c, c * grid_size + (r + j) % grid_size)
            for r in range(grid_size)
            for c in range(grid_size)
        ]
        piece = lax.ppermute(piece, ("row", "col"), pairs)
        total = piece if total is None else total + piece
    return total


def gather_rows(block, grid_size):
    return [block] + [
        lax.ppermute(block, "row", [(i, (i + shift) % grid_size) for i in range(grid_size)])
        for shift in range(1, grid_size)
    ]


def plane_chips(grid_size):
    return 2 if grid_size == 4 else grid_size


def core_sum(partial, cap, grid_size, col):
    if grid_size != 4:
        return lax.psum_scatter(partial[:, :cap * B], "col", scatter_dimension=0, tiled=True)
    share = partial.shape[0] // grid_size
    core = col % 2
    pieces = partial.reshape(2, 2, share, partial.shape[1])
    part = (2, 1, share, cap * B)
    away = lax.dynamic_slice(pieces, (0, 1 - core, 0, 0), part)[:, 0]
    stay = lax.dynamic_slice(pieces, (0, core, 0, 0), part)[:, 0]
    return (stay + flip(away, "col", 1, grid_size)).reshape(2 * share, cap * B)


def chip_sum(partial, grid_size, col):
    if grid_size != 4:
        return partial
    chip = col // 2
    pieces = partial.reshape(2, -1, partial.shape[1])
    away = lax.dynamic_index_in_dim(pieces, 1 - chip, 0, keepdims=False)
    stay = lax.dynamic_index_in_dim(pieces, chip, 0, keepdims=False)
    return stay + flip(away, "col", 2, grid_size)


def flip(block, axis, bit, grid_size):
    return lax.ppermute(block, axis, [(i, i ^ bit) for i in range(grid_size)])


def gather_cols(block, grid_size, between=None):
    if grid_size != 4:
        gathered = lax.all_gather(block, "col")
        position = lax.axis_index("col")
        return [
            lax.dynamic_index_in_dim(gathered, position ^ j, 0, keepdims=False)
            for j in range(grid_size)
        ], between
    far = flip(block, "col", 2, grid_size)
    near = flip(block, "col", 1, grid_size)
    if between is not None:
        far, between = lax.optimization_barrier((far, between))
    return [block, near, far, flip(far, "col", 1, grid_size)], between


def exchange(gathered, start, size, grid_size, col):
    share = gathered.shape[2]
    pieces = [
        lax.dynamic_slice(gathered, (col ^ j, start, 0), (1, size, share))[0]
        for j in range(grid_size)
    ]
    return [flip(piece, "col", j, grid_size) if j else piece for j, piece in enumerate(pieces)]


def run(
    cap_one, cap_two, covariance, row_order, col_order, info, place, factor_one, inverse_one,
    factor_parent, factor_root, inverse_two,
):
    grid_size = lax.axis_size("row")
    row = lax.axis_index("row")
    col = lax.axis_index("col")
    share, width = inverse_one.shape
    blocks = row_order.shape[0]
    col_info = info[2:4]

    half = padded(pl.cdiv(cap_one, 2)) if cap_one < blocks else cap_one
    parts = [(lead_in, min(half, cap_one - lead_in)) for lead_in in range(0, cap_one, half)]
    packed_one, bare_one = call(
        functools.partial(pack_one_kernel, cap_one),
        "pack_one",
        (
            shape_of((cap_one * B + 2 * width, share)),
            shape_of((cap_one * B, share)),
        ),
        (row_order, info, factor_one.reshape(blocks, B, share), inverse_one, inverse_two),
        1,
        in_specs=[SMEM, SMEM, VMEM, VMEM, VMEM],
    )
    every_row = lax.all_gather(bare_one, "row")
    parent_rows = call(
        place_kernel,
        "parent_rows",
        shape_of((width, share)),
        (place, *gather_rows(factor_parent, grid_size)),
        1,
        in_specs=[SMEM] + [VMEM] * grid_size,
    )
    packed_two = call(
        functools.partial(pack_two_kernel, cap_two),
        "pack_two",
        shape_of((cap_two * B, share)),
        (row_order, info, factor_root.reshape(blocks, B, share)),
        1,
        in_specs=[SMEM] * 2 + [VMEM],
    )
    gathered_parent, _ = gather_cols(parent_rows, grid_size)
    gathered_one, (gathered_parent, packed_two) = gather_cols(
        packed_one, grid_size, (gathered_parent, packed_two)
    )

    solved_one, lag, lead_inverse, inverse_two, lead, diag_one, diag_two, parent = call(
        functools.partial(solve_one_kernel, cap_one, grid_size),
        "solve_one",
        (
            shape_of((2 * width, padded(cap_one) * B), jnp.bfloat16),
            shape_of((width, cap_one * B)),
            shape_of((2 * width, width), jnp.bfloat16),
            shape_of((2 * width, width), jnp.bfloat16),
            shape_of((share, width)),
            shape_of((share, share)),
            shape_of((share, share)),
            shape_of((width, share)),
        ),
        (place, *gathered_one, *gathered_parent),
        12 * width * width * cap_one * B,
        in_specs=[SMEM] + [VMEM] * (2 * grid_size),
        scratch=[pltpu.VMEM((2 * width, width), jnp.bfloat16)] * 3,
    )
    gathered_two, lag = gather_cols(packed_two, grid_size, lag)
    solved_two, solved_root = call(
        functools.partial(solve_two_kernel, cap_one, cap_two),
        "solve_two",
        (
            shape_of((2 * width, padded(cap_one) * B), jnp.bfloat16),
            shape_of((2 * width, padded(cap_two) * B), jnp.bfloat16),
        ),
        (inverse_two, lag, *gathered_two),
        6 * width * width * cap_two * B,
    )
    counts = jnp.stack([info[0], info[3]])
    image_two = image(covariance, blocks, solved_two, row_order, col_order, counts, cap_two, "image_two")
    every_row, image_two = lax.optimization_barrier((every_row, image_two))
    image_two = lax.psum_scatter(image_two, "row", scatter_dimension=0, tiled=True)

    counts = jnp.stack([info[2], info[0]])

    def far_product(far_rows, lead_inverse, lead_in, before):
        size = far_rows[0].shape[0] // B
        solved_far = call(
            functools.partial(solve_far_kernel, size),
            f"solve_far_{lead_in}",
            shape_of((2 * width, padded(size) * B), jnp.bfloat16),
            (lead_inverse, *far_rows),
            6 * width * width * size * B,
        )
        return mirror_image(
            covariance, blocks, solved_far, col_order, row_order, counts, cap_one, lead_in, before,
            f"image_one_{lead_in}",
        )

    def far_part(every_row, part):
        return exchange(every_row, part[0] * B, part[1] * B, grid_size, col)

    def first_part(every_row, lead_inverse):
        far_rows = far_part(every_row, parts[0])
        rest = []
        if len(parts) > 1:
            every_row, _ = lax.optimization_barrier((every_row, far_rows))
            rest = far_part(every_row, parts[1])
        return far_product(far_rows, lead_inverse, 0, None), rest

    def no_first_part(every_row, lead_inverse):
        rest = [jnp.zeros((parts[1][1] * B, share), jnp.float32)] * grid_size if len(parts) > 1 else []
        return jnp.zeros((width, padded(cap_one) * B), jnp.float32), rest

    def last_part(partial, rest, lead_inverse):
        if rest:
            partial = far_product(rest, lead_inverse, parts[1][0], partial)
        return core_sum(partial, cap_one, grid_size, col)

    def no_last_part(partial, rest, lead_inverse):
        return jnp.zeros((width // plane_chips(grid_size), cap_one * B), jnp.float32)

    some = info[5] > 0
    rows_one, rest = lax.cond(some, first_part, no_first_part, every_row, lead_inverse)
    rows_one, rest, image_two = lax.optimization_barrier((rows_one, rest, image_two))
    rows_two = swap_grid(image_two, grid_size)
    rows_one = lax.cond(some, last_part, no_last_part, rows_one, rest, lead_inverse)
    rows_one, rows_two = lax.optimization_barrier((rows_one, rows_two))
    rows_one = chip_sum(rows_one, grid_size, col)
    gram_one = call(
        gram_one_kernel,
        "gram_one",
        shape_of((grid_size, 2 * share, share)),
        (rows_one, solved_one, solved_two),
        12 * share * width * cap_one * B,
        scratch=[pltpu.VMEM((share, width), jnp.float32)],
    )
    mixed = mixed_sum(mixed_pieces(gram_one[:, share:], grid_size, row), grid_size)
    image_one = swap_grid(rows_one, grid_size)
    mixed, image_one = lax.optimization_barrier((mixed, image_one))
    own_lead = lax.dynamic_slice_in_dim(lead, col * share, share, 1)
    gram_two = call(
        gram_two_kernel,
        "gram_two",
        shape_of((grid_size, share, share)),
        (rows_two, solved_root, own_lead - mixed, parent),
        6 * share * width * cap_two * B,
        scratch=[pltpu.VMEM((share, width), jnp.float32)],
    )
    grams = jnp.concatenate([gram_one[:, :share], gram_two], 1)
    pieces, mixed = lax.optimization_barrier((scatter_pieces(grams, grid_size, row), mixed))
    grams = scatter_sum(pieces, grid_size)
    mixed_parts = gather_cols(mixed, grid_size)[0]
    block_one = grams[:share] + diag_one
    block_two = grams[share:] + diag_two
    parent_out = call(
        parent_out_kernel,
        "parent_out",
        shape_of((share, width)),
        (place, lead, *mixed_parts),
        1,
        in_specs=[SMEM] + [VMEM] * (1 + grid_size),
    )
    cross_two = unpack([image_two], col_order, col_info, 1, blocks, "cross_two")
    cross_one = unpack([image_one], col_order, col_info, 0, blocks, "cross_one")
    return cross_one, block_one, parent_out, cross_two, block_two


def capacities_of(blocks):
    parts = ((0.85, 0.7), (0.75, 0.6)) if blocks >= 16 else ()
    return [(blocks, blocks)] + [(round(one * blocks), round(two * blocks)) for one, two in parts]


def local(
    root_covariance, factor_one, inverse_one, pattern_one, factor_parent, factor_root, inverse_two,
    pattern_two,
):
    blocks = root_covariance.shape[3]
    capacities = capacities_of(blocks)
    place = jnp.stack([lax.axis_index("row"), lax.axis_index("col")]).astype(jnp.int32)
    row_order, col_order, info = pl.pallas_call(
        functools.partial(plan_kernel, capacities),
        name="plan",
        out_shape=(
            shape_of((blocks,), jnp.int32), shape_of((blocks,), jnp.int32), shape_of((6,), jnp.int32)
        ),
        in_specs=[SMEM] * 3,
        out_specs=(SMEM,) * 3,
    )(place, pattern_one, pattern_two)
    operands = (
        root_covariance.reshape(-1, B), row_order, col_order, info, place, factor_one, inverse_one,
        factor_parent, factor_root, inverse_two,
    )
    branches = [functools.partial(run, one, two) for one, two in capacities]
    if len(branches) == 1:
        results = branches[0](*operands)
    else:
        results = lax.switch(info[4], branches, *operands)
    cross_one, block_one, parent_out, cross_two, block_two = results
    cross_one = cross_one.reshape(-1, blocks, 1, B)
    cross_two = cross_two.reshape(-1, blocks, 1, B)
    return cross_one, block_one, parent_out, cross_two, block_two


def solution(mesh):
    return jax.shard_map(
        local,
        mesh=mesh,
        in_specs=(
            P("grp", "col", None, None, "row", None),
            P("grp", "row", None, "col"),
            P(("grp", "col"), None),
            P("grp"),
            P(("grp", "row"), "col"),
            P("grp", "row", None, "col"),
            P(("grp", "col"), None),
            P("grp"),
        ),
        out_specs=(
            P(("grp", "row"), None, "col", None),
            P(("grp", "col"), "row"),
            P(("grp", "row"), None),
            P(("grp", "row"), None, "col", None),
            P(("grp", "col"), "row"),
        ),
        check_vma=False,
    )
```

```python
import functools

import jax
import jax.numpy as jnp
from jax import lax
from jax.experimental import pallas as pl
from jax.experimental.pallas import tpu as pltpu
from jax.sharding import PartitionSpec as P

B = 128
VMEM_LIMIT = 52 * 1024 * 1024
GROUP = 4
VMEM = pl.BlockSpec(memory_space=pltpu.VMEM)
SMEM = pl.BlockSpec(memory_space=pltpu.SMEM)


def split(values):
    high = values.astype(jnp.bfloat16)
    low = (values - high.astype(jnp.float32)).astype(jnp.bfloat16)
    return high, low


def lanes_dot(left, right):
    return lax.dot_general(
        left, right, (((1,), (1,)), ((), ())), preferred_element_type=jnp.float32
    )


def plain_dot(left, right):
    return lax.dot_general(
        left, right, (((1,), (0,)), ((), ())), preferred_element_type=jnp.float32
    )


def three_products(dot, left, right):
    left_high, left_low = left
    right_high, right_low = right
    rows = left_high.shape[0]
    both = dot(jnp.concatenate([left_high, left_low], 0), right_high)
    return both[:rows] + both[rows:] + dot(left_high, right_low)


def stacked(high, low):
    return jnp.concatenate([high, low], 0)


def call(kernel, name, out_shape, operands, flops, in_specs=None, scratch=()):
    size = sum(a.size * a.dtype.itemsize for a in operands)
    size += sum(a.size * a.dtype.itemsize for a in jax.tree.leaves(out_shape))
    return pl.pallas_call(
        kernel,
        name=name,
        out_shape=out_shape,
        in_specs=in_specs or [VMEM] * len(operands),
        out_specs=jax.tree.map(lambda _: VMEM, out_shape),
        scratch_shapes=scratch,
        compiler_params=pltpu.CompilerParams(vmem_limit_bytes=VMEM_LIMIT),
        cost_estimate=pl.CostEstimate(
            flops=flops, bytes_accessed=size, transcendentals=0
        ),
    )(*operands)


def shape_of(shape, dtype=jnp.float32):
    return jax.ShapeDtypeStruct(shape, dtype)


def plan_kernel(capacities, place, pattern_one, pattern_two, row_order, col_order, info):
    blocks = row_order.shape[0]
    grid_size = pattern_one.shape[0] // blocks
    largest_one, largest_two = jnp.int32(0), jnp.int32(0)
    counts_one, counts_two = [], []
    for p in range(grid_size):

        def count(b, carry):
            return (
                carry[0] + pattern_one[b * grid_size + p],
                carry[1] + pattern_two[b * grid_size + p],
            )

        one, two = lax.fori_loop(0, blocks, count, (jnp.int32(0), jnp.int32(0)))
        counts_one.append(one)
        counts_two.append(two)
        largest_one = jnp.maximum(largest_one, one)
        largest_two = jnp.maximum(largest_two, two)
    choice = jnp.int32(len(capacities) - 1)
    for i in range(len(capacities) - 1):
        fits = (largest_one <= capacities[i][0]) & (largest_two <= capacities[i][1])
        choice = jnp.where(fits, i, choice)
    info[4] = choice
    info[5] = largest_one
    for axis, order in enumerate((row_order, col_order)):
        position = place[axis]
        own_one, own_two = jnp.int32(0), jnp.int32(0)
        for p in range(grid_size):
            own_one = jnp.where(position == p, counts_one[p], own_one)
            own_two = jnp.where(position == p, counts_two[p], own_two)
        info[2 * axis] = own_one
        info[2 * axis + 1] = own_two

        def put(b, carry):
            one = pattern_one[b * grid_size + position]
            two = pattern_two[b * grid_size + position]
            slot = jnp.where(two > 0, carry[0], jnp.where(one > 0, carry[1], carry[2]))
            order[slot] = b
            return (carry[0] + two, carry[1] + one - two, carry[2] + 1 - one)

        lax.fori_loop(0, blocks, put, (jnp.int32(0), own_two, own_one))


def pack_one_kernel(cap, order, info, factor, inverse_one, inverse_two, out, out_bare):
    width = inverse_one.shape[1]
    for i in range(cap):
        block = jnp.where(i < info[0], factor[order[i]], 0.0)
        out[pl.ds(i * B, B), :] = block
        out_bare[pl.ds(i * B, B), :] = block
    out[pl.ds(cap * B, width), :] = inverse_one[...].T
    out[pl.ds(cap * B + width, width), :] = inverse_two[...].T


def pack_two_kernel(cap, order, info, factor, out):
    for i in range(cap):
        out[pl.ds(i * B, B), :] = jnp.where(i < info[1], factor[order[i]], 0.0)


def place_kernel(place, *refs):
    pieces, out = refs[:-1], refs[-1]
    share = pieces[0].shape[0]
    grid_size = len(pieces)
    for shift, piece in enumerate(pieces):
        source = lax.rem(place[0] + grid_size - shift, grid_size)
        out[pl.ds(pl.multiple_of(source * share, share), share), :] = piece[...]


def all_rows(cap, body):
    size = min(cap, GROUP)

    def turn(i, carry):
        body(pl.multiple_of(jnp.minimum(i * GROUP, cap - size) * B, B), size * B)
        return carry

    lax.fori_loop(0, pl.cdiv(cap, GROUP), turn, 0)


def joined(refs, start, size):
    return jnp.concatenate([ref[pl.ds(start, size), :] for ref in refs], 1)


def padded(cap):
    return pl.cdiv(cap, GROUP) * GROUP


def over_rows(first, last, step, body):
    whole = (last - first) // step

    def turn(i, carry):
        body(pl.multiple_of(first * B + i * (step * B), B), step * B)
        return carry

    lax.fori_loop(0, whole, turn, 0)
    rest = last - first - whole * step
    if rest:
        body((first + whole * step) * B, rest * B)


def clear_rest(out, cap):
    if out.shape[1] > cap * B:
        out[:, cap * B:] = jnp.zeros((out.shape[0], out.shape[1] - cap * B), out.dtype)


def solve_rows(inverse, refs, out, cap):
    width = out.shape[0] // 2
    clear_rest(out, cap)

    def body(start, size):
        rows = split(joined(refs, start, size))
        high, low = split(three_products(lanes_dot, inverse, rows))
        out[:width, pl.ds(start, size)] = high
        out[width:, pl.ds(start, size)] = low

    all_rows(cap, body)


def solve_one_kernel(cap, grid_size, place, *refs):
    gathered, parents = refs[:grid_size], refs[grid_size:2 * grid_size]
    (
        out, out_lag, out_inverse_one, out_inverse_two, out_lead, out_diag_one, out_diag_two,
        out_parent, parent, solved_parent, weight,
    ) = refs[2 * grid_size:]
    share, width = out_lead.shape
    row, col = place[0], place[1]
    first, second = cap * B, cap * B + width
    part = width // 4

    def halves(ref):
        return ref[:width, :], ref[width:, :]

    def by_parts(target, part_of):
        def turn(i, carry):
            start = pl.multiple_of(i * part, part)
            high, low = split(part_of(start))
            target[pl.ds(start, part), :] = high
            target[pl.ds(width + start, part), :] = low
            return carry

        lax.fori_loop(0, 4, turn, 0)

    def product_of(dot, left, right):
        def part_of(start):
            pair = left[pl.ds(start, part), :], left[pl.ds(width + start, part), :]
            return three_products(dot, pair, halves(right))

        return part_of

    by_parts(out_inverse_one, lambda start: joined(gathered, first + start, part))
    by_parts(out_inverse_two, lambda start: joined(gathered, second + start, part))
    by_parts(parent, lambda start: joined(parents, start, part))
    by_parts(solved_parent, product_of(lanes_dot, out_inverse_two, parent))
    by_parts(weight, product_of(plain_dot, solved_parent, out_inverse_one))
    row_start = pl.multiple_of(row * share, share)
    col_start = pl.multiple_of(col * share, share)
    out_parent[...] = three_products(
        lanes_dot, halves(out_inverse_two), split(joined(parents, row_start, share))
    )
    for start, diag in ((first, out_diag_one), (second, out_diag_two)):
        inv_row = split(joined(gathered, start + row_start, share))
        inv_col = split(joined(gathered, start + col_start, share))
        diag[...] = three_products(lanes_dot, inv_col, inv_row)
        if start == first:
            out_lead[...] = three_products(lanes_dot, inv_row, halves(weight))

    clear_rest(out, cap)

    def body(start, size):
        rows = split(joined(gathered, start, size))
        high, low = split(three_products(lanes_dot, halves(out_inverse_one), rows))
        out[:width, pl.ds(start, size)] = high
        out[width:, pl.ds(start, size)] = low
        out_lag[:, pl.ds(start, size)] = three_products(lanes_dot, halves(weight), rows)

    all_rows(cap, body)


def solve_far_kernel(cap, inverse, *refs):
    gathered, out = refs[:-1], refs[-1]
    width = out.shape[0] // 2
    solve_rows((inverse[:width, :], inverse[width:, :]), gathered, out, cap)


def solve_two_kernel(cap_one, cap_two, inverse, lag, *refs):
    gathered, (out_full, out_root) = refs[:-2], refs[-2:]
    width = lag.shape[0]
    halves = (inverse[:width, :], inverse[width:, :])
    clear_rest(out_full, cap_one)
    clear_rest(out_root, cap_two)

    def both(start, size):
        own = three_products(lanes_dot, halves, split(joined(gathered, start, size)))
        high, low = split(own)
        out_root[:width, pl.ds(start, size)] = high
        out_root[width:, pl.ds(start, size)] = low
        high, low = split(own - lag[:, pl.ds(start, size)])
        out_full[:width, pl.ds(start, size)] = high
        out_full[width:, pl.ds(start, size)] = low

    all_rows(cap_two, both)
    if cap_one > cap_two:
        high, low = split(-lag[:, cap_two * B:])
        out_full[:width, cap_two * B:cap_one * B] = high
        out_full[width:, cap_two * B:cap_one * B] = low


def load_blocks(covs, blocks, order, lead, high, low):
    for j in range(GROUP):
        column = order[jnp.minimum(lead + j, blocks - 1)]
        for part, cov in enumerate(covs):
            piece = cov[pl.ds(column, B, stride=blocks), :]
            piece_high, piece_low = split(piece)
            high[part * B:(part + 1) * B, j * B:(j + 1) * B] = piece_high
            low[part * B:(part + 1) * B, j * B:(j + 1) * B] = piece_low


def groups_of(count):
    return (count + GROUP - 1) // GROUP


def image_kernel(blocks, order_in, order_out, counts, solved, *refs):
    covs, (out, high, low) = refs[:GROUP], refs[GROUP:]
    step = pl.program_id(0)
    width = out.shape[0]
    out[...] = jnp.zeros_like(out)

    @pl.when(GROUP * step < counts[1])
    def _():
        def turn(i, carry):
            load_blocks(covs, blocks, order_in, i * GROUP, high, low)
            span = pl.ds(pl.multiple_of(i * GROUP * B, GROUP * B), GROUP * B)
            both = lanes_dot(solved[:, span], high[...])
            more = lanes_dot(solved[:width, span], low[...])
            out[...] += both[:width] + both[width:] + more
            return carry

        lax.fori_loop(0, groups_of(counts[0]), turn, 0)


def image(covariance, blocks, solved, order_in, order_out, counts, cap_out, name):
    width = solved.shape[0] // 2
    cap_in = solved.shape[1] // B
    group = GROUP

    def place(which):
        def index_map(i, order_in, order_out, counts):
            last = jnp.maximum(counts[1] - 1, 0)
            return (order_out[jnp.minimum(group * i + which, last)], 0)

        return pl.BlockSpec((B * blocks, B), index_map)

    grid_spec = pltpu.PrefetchScalarGridSpec(
        num_scalar_prefetch=3,
        grid=(pl.cdiv(cap_out, group),),
        in_specs=[
            pl.BlockSpec(solved.shape, lambda i, *_: (0, 0), pipeline_mode=pl.Buffered(1)),
            *[place(which) for which in range(group)],
        ],
        out_specs=pl.BlockSpec((width, group * B), lambda i, *_: (0, i)),
        scratch_shapes=[
            pltpu.VMEM((group * B, group * B), jnp.bfloat16),
            pltpu.VMEM((group * B, group * B), jnp.bfloat16),
        ],
    )
    return pl.pallas_call(
        functools.partial(image_kernel, blocks),
        name=name,
        grid_spec=grid_spec,
        out_shape=shape_of((width, cap_out * B)),
        compiler_params=pltpu.CompilerParams(vmem_limit_bytes=VMEM_LIMIT),
        cost_estimate=pl.CostEstimate(
            flops=6 * width * cap_in * B * cap_out * B,
            bytes_accessed=(4 * blocks * B + 8 * width) * cap_out * B,
            transcendentals=0,
        ),
    )(order_in, order_out, counts, solved, *[covariance] * group)


def mirror_kernel(blocks, lead_in, order_in, order_out, counts, solved, *refs):
    covs, (out, high, low) = refs[:GROUP], refs[-3:]
    step = pl.program_id(0)
    width = out.shape[0]

    @pl.when(step == 0)
    def _():
        out[...] = refs[GROUP][...] if len(refs) > GROUP + 3 else jnp.zeros_like(out)

    @pl.when(lead_in + GROUP * step < counts[0])
    def _():
        def turn(i, carry):
            load_blocks(covs, blocks, order_out, i * GROUP, high, low)
            span = pl.ds(pl.multiple_of(i * GROUP * B, GROUP * B), GROUP * B)
            both = plain_dot(solved[...], high[...])
            more = plain_dot(solved[:width, :], low[...])
            out[:, span] += both[:width] + both[width:] + more
            return carry

        lax.fori_loop(0, groups_of(counts[1]), turn, 0)


def mirror_image(covariance, blocks, solved, order_in, order_out, counts, cap, lead_in, before, name):
    width = solved.shape[0] // 2
    group = GROUP
    cap = padded(cap)
    steps = solved.shape[1] // (group * B)

    def place(which):
        def index_map(i, order_in, order_out, counts):
            last = jnp.maximum(counts[0] - 1, 0)
            return (order_in[jnp.minimum(lead_in + group * i + which, last)], 0)

        return pl.BlockSpec((B * blocks, B), index_map)

    whole = pl.BlockSpec((width, cap * B), lambda i, *_: (0, 0), pipeline_mode=pl.Buffered(1))
    extra = () if before is None else (before,)
    grid_spec = pltpu.PrefetchScalarGridSpec(
        num_scalar_prefetch=3,
        grid=(steps,),
        in_specs=[
            pl.BlockSpec((2 * width, group * B), lambda i, *_: (0, i)),
            *[place(which) for which in range(group)],
            *[whole for _ in extra],
        ],
        out_specs=pl.BlockSpec((width, cap * B), lambda i, *_: (0, 0)),
        scratch_shapes=[pltpu.VMEM((group * B, group * B), jnp.bfloat16)] * 2,
    )
    return pl.pallas_call(
        functools.partial(mirror_kernel, blocks, lead_in),
        name=name,
        grid_spec=grid_spec,
        out_shape=shape_of((width, cap * B)),
        compiler_params=pltpu.CompilerParams(vmem_limit_bytes=VMEM_LIMIT),
        cost_estimate=pl.CostEstimate(
            flops=6 * width * cap * B * solved.shape[1],
            bytes_accessed=4 * (steps * group * B * blocks + 2 * width * cap) * B,
            transcendentals=0,
        ),
    )(order_in, order_out, counts, solved, *[covariance] * group, *extra)


def unpack_kernel(blocks, which, order, counts, *refs):
    parts, out = refs[:-1], refs[-1]
    share = parts[0].shape[0]
    out[...] = jnp.zeros_like(out)
    for i in range(min(blocks, parts[0].shape[1] // B)):

        @pl.when(i < counts[which])
        def _():
            span = slice(i * B, (i + 1) * B)
            block = -parts[0][:, span]
            for part in parts[1:]:
                block = block - part[:, span]
            out[pl.ds(order[i], share, stride=blocks), :] = block


def unpack(parts, order, counts, which, blocks, name):
    return call(
        functools.partial(unpack_kernel, blocks, which),
        name,
        shape_of((parts[0].shape[0] * blocks, B)),
        (order, counts, *parts),
        1,
        in_specs=[SMEM, SMEM] + [VMEM] * len(parts),
    )


def parent_out_kernel(place, lead, *refs):
    pieces, out = refs[:-1], refs[-1]
    share = pieces[0].shape[0]
    for k in range(len(pieces)):
        for j, piece in enumerate(pieces):

            @pl.when(place[1] ^ j == k)
            def _():
                span = slice(k * share, (k + 1) * share)
                out[:, span] = piece[...] - lead[:, span]


def gram_rows(image_rows, solved, total):
    width = solved.shape[0] // 2

    def body(start, size):
        span = pl.ds(start, size)
        rows = split(image_rows[:, span])
        total[...] += three_products(
            lanes_dot, rows, (solved[:width, span], solved[width:, span])
        )

    over_rows(0, image_rows.shape[1] // B, GROUP, body)


def gram_one_kernel(image_rows, solved_one, solved_two, out, total):
    grid_size, _, share = out.shape
    for half, solved in enumerate((solved_one, solved_two)):
        total[...] = jnp.zeros_like(total)
        gram_rows(image_rows, solved, total)
        for k in range(grid_size):
            out[k, half * share:(half + 1) * share, :] = total[:, k * share:(k + 1) * share]


def gram_two_kernel(image_rows, solved_root, image_parent, parent, out, total):
    grid_size, share, _ = out.shape
    total[...] = three_products(lanes_dot, split(image_parent[...].T), split(parent[...]))
    gram_rows(image_rows, solved_root, total)
    for k in range(grid_size):
        out[k, :, :] = total[:, k * share:(k + 1) * share]


def swap_grid(block, grid_size):
    pairs = [
        (r * grid_size + c, c * grid_size + r) for r in range(grid_size) for c in range(grid_size)
    ]
    return lax.ppermute(block, ("row", "col"), pairs)


def scatter_pieces(pieces, grid_size, position):
    return [
        lax.dynamic_index_in_dim(pieces, lax.rem(position + shift, grid_size), 0, keepdims=False)
        for shift in range(grid_size)
    ]


def scatter_sum(pieces, grid_size):
    total = pieces[0]
    for shift in range(1, grid_size):
        total = total + lax.ppermute(
            pieces[shift], "row", [(i, (i + shift) % grid_size) for i in range(grid_size)]
        )
    return total


def mixed_pieces(pieces, grid_size, position):
    return [
        lax.dynamic_index_in_dim(pieces, lax.rem(position + j, grid_size), 0, keepdims=False)
        for j in range(grid_size)
    ]


def mixed_sum(pieces, grid_size):
    total = None
    for j, piece in enumerate(pieces):
        pairs = [
            (r * grid_size + c, c * grid_size + (r + j) % grid_size)
            for r in range(grid_size)
            for c in range(grid_size)
        ]
        piece = lax.ppermute(piece, ("row", "col"), pairs)
        total = piece if total is None else total + piece
    return total


def gather_rows(block, grid_size):
    return [block] + [
        lax.ppermute(block, "row", [(i, (i + shift) % grid_size) for i in range(grid_size)])
        for shift in range(1, grid_size)
    ]


def plane_chips(grid_size):
    return 2 if grid_size == 4 else grid_size


def core_sum(partial, cap, grid_size, col):
    if grid_size != 4:
        return lax.psum_scatter(partial[:, :cap * B], "col", scatter_dimension=0, tiled=True)
    share = partial.shape[0] // grid_size
    core = col % 2
    pieces = partial.reshape(2, 2, share, partial.shape[1])
    part = (2, 1, share, cap * B)
    away = lax.dynamic_slice(pieces, (0, 1 - core, 0, 0), part)[:, 0]
    stay = lax.dynamic_slice(pieces, (0, core, 0, 0), part)[:, 0]
    return (stay + flip(away, "col", 1, grid_size)).reshape(2 * share, cap * B)


def chip_sum(partial, grid_size, col):
    if grid_size != 4:
        return partial
    chip = col // 2
    pieces = partial.reshape(2, -1, partial.shape[1])
    away = lax.dynamic_index_in_dim(pieces, 1 - chip, 0, keepdims=False)
    stay = lax.dynamic_index_in_dim(pieces, chip, 0, keepdims=False)
    return stay + flip(away, "col", 2, grid_size)


def flip(block, axis, bit, grid_size):
    return lax.ppermute(block, axis, [(i, i ^ bit) for i in range(grid_size)])


def gather_cols(block, grid_size, between=None):
    if grid_size != 4:
        gathered = lax.all_gather(block, "col")
        position = lax.axis_index("col")
        return [
            lax.dynamic_index_in_dim(gathered, position ^ j, 0, keepdims=False)
            for j in range(grid_size)
        ], between
    far = flip(block, "col", 2, grid_size)
    near = flip(block, "col", 1, grid_size)
    if between is not None:
        far, between = lax.optimization_barrier((far, between))
    return [block, near, far, flip(far, "col", 1, grid_size)], between


def exchange(gathered, start, size, grid_size, col):
    share = gathered.shape[2]
    pieces = [
        lax.dynamic_slice(gathered, (col ^ j, start, 0), (1, size, share))[0]
        for j in range(grid_size)
    ]
    return [flip(piece, "col", j, grid_size) if j else piece for j, piece in enumerate(pieces)]


def run(
    cap_one, cap_two, covariance, row_order, col_order, info, place, factor_one, inverse_one,
    factor_parent, factor_root, inverse_two,
):
    grid_size = lax.axis_size("row")
    row = lax.axis_index("row")
    col = lax.axis_index("col")
    share, width = inverse_one.shape
    blocks = row_order.shape[0]
    col_info = info[2:4]

    half = padded(pl.cdiv(cap_one, 2)) if cap_one < blocks else cap_one
    parts = [(lead_in, min(half, cap_one - lead_in)) for lead_in in range(0, cap_one, half)]
    packed_one, bare_one = call(
        functools.partial(pack_one_kernel, cap_one),
        "pack_one",
        (
            shape_of((cap_one * B + 2 * width, share)),
            shape_of((cap_one * B, share)),
        ),
        (row_order, info, factor_one.reshape(blocks, B, share), inverse_one, inverse_two),
        1,
        in_specs=[SMEM, SMEM, VMEM, VMEM, VMEM],
    )
    every_row = lax.all_gather(bare_one, "row")
    parent_rows = call(
        place_kernel,
        "parent_rows",
        shape_of((width, share)),
        (place, *gather_rows(factor_parent, grid_size)),
        1,
        in_specs=[SMEM] + [VMEM] * grid_size,
    )
    packed_two = call(
        functools.partial(pack_two_kernel, cap_two),
        "pack_two",
        shape_of((cap_two * B, share)),
        (row_order, info, factor_root.reshape(blocks, B, share)),
        1,
        in_specs=[SMEM] * 2 + [VMEM],
    )
    gathered_parent, _ = gather_cols(parent_rows, grid_size)
    gathered_one, (gathered_parent, packed_two) = gather_cols(
        packed_one, grid_size, (gathered_parent, packed_two)
    )

    solved_one, lag, lead_inverse, inverse_two, lead, diag_one, diag_two, parent = call(
        functools.partial(solve_one_kernel, cap_one, grid_size),
        "solve_one",
        (
            shape_of((2 * width, padded(cap_one) * B), jnp.bfloat16),
            shape_of((width, cap_one * B)),
            shape_of((2 * width, width), jnp.bfloat16),
            shape_of((2 * width, width), jnp.bfloat16),
            shape_of((share, width)),
            shape_of((share, share)),
            shape_of((share, share)),
            shape_of((width, share)),
        ),
        (place, *gathered_one, *gathered_parent),
        12 * width * width * cap_one * B,
        in_specs=[SMEM] + [VMEM] * (2 * grid_size),
        scratch=[pltpu.VMEM((2 * width, width), jnp.bfloat16)] * 3,
    )
    gathered_two, lag = gather_cols(packed_two, grid_size, lag)
    solved_two, solved_root = call(
        functools.partial(solve_two_kernel, cap_one, cap_two),
        "solve_two",
        (
            shape_of((2 * width, padded(cap_one) * B), jnp.bfloat16),
            shape_of((2 * width, padded(cap_two) * B), jnp.bfloat16),
        ),
        (inverse_two, lag, *gathered_two),
        6 * width * width * cap_two * B,
    )
    counts = jnp.stack([info[0], info[3]])
    image_two = image(covariance, blocks, solved_two, row_order, col_order, counts, cap_two, "image_two")
    every_row, image_two = lax.optimization_barrier((every_row, image_two))
    image_two = lax.psum_scatter(image_two, "row", scatter_dimension=0, tiled=True)

    counts = jnp.stack([info[2], info[0]])

    def far_product(far_rows, lead_inverse, lead_in, before):
        size = far_rows[0].shape[0] // B
        solved_far = call(
            functools.partial(solve_far_kernel, size),
            f"solve_far_{lead_in}",
            shape_of((2 * width, padded(size) * B), jnp.bfloat16),
            (lead_inverse, *far_rows),
            6 * width * width * size * B,
        )
        return mirror_image(
            covariance, blocks, solved_far, col_order, row_order, counts, cap_one, lead_in, before,
            f"image_one_{lead_in}",
        )

    def far_part(every_row, part):
        return exchange(every_row, part[0] * B, part[1] * B, grid_size, col)

    def first_part(every_row, lead_inverse):
        far_rows = far_part(every_row, parts[0])
        rest = []
        if len(parts) > 1:
            every_row, _ = lax.optimization_barrier((every_row, far_rows))
            rest = far_part(every_row, parts[1])
        return far_product(far_rows, lead_inverse, 0, None), rest

    def no_first_part(every_row, lead_inverse):
        rest = [jnp.zeros((parts[1][1] * B, share), jnp.float32)] * grid_size if len(parts) > 1 else []
        return jnp.zeros((width, padded(cap_one) * B), jnp.float32), rest

    def last_part(partial, rest, lead_inverse):
        if rest:
            partial = far_product(rest, lead_inverse, parts[1][0], partial)
        return core_sum(partial, cap_one, grid_size, col)

    def no_last_part(partial, rest, lead_inverse):
        return jnp.zeros((width // plane_chips(grid_size), cap_one * B), jnp.float32)

    some = info[5] > 0
    rows_one, rest = lax.cond(some, first_part, no_first_part, every_row, lead_inverse)
    rows_one, rest, image_two = lax.optimization_barrier((rows_one, rest, image_two))
    rows_two = swap_grid(image_two, grid_size)
    rows_one = lax.cond(some, last_part, no_last_part, rows_one, rest, lead_inverse)
    rows_one, rows_two = lax.optimization_barrier((rows_one, rows_two))
    rows_one = chip_sum(rows_one, grid_size, col)
    gram_one = call(
        gram_one_kernel,
        "gram_one",
        shape_of((grid_size, 2 * share, share)),
        (rows_one, solved_one, solved_two),
        12 * share * width * cap_one * B,
        scratch=[pltpu.VMEM((share, width), jnp.float32)],
    )
    mixed = mixed_sum(mixed_pieces(gram_one[:, share:], grid_size, row), grid_size)
    image_one = swap_grid(rows_one, grid_size)
    mixed, image_one = lax.optimization_barrier((mixed, image_one))
    own_lead = lax.dynamic_slice_in_dim(lead, col * share, share, 1)
    gram_two = call(
        gram_two_kernel,
        "gram_two",
        shape_of((grid_size, share, share)),
        (rows_two, solved_root, own_lead - mixed, parent),
        6 * share * width * cap_two * B,
        scratch=[pltpu.VMEM((share, width), jnp.float32)],
    )
    grams = jnp.concatenate([gram_one[:, :share], gram_two], 1)
    pieces, mixed = lax.optimization_barrier((scatter_pieces(grams, grid_size, row), mixed))
    grams = scatter_sum(pieces, grid_size)
    mixed_parts = gather_cols(mixed, grid_size)[0]
    block_one = grams[:share] + diag_one
    block_two = grams[share:] + diag_two
    parent_out = call(
        parent_out_kernel,
        "parent_out",
        shape_of((share, width)),
        (place, lead, *mixed_parts),
        1,
        in_specs=[SMEM] + [VMEM] * (1 + grid_size),
    )
    cross_two = unpack([image_two], col_order, col_info, 1, blocks, "cross_two")
    cross_one = unpack([image_one], col_order, col_info, 0, blocks, "cross_one")
    return cross_one, block_one, parent_out, cross_two, block_two


def capacities_of(blocks):
    parts = ((0.85, 0.7), (0.75, 0.6)) if blocks >= 16 else ()
    return [(round(one * blocks), round(two * blocks)) for one, two in parts] + [(blocks, blocks)]


def local(
    root_covariance, factor_one, inverse_one, pattern_one, factor_parent, factor_root, inverse_two,
    pattern_two,
):
    blocks = root_covariance.shape[3]
    capacities = capacities_of(blocks)
    place = jnp.stack([lax.axis_index("row"), lax.axis_index("col")]).astype(jnp.int32)
    row_order, col_order, info = pl.pallas_call(
        functools.partial(plan_kernel, capacities),
        name="plan",
        out_shape=(
            shape_of((blocks,), jnp.int32), shape_of((blocks,), jnp.int32), shape_of((6,), jnp.int32)
        ),
        in_specs=[SMEM] * 3,
        out_specs=(SMEM,) * 3,
    )(place, pattern_one, pattern_two)
    operands = (
        root_covariance.reshape(-1, B), row_order, col_order, info, place, factor_one, inverse_one,
        factor_parent, factor_root, inverse_two,
    )
    branches = [functools.partial(run, one, two) for one, two in capacities]
    if len(branches) == 1:
        results = branches[0](*operands)
    else:
        results = lax.switch(info[4], branches, *operands)
    cross_one, block_one, parent_out, cross_two, block_two = results
    cross_one = cross_one.reshape(-1, blocks, 1, B)
    cross_two = cross_two.reshape(-1, blocks, 1, B)
    return cross_one, block_one, parent_out, cross_two, block_two


def solution(mesh):
    return jax.shard_map(
        local,
        mesh=mesh,
        in_specs=(
            P("grp", "col", None, None, "row", None),
            P("grp", "row", None, "col"),
            P(("grp", "col"), None),
            P("grp"),
            P(("grp", "row"), "col"),
            P("grp", "row", None, "col"),
            P(("grp", "col"), None),
            P("grp"),
        ),
        out_specs=(
            P(("grp", "row"), None, "col", None),
            P(("grp", "col"), "row"),
            P(("grp", "row"), None),
            P(("grp", "row"), None, "col", None),
            P(("grp", "col"), "row"),
        ),
        check_vma=False,
    )
```
